256 devices in a mesh: mp: 16 (over y_hi, x, core), dp: 16 (over y_lo, z).
Axes of the slice: x: 4, y: 4 (y_hi: 2, y_lo: 2; y = y_hi * 2 + y_lo), z: 8, core: 2. Of those that a mesh axis runs over, the one named last changes fastest.
Arguments:
- inputs: bfloat16 [16, 256, 4096], P('dp'), may hold values from -6 to 6
- out_grad: bfloat16 [16, 256, 4096], P('dp'), may hold values from -6 to 6
- w_gate: bfloat16 [4096, 7168], P('dp', 'mp'), may hold values from -0.09375 to 0.09375
- w_up: bfloat16 [4096, 7168], P('dp', 'mp'), may hold values from -0.09375 to 0.09375
- w_down: bfloat16 [7168, 4096], P('mp', 'dp'), may hold values from -0.0625 to 0.0625
Outputs:
- in_grad: bfloat16 [16, 256, 4096], P('dp', 'mp')
- gate_grad: bfloat16 [4096, 7168], P('dp', 'mp')
- up_grad: bfloat16 [4096, 7168], P('dp', 'mp')
- down_grad: bfloat16 [7168, 4096], P('mp', 'dp')
The draws below stay inside these ranges and needn't reach their ends.
All inputs are finite; a program needn't handle non-finite values.
Results may differ from the reference program's by a relative error of at most 0.022.
Values may be sent and summed in bfloat16 or wider, within the bound.
No kernel may reach another device: no remote copies, remote signals or barrier semaphores. Data moves between devices by JAX's collectives and lax.ppermute only.
A program may use at most 64 MiB of HBM per device.

```python
import jax
import jax.numpy as jnp
from jax import lax

D = 4096
FF = 7168
ROWS = 256
REPLICAS = 16


def spiked(drawn, rng, source, target, parts, factor):
    owner, partner = [(jnp.arange(drawn.shape[axis_at]) // (drawn.shape[axis_at] // parts)).reshape([-1 if axis == axis_at else 1 for axis in range(drawn.ndim)]) for axis_at in (source, target)]
    chosen = jax.random.permutation(rng, parts)[partner]
    strong = (owner == chosen) | (owner == (partner + parts // 2) % parts)
    return jnp.where(strong, factor * drawn, drawn)


def block_levels(rng, shape, split, smallest, top_value):
    factor_of = 1.0
    for dim, blocks in split:
        draws = jax.random.uniform(jax.random.fold_in(jax.random.fold_in(rng, 6), dim), (blocks,), jnp.float32, smallest / len(split), top_value / len(split))
        factor_of = factor_of * jnp.repeat(jnp.exp(draws), shape[dim] // blocks).reshape((-1,) + (1,) * (len(shape) - 1 - dim))
    return factor_of


def noise(own_key, extent, deviation, bound, pieces=(), held_as=jnp.bfloat16):
    array = jax.random.normal(own_key, extent, jnp.float32) * deviation
    if len(pieces) > 0:
        array = block_levels(own_key, extent, pieces, -0.22, 0.18) * array
    return jnp.clip(array, min=-bound, max=bound).astype(held_as)


def noise_with(rng, shape, spread, limit, cuts, heavy, dtype=jnp.bfloat16):
    result = spread * jax.random.normal(rng, shape, jnp.float32)
    if cuts:
        result = result * block_levels(rng, shape, cuts, -0.22, 0.18)
    return jnp.clip(spiked(result, jax.random.fold_in(rng, 3), *heavy), -limit, limit).astype(dtype)


def setup_inputs(seed: int = 0) -> dict:
    arg_keys = jax.random.split(jax.random.key(seed), 6)
    return {
        "inputs": noise_with(arg_keys[0], (REPLICAS, ROWS, D), 1.0, 6.0, ((0, 16),), (0, 2, 16, 2.0)),
        "out_grad": noise_with(arg_keys[1], (REPLICAS, ROWS, D), 1.0, 6.0, ((0, 16),), (0, 2, 16, 2.0)),
        "w_gate": noise(arg_keys[2], (D, FF), D ** -0.5, 0.09375, ((0, 16), (1, 16))),
        "w_up": noise(arg_keys[3], (D, FF), D ** -0.5, 0.09375, ((0, 16), (1, 16))),
        "w_down": noise(arg_keys[4], (FF, D), FF ** -0.5, 0.0625, ((0, 16), (1, 16))),
    }


def replica_pass(x_rows, dy_rows, w_gate, w_up, w_down):
    gate = jnp.dot(x_rows, w_gate, preferred_element_type=jnp.float32)
    up = jnp.dot(x_rows, w_up, preferred_element_type=jnp.float32)
    sig = jax.nn.sigmoid(gate)
    silu = gate * sig
    hidden = (silu * up).astype(jnp.bfloat16)
    dhid = jnp.dot(dy_rows, w_down.T, preferred_element_type=jnp.float32)
    dup = (dhid * silu).astype(jnp.bfloat16)
    dgate = (dhid * up * sig * (1.0 + gate * (1.0 - sig))).astype(jnp.bfloat16)
    dx_rows = (jnp.dot(dgate, w_gate.T, preferred_element_type=jnp.float32)
               + jnp.dot(dup, w_up.T, preferred_element_type=jnp.float32)).astype(jnp.bfloat16)
    term_gate = jnp.dot(x_rows.T, dgate, preferred_element_type=jnp.float32).astype(jnp.bfloat16)
    term_up = jnp.dot(x_rows.T, dup, preferred_element_type=jnp.float32).astype(jnp.bfloat16)
    term_down = jnp.dot(hidden.T, dy_rows, preferred_element_type=jnp.float32).astype(jnp.bfloat16)
    return dx_rows, term_gate, term_up, term_down


def reference(inputs, out_grad, w_gate, w_up, w_down):
    def step(carry, pair):
        dx_rows, term_gate, term_up, term_down = replica_pass(pair[0], pair[1], w_gate, w_up, w_down)
        carry = (carry[0] + term_gate.astype(jnp.float32),
                 carry[1] + term_up.astype(jnp.float32),
                 carry[2] + term_down.astype(jnp.float32))
        return carry, dx_rows

    start = (jnp.zeros(w_gate.shape, jnp.float32), jnp.zeros(w_up.shape, jnp.float32),
             jnp.zeros(w_down.shape, jnp.float32))
    sums, in_grad = lax.scan(step, start, (inputs, out_grad))
    return (in_grad, sums[0].astype(jnp.bfloat16), sums[1].astype(jnp.bfloat16),
            sums[2].astype(jnp.bfloat16))
```

```python
import jax
import jax.numpy as jnp
from jax import lax
from jax.sharding import PartitionSpec as P

BF = jnp.bfloat16
F32 = jnp.float32
NX, NZ, NB = 4, 8, 16


def dot_rows(left, right):
    return lax.dot_general(left, right, (((0,), (0,)), ((), ())), preferred_element_type=F32)


def dot_cols(left, right):
    return lax.dot_general(left, right, (((1,), (1,)), ((), ())), preferred_element_type=F32)


def pz(value, step):
    pairs = [(y * NZ + z, y * NZ + (z + step) % NZ) for y in range(2) for z in range(NZ)]
    return lax.ppermute(value, "dp", pairs)


def pyl(value):
    return lax.ppermute(value, "dp", [(i, (i + NZ) % (2 * NZ)) for i in range(2 * NZ)])


def px(value, step):
    pairs = [
        (y * 8 + x * 2 + c, y * 8 + (x + step) % NX * 2 + c)
        for y in range(2) for x in range(NX) for c in range(2)
    ]
    return lax.ppermute(value, "mp", pairs)


def pc(value):
    return lax.ppermute(value, "mp", [(i, i ^ 1) for i in range(16)])


def pyh(value):
    return lax.ppermute(value, "mp", [(i, i ^ 8) for i in range(16)])


def halves(array, index):
    rows = array.shape[0] // 2
    return (
        lax.dynamic_slice_in_dim(array, index * rows, rows, 0),
        lax.dynamic_slice_in_dim(array, (1 - index) * rows, rows, 0),
    )


def local(inputs, out_grad, w_gate, w_up, w_down):
    rows, width = inputs.shape[1:]
    part = w_down.shape[0] // 2
    block = w_down.shape[1]
    dp, mp = lax.axis_index("dp"), lax.axis_index("mp")
    yl, z = dp // NZ, dp % NZ
    yh, x, c = mp // 8, mp // 2 % NX, mp % 2
    group = rows // 16

    wts = [halves(w, yl) for w in (w_gate.T, w_up.T, w_down)]
    own = jnp.concatenate([w[0] for w in wts])
    other = pyl(jnp.concatenate([w[1] for w in wts]))
    mid = own.shape[0] // 2

    def gather(chunk):
        out = [chunk] + [None] * (NZ - 1)
        up = down = chunk
        for step in range(1, 4):
            up, down = pz(up, 1), pz(down, -1)
            out[NZ - step], out[step] = up, down
        out[4] = jnp.concatenate([pz(up[:mid], 1), pz(down[mid:], -1)])
        return out

    def roll_cols(array, shift_y, shift_z):
        array = array.reshape(array.shape[0], 2, NZ, block)
        array = jnp.roll(array, (-shift_y, -shift_z), (1, 2))
        return array.reshape(array.shape[0], width)

    x_own = roll_cols(inputs[0], yl, z)
    dy_own = roll_cols(out_grad[0], yl, z)

    def rows_at(array, index):
        return lax.dynamic_slice_in_dim(array, index * group, group, 0)

    def piece(array):
        array = jnp.concatenate([rows_at(array, mp), rows_at(array, mp ^ 8)])
        return jnp.concatenate([array[:, width // 2 :], array[:, : width // 2]], axis=1)

    first = pyl(jnp.stack([piece(x_own), piece(dy_own)]))
    same = [first, px(first, -1), px(first, 2), px(first, 1)]
    pieces = same + [pc(p) for p in same]
    x_par = jnp.concatenate([p[0] for p in pieces])
    dy_par = jnp.concatenate([p[1] for p in pieces])

    chunks = gather(own) + gather(other)
    w_all = jnp.concatenate(chunks, axis=1)
    wg, wu, wd = w_all[:part], w_all[part : 2 * part], w_all[2 * part :]

    x_all = jnp.concatenate([x_own, x_par])
    dy_all = jnp.concatenate([dy_own, dy_par])
    gate = dot_cols(x_all, wg)
    up_val = dot_cols(x_all, wu)
    dhid = dot_cols(dy_all, wd)
    sig = jax.nn.sigmoid(gate)
    silu = gate * sig
    hidden = (silu * up_val).astype(BF)
    dup = (dhid * silu).astype(BF)
    dgate = (dhid * up_val * sig * (1.0 + gate * (1.0 - sig))).astype(BF)

    def term(k, s):
        at = (k * NZ + s) * block
        cols_x, cols_dy = x_all[:, at : at + block], dy_all[:, at : at + block]
        return jnp.concatenate([dot_rows(dgate, cols_x), dot_rows(dup, cols_x), dot_rows(hidden, cols_dy)])

    def reduce(k):
        far = term(k, 4).astype(BF)
        up, down = pz(far[:mid], 1), pz(far[mid:], -1)
        for s in (3, 2, 1):
            up_t, down_t = term(k, s), term(k, NZ - s)
            if s == 3:
                up = jnp.concatenate([up_t[:mid] + up, up_t[mid:]])
                down = jnp.concatenate([down_t[:mid], down_t[mid:] + down])
            else:
                up, down = up_t + up, down_t + down
            up, down = pz(up.astype(BF), 1), pz(down.astype(BF), -1)
        return (term(k, 0) + up.astype(F32) + down.astype(F32)).astype(BF)

    sum_other = pyl(reduce(1))
    sum_own = reduce(0)

    order = []
    for dc in range(2):
        for dx in range(NX):
            for dh in range(2):
                order.append((yh ^ dh) * 8 + (x + dx) % NX * 2 + (c ^ dc))
    order = jnp.stack(order)

    def arrange(array):
        first = jnp.take(array[:rows].reshape(16, group, part), order, axis=0)
        both = jnp.stack([first.reshape(8, 2 * group, part), array[rows:].reshape(8, 2 * group, part)], axis=1)
        return both.reshape(2 * rows, part)

    dg_r, du_r = arrange(dgate), arrange(dup)

    def dx_rows(lo, hi):
        return jnp.dot(dg_r[lo:hi], wg, preferred_element_type=F32) + jnp.dot(
            du_r[lo:hi], wu, preferred_element_type=F32
        )

    sent = pc(dx_rows(rows, 2 * rows).astype(BF))
    acc = dx_rows(0, rows) + sent
    quarter = rows // NX
    acc_b = acc.astype(BF)
    got = [px(acc_b[i * quarter : (i + 1) * quarter], i) for i in range(1, NX)]
    acc = acc[:quarter] + got[0] + got[1] + got[2]
    half = quarter // 2
    got = pyl(acc[half:].astype(BF))
    acc = acc[:half] + jnp.concatenate([got[:, width // 2 :], got[:, : width // 2]], axis=1)
    acc = acc[:group] + pyh(acc[group:].astype(BF))
    in_grad = roll_cols(acc.astype(BF), yl, -z).reshape(1, group, width)

    def whole(index):
        mine = sum_own[index * part : (index + 1) * part]
        theirs = sum_other[index * part : (index + 1) * part]
        return jnp.where(yl == 0, jnp.concatenate([mine, theirs]), jnp.concatenate([theirs, mine]))

    return in_grad, whole(0).T, whole(1).T, whole(2)


def solution(mesh):
    placed = (P("dp", None, None), P("dp", None, None), P("dp", "mp"), P("dp", "mp"), P("mp", "dp"))
    return jax.shard_map(
        local,
        mesh=mesh,
        in_specs=placed,
        out_specs=(P("dp", "mp", None), P("dp", "mp"), P("dp", "mp"), P("mp", "dp")),
        check_vma=False,
    )
```

```python
import functools

import jax
import jax.numpy as jnp
from jax import lax
from jax.experimental import pallas as pl
from jax.experimental.pallas import tpu as pltpu
from jax.sharding import PartitionSpec as P

BF = jnp.bfloat16
F32 = jnp.float32
NX, NZ = 4, 8
LANES = 256
ANY = pl.BlockSpec(memory_space=pl.ANY)
VMEM = pl.BlockSpec(memory_space=pltpu.VMEM)
SMEM = pl.BlockSpec(memory_space=pltpu.SMEM)
LIMIT = 56 * 1024 * 1024


def mm(left, right):
    return lax.dot_general(left, right, (((1,), (0,)), ((), ())), preferred_element_type=F32)


def mm_t(left, right):
    return lax.dot_general(left, right, (((1,), (1,)), ((), ())), preferred_element_type=F32)


def pz(value, step):
    pairs = [(y * NZ + z, y * NZ + (z + step) % NZ) for y in range(2) for z in range(NZ)]
    return lax.ppermute(value, "dp", pairs)


def pyl(value):
    return lax.ppermute(value, "dp", [(i, (i + NZ) % (2 * NZ)) for i in range(2 * NZ)])


def px(value, step):
    pairs = [
        (y * 8 + x * 2 + c, y * 8 + (x + step) % NX * 2 + c)
        for y in range(2) for x in range(NX) for c in range(2)
    ]
    return lax.ppermute(value, "mp", pairs)


def pc(value):
    return lax.ppermute(value, "mp", [(i, i ^ 1) for i in range(16)])


def pyh(value):
    return lax.ppermute(value, "mp", [(i, i ^ 8) for i in range(16)])


def after(value, *others):
    return lax.optimization_barrier((value, *others))[0]


def col_block(sc, k, s):
    yl = 1 - sc[1] if k else sc[1]
    return yl * NZ + lax.rem(sc[0] + s, NZ)


def offset(sc, k, s):
    return pl.multiple_of(col_block(sc, k, s) * LANES, LANES)


def load_chunks(where, refs, buf, sems):
    waits, at = [], 0
    for i, parts in enumerate(where):
        mine, row = [], 0
        for _ in range(parts):
            ref = refs[at]
            copy = pltpu.make_async_copy(ref, buf.at[i, pl.ds(row, ref.shape[0])], sems.at[at])
            copy.start()
            mine.append(copy)
            row += ref.shape[0]
            at += 1
        waits.append(mine)
    return waits


def accumulate(acc, first, xs, dys, w, part):
    for m, rows in ((0, xs), (1, xs), (2, dys)):
        got = mm_t(rows, w[m * part : m * part + LANES])
        if first:
            acc[m] = got
        else:
            acc[m] += got


def early_kernel(keys, parts, n_pieces, part, sc, x, dy, *refs):
    pieces, chunks = refs[:n_pieces], refs[n_pieces : n_pieces + sum(parts)]
    acc, xp, xs, buf, w_sems, x_sems, out_sem = refs[n_pieces + sum(parts) :]
    rows = x.shape[0]
    loads = [
        pltpu.make_async_copy(x, xs.at[0, pl.ds(0, rows)], x_sems.at[0]),
        pltpu.make_async_copy(dy, xs.at[1, pl.ds(0, rows)], x_sems.at[1]),
    ]
    row = rows
    for i, piece in enumerate(pieces):
        n = piece.shape[1]
        loads.append(pltpu.make_async_copy(piece, xs.at[:, pl.ds(row, n)], x_sems.at[2 + i]))
        row += n
    for copy in loads:
        copy.start()
    waits = load_chunks(parts, chunks, buf, w_sems)
    for i in range(len(keys)):
        buf[i, 3 * part :] = jnp.zeros((buf.shape[1] - 3 * part, LANES), BF)
    for copy in loads:
        copy.wait()
    store = pltpu.make_async_copy(xs.at[:, pl.ds(rows, rows)], xp, out_sem)
    store.start()
    for i, (k, s) in enumerate(keys):
        for copy in waits[i]:
            copy.wait()
        at = offset(sc, k, s)
        accumulate(acc, i == 0, xs[0, :, pl.ds(at, LANES)], xs[1, :, pl.ds(at, LANES)], buf[i], part)
    store.wait()


def late_kernel(keys, parts, part, sc, acc_in, x, dy, xp, *refs):
    chunks = refs[: sum(parts)]
    gt, dgu, acc, rowbuf, xb, buf, w_sems, x_sems = refs[sum(parts) :]
    rows = x.shape[0]
    loads = []
    for i, (k, s) in enumerate(keys):
        cols = pl.ds(offset(sc, k, s), LANES)
        mine = [
            pltpu.make_async_copy(x.at[:, cols], xb.at[i, 0, pl.ds(0, rows)], x_sems.at[i, 0]),
            pltpu.make_async_copy(dy.at[:, cols], xb.at[i, 1, pl.ds(0, rows)], x_sems.at[i, 1]),
            pltpu.make_async_copy(xp.at[:, :, cols], xb.at[i, :, pl.ds(rows, rows)], x_sems.at[i, 2]),
        ]
        for copy in mine:
            copy.start()
        loads.append(mine)
    waits = load_chunks(parts, chunks, buf, w_sems)
    for i in range(len(keys)):
        buf[i, 3 * part :] = jnp.zeros((buf.shape[1] - 3 * part, LANES), BF)
    acc[...] = acc_in[...]
    for i in range(len(keys)):
        for copy in loads[i] + waits[i]:
            copy.wait()
        accumulate(acc, False, xb[i, 0], xb[i, 1], buf[i], part)
    gate, up_val, dhid = acc[0], acc[1], acc[2]
    sig = 1.0 / (1.0 + jnp.exp(-gate))
    silu = gate * sig
    valid = lax.broadcasted_iota(jnp.int32, gate.shape, 1) < part
    hidden = silu * up_val
    dup = jnp.where(valid, dhid * silu, 0.0)
    dgate = jnp.where(valid, dhid * up_val * sig * (1.0 + gate * (1.0 - sig)), 0.0)
    for m, value in enumerate((dgate, dup, hidden)):
        gt[m * part : (m + 1) * part] = value.T[:part].astype(BF)
    group = rows // 16
    for m, value in enumerate((dgate, dup)):
        rowbuf[...] = value.astype(BF)
        for g in range(16):
            to = g // 2 * 4 * group + g % 2 * group
            at = pl.multiple_of(sc[2 + g] * group, group)
            dgu[m, to : to + group] = rowbuf[pl.ds(at, group)]
            to += 2 * group
            dgu[m, to : to + group] = rowbuf[rows + g * group : rows + (g + 1) * group]


def dx_kernel(keys, parts, part, sc, dgu, *refs):
    chunks = refs[: sum(parts)]
    keep, send, buf, w_sems = refs[sum(parts) :]
    rows = keep.shape[0]
    waits = load_chunks(parts, chunks, buf, w_sems)
    for i, (k, s) in enumerate(keys):
        for copy in waits[i]:
            copy.wait()
        cols = pl.ds(offset(sc, k, s), LANES)
        dx = mm(dgu[0], buf[i, :LANES]) + mm(dgu[1], buf[i, part : part + LANES])
        keep[:, cols] = dx[:rows].astype(BF)
        send[:, cols] = dx[rows:].astype(BF)


def term_kernel(mode, part, sc, gt, x, xp, dy, dyp, *refs):
    rows = x.shape[0]
    two = 2 * part
    top = mm(gt[:two, :rows], x[...]) + mm(gt[:two, rows:], xp[0])
    low = mm(gt[two:, :rows], dy[...]) + mm(gt[two:, rows:], dyp[0])
    mid = 3 * part // 2
    if mode == "far":
        up, down = refs
        up[...] = top[:mid].astype(BF)
        down[: two - mid] = top[mid:].astype(BF)
        down[two - mid :] = low.astype(BF)
        return
    *given, out = refs
    if mode == "upper":
        out[:mid] = (top[:mid] + given[0][...].astype(F32)).astype(BF)
        out[mid:two] = top[mid:].astype(BF)
        out[two:] = low.astype(BF)
    elif mode == "lower":
        out[:mid] = top[:mid].astype(BF)
        out[mid:two] = (top[mid:] + given[0][: two - mid].astype(F32)).astype(BF)
        out[two:] = (low + given[0][two - mid :].astype(F32)).astype(BF)
    else:
        for ref in given:
            top += ref[:two].astype(F32)
            low += ref[two:].astype(F32)
        out[:two] = top.astype(BF)
        out[two:] = low.astype(BF)


def halves(array, index):
    rows = array.shape[0] // 2
    return (
        lax.dynamic_slice_in_dim(array, index * rows, rows, 0),
        lax.dynamic_slice_in_dim(array, (1 - index) * rows, rows, 0),
    )


def params():
    return pltpu.CompilerParams(vmem_limit_bytes=LIMIT)


def local(inputs, out_grad, w_gate, w_up, w_down):
    rows, width = inputs.shape[1:]
    part = w_down.shape[0] // 2
    dp, mp = lax.axis_index("dp"), lax.axis_index("mp")
    yl, z = dp // NZ, dp % NZ
    yh, x, c = mp // 8, mp // 2 % NX, mp % 2
    group = rows // 16
    x_own, dy_own = inputs[0], out_grad[0]

    order = []
    for dc in range(2):
        for dx in range(NX):
            for dh in range(2):
                order.append((yh ^ dh) * 8 + (x + dx) % NX * 2 + (c ^ dc))
    sc = jnp.stack([z, yl, *order]).astype(jnp.int32)

    wts = [halves(w, yl) for w in (w_gate.T, w_up.T, w_down)]
    own = jnp.concatenate([w[0] for w in wts])
    other = pyl(jnp.concatenate([w[1] for w in wts]))
    mid = own.shape[0] // 2

    def rows_at(array, index):
        return lax.dynamic_slice_in_dim(array, index * group, group, 0)

    def piece(array):
        return jnp.concatenate([rows_at(array, mp), rows_at(array, mp ^ 8)])

    first = pyl(jnp.stack([piece(x_own), piece(dy_own)]))
    same = [first, px(first, -1), px(first, 2), px(first, 1)]
    pieces = same + [pc(p) for p in same]

    def gather(k, chunk):
        out = {(k, 0): [chunk]}
        up = down = chunk
        for step in range(1, 4):
            up, down = pz(up, 1), pz(down, -1)
            out[k, NZ - step], out[k, step] = [up], [down]
        out[k, 4] = [pz(up[:mid], 1), pz(down[mid:], -1)]
        return out

    chunks = gather(0, own) | gather(1, other)
    late = [(1, 3), (1, 5), (0, 4), (1, 4)]
    early = [key for key in chunks if key not in late]

    def listed(keys):
        refs = [chunks[key] for key in keys]
        return tuple(len(r) for r in refs), [a for r in refs for a in r]

    acc_shape = jax.ShapeDtypeStruct((3, 2 * rows, LANES), F32)
    padded = 2 * part + LANES
    parts, refs = listed(early)
    acc, xp = pl.pallas_call(
        functools.partial(early_kernel, early, parts, len(pieces), part),
        out_shape=(acc_shape, jax.ShapeDtypeStruct((2, rows, width), BF)),
        in_specs=[SMEM] + [ANY] * (2 + len(pieces) + len(refs)),
        out_specs=(VMEM, ANY),
        scratch_shapes=[
            pltpu.VMEM((2, 2 * rows, width), BF),
            pltpu.VMEM((len(early), padded, LANES), BF),
            pltpu.SemaphoreType.DMA((len(refs),)),
            pltpu.SemaphoreType.DMA((2 + len(pieces),)),
            pltpu.SemaphoreType.DMA,
        ],
        compiler_params=params(),
        name="early",
    )(sc, x_own, dy_own, *pieces, *refs)

    parts, refs = listed(late)
    gt, dgu = pl.pallas_call(
        functools.partial(late_kernel, late, parts, part),
        out_shape=(
            jax.ShapeDtypeStruct((3 * part, 2 * rows), BF),
            jax.ShapeDtypeStruct((2, 2 * rows, LANES), BF),
        ),
        in_specs=[SMEM, VMEM] + [ANY] * (3 + len(refs)),
        out_specs=(VMEM, VMEM),
        scratch_shapes=[
            pltpu.VMEM(acc_shape.shape, F32),
            pltpu.VMEM((2 * rows, LANES), BF),
            pltpu.VMEM((len(late), 2, 2 * rows, LANES), BF),
            pltpu.VMEM((len(late), padded, LANES), BF),
            pltpu.SemaphoreType.DMA((len(refs),)),
            pltpu.SemaphoreType.DMA((len(late), 3)),
        ],
        compiler_params=params(),
        name="late",
    )(sc, acc, x_own, dy_own, xp, *refs)

    def term(k, s, mode, *given):
        def block(which):
            if which is None:
                return pl.BlockSpec((rows, LANES), lambda i, sc: (0, col_block(sc, k, s)))
            return pl.BlockSpec((1, rows, LANES), lambda i, sc: (which, 0, col_block(sc, k, s)))

        full = jax.ShapeDtypeStruct((3 * part, LANES), BF)
        half = jax.ShapeDtypeStruct((mid, LANES), BF)
        return pl.pallas_call(
            functools.partial(term_kernel, mode, part),
            out_shape=(half, half) if mode == "far" else full,
            grid_spec=pltpu.PrefetchScalarGridSpec(
                num_scalar_prefetch=1,
                grid=(1,),
                in_specs=[pl.BlockSpec(gt.shape, lambda i, sc: (0, 0)), block(None), block(0), block(None), block(1)]
                + [pl.BlockSpec(g.shape, lambda i, sc: (0, 0)) for g in given],
                out_specs=[pl.BlockSpec(half.shape, lambda i, sc: (0, 0))] * 2
                if mode == "far"
                else pl.BlockSpec(full.shape, lambda i, sc: (0, 0)),
            ),
            compiler_params=params(),
            name="term",
        )(sc, gt, x_own, xp, dy_own, xp, *given)

    keys = list(chunks)
    parts, refs = listed(keys)
    keep, send = pl.pallas_call(
        functools.partial(dx_kernel, keys, parts, part),
        out_shape=(jax.ShapeDtypeStruct((rows, width), BF),) * 2,
        in_specs=[SMEM, VMEM] + [ANY] * len(refs),
        out_specs=(VMEM, VMEM),
        scratch_shapes=[
            pltpu.VMEM((len(keys), 3 * part, LANES), BF),
            pltpu.SemaphoreType.DMA((len(refs),)),
        ],
        compiler_params=params(),
        name="dx",
    )(sc, dgu, *refs)

    up, down = {}, {}
    for k in (1, 0):
        up[k], down[k] = term(k, 4, "far")
        up[k], down[k] = pz(up[k], 1), pz(down[k], -1)
    sent = pc(send)
    acc_x = (keep.astype(F32) + sent.astype(F32)).astype(BF)
    quarter = rows // NX
    got = [px(acc_x[i * quarter : (i + 1) * quarter], i) for i in range(1, NX)]
    for s in (3, 2, 1):
        for k in (1, 0):
            up[k] = pz(term(k, s, "upper" if s == 3 else "full", up[k]), 1)
            down[k] = pz(term(k, NZ - s, "lower" if s == 3 else "full", down[k]), -1)
    sum_other = pyl(term(1, 0, "full", up[1], down[1]))
    sum_own = term(0, 0, "full", up[0], down[0])

    acc_x = acc_x[:quarter].astype(F32) + got[0] + got[1] + got[2]
    half = quarter // 2
    acc_x = acc_x[:half] + pyl(acc_x[half:].astype(BF))
    acc_x = acc_x[:group] + pyh(acc_x[group:].astype(BF))
    in_grad = acc_x.astype(BF).reshape(1, group, width)

    def whole(index):
        mine = sum_own[index * part : (index + 1) * part]
        theirs = sum_other[index * part : (index + 1) * part]
        return jnp.where(yl == 0, jnp.concatenate([mine, theirs]), jnp.concatenate([theirs, mine]))

    return in_grad, whole(0).T, whole(1).T, whole(2)


def solution(mesh):
    placed = (P("dp", None, None), P("dp", None, None), P("dp", "mp"), P("dp", "mp"), P("mp", "dp"))
    return jax.shard_map(
        local,
        mesh=mesh,
        in_specs=placed,
        out_specs=(P("dp", "mp", None), P("dp", "mp"), P("dp", "mp"), P("mp", "dp")),
        check_vma=False,
    )
```

```python
import functools

import jax
import jax.numpy as jnp
from jax import lax
from jax.experimental import pallas as pl
from jax.experimental.pallas import tpu as pltpu
from jax.sharding import PartitionSpec as P

BF = jnp.bfloat16
F32 = jnp.float32
NX, NZ = 4, 8
LANES = 256
ANY = pl.BlockSpec(memory_space=pl.ANY)
VMEM = pl.BlockSpec(memory_space=pltpu.VMEM)
COST = pl.CostEstimate(flops=1, bytes_accessed=1, transcendentals=0)
SMEM = pl.BlockSpec(memory_space=pltpu.SMEM)


def mm(left, right):
    return lax.dot_general(left, right, (((1,), (0,)), ((), ())), preferred_element_type=F32)


def mm_t(left, right):
    return lax.dot_general(left, right, (((1,), (1,)), ((), ())), preferred_element_type=F32)


def pz(value, step):
    pairs = [(y * NZ + z, y * NZ + (z + step) % NZ) for y in range(2) for z in range(NZ)]
    return lax.ppermute(value, "dp", pairs)


def pyl(value):
    return lax.ppermute(value, "dp", [(i, (i + NZ) % (2 * NZ)) for i in range(2 * NZ)])


def px(value, step):
    pairs = [
        (y * 8 + x * 2 + c, y * 8 + (x + (-step if c else step)) % NX * 2 + c)
        for y in range(2) for x in range(NX) for c in range(2)
    ]
    return lax.ppermute(value, "mp", pairs)


def pxs(value, step):
    pairs = [
        (y * 8 + x * 2 + c, y * 8 + (x + step) % NX * 2 + c)
        for y in range(2) for x in range(NX) for c in range(2)
    ]
    return lax.ppermute(value, "mp", pairs)


def pc(value):
    return lax.ppermute(value, "mp", [(i, i ^ 1) for i in range(16)])


def pyh(value):
    return lax.ppermute(value, "mp", [(i, i ^ 8) for i in range(16)])


def after(value, *others):
    return lax.optimization_barrier((value, *others))[0]


def after_all(*values):
    return lax.optimization_barrier(values)


def col_block(sc, k, s):
    yl = 1 - sc[1] if k else sc[1]
    return yl * NZ + lax.rem(sc[0] + s, NZ)


def offset(sc, k, s):
    return pl.multiple_of(col_block(sc, k, s) * LANES, LANES)


def spread(row, count, part):
    out, end = [], row + count
    while row < end:
        m = row // part
        n = min(end, (m + 1) * part) - row
        out.append((row, n, m * LANES + row - m * part))
        row += n
    return out


def load_chunks(where, places, part, refs, buf, sems):
    waits, sem = [], 0
    for parts, place in zip(where, places):
        mine = []
        for at, row, start, count in parts:
            for first, n, to in spread(start, count, part):
                copy = pltpu.make_async_copy(
                    refs[at].at[pl.ds(row + first - start, n)],
                    buf.at[pl.ds(to, n), pl.ds(place, LANES)],
                    sems.at[sem],
                )
                copy.start()
                mine.append(copy)
                sem += 1
        waits.append(mine)
    return waits


def copies_of(where, part):
    return sum(len(spread(start, count, part)) for parts in where for _, _, start, count in parts)


def clear_pad(buf, part):
    for m in range(3):
        buf[m * LANES + part : (m + 1) * LANES] = jnp.zeros((LANES - part, buf.shape[1]), BF)


def early_kernel(keys, missing, parts, n_pieces, piece_at, part, sc, x, dy, *refs):
    pieces, chunks = refs[:n_pieces], refs[n_pieces:-7]
    acc, xp, xs, buf, w_sems, x_sems, out_sem = refs[-7:]
    rows = x.shape[0]
    loads = [
        pltpu.make_async_copy(x, xs.at[0, pl.ds(0, rows)], x_sems.at[0]),
        pltpu.make_async_copy(dy, xs.at[1, pl.ds(0, rows)], x_sems.at[1]),
    ]
    row = rows
    pieces = [pieces[i].at[j] for i, j in piece_at]
    for i, piece in enumerate(pieces):
        n = piece.shape[1]
        loads.append(pltpu.make_async_copy(piece, xs.at[:, pl.ds(row, n)], x_sems.at[2 + i]))
        row += n
    for copy in loads:
        copy.start()
    waits = load_chunks(parts, [offset(sc, *key) for key in keys], part, chunks, buf, w_sems)
    clear_pad(buf, part)
    for key in missing:
        buf[:, pl.ds(offset(sc, *key), LANES)] = jnp.zeros((buf.shape[0], LANES), BF)
    for copy in loads:
        copy.wait()
    store = pltpu.make_async_copy(xs.at[:, pl.ds(rows, rows)], xp, out_sem)
    store.start()
    for mine in waits:
        for copy in mine:
            copy.wait()
    acc[:, : 2 * LANES] = mm_t(xs[0], buf[: 2 * LANES])
    acc[:, 2 * LANES :] = mm_t(xs[1], buf[2 * LANES :])
    store.wait()


def late_kernel(keys, parts, part, sc, acc, x, dy, xp, *refs):
    chunks = refs[:-10]
    gt, dgu, *far = refs[-10:-4]
    rowbuf, xb, buf, x_sems = refs[-4:]
    rows = x.shape[0]
    loads = []
    for i, (k, s) in enumerate(keys):
        cols, to = pl.ds(offset(sc, k, s), LANES), pl.ds(i * LANES, LANES)
        loads += [
            pltpu.make_async_copy(x.at[:, cols], xb.at[0, pl.ds(0, rows), to], x_sems.at[i, 0]),
            pltpu.make_async_copy(dy.at[:, cols], xb.at[1, pl.ds(0, rows), to], x_sems.at[i, 1]),
            pltpu.make_async_copy(xp.at[:, :, cols], xb.at[:, pl.ds(rows, rows), to], x_sems.at[i, 2]),
        ]
    for copy in loads:
        copy.start()
    clear_pad(buf, part)
    for i, pieces in enumerate(parts):
        for at, row, start, count in pieces:
            for first, n, to in spread(start, count, part):
                row_at = row + first - start
                buf[to : to + n, i * LANES : (i + 1) * LANES] = chunks[at][row_at : row_at + n]
    for copy in loads:
        copy.wait()
    both = acc[:, : 2 * LANES] + mm_t(xb[0], buf[: 2 * LANES])
    dhid = acc[:, 2 * LANES :] + mm_t(xb[1], buf[2 * LANES :])
    gate, up_val = both[:, :LANES], both[:, LANES:]
    sig = 1.0 / (1.0 + jnp.exp(-gate))
    silu = gate * sig
    hidden = silu * up_val
    dup = dhid * silu
    dgate = dhid * up_val * sig * (1.0 + gate * (1.0 - sig))
    for m, value in enumerate((dgate, dup, hidden)):
        gt[m * part : (m + 1) * part] = value.T[:part].astype(BF)
    mid = 3 * part // 2
    two = 2 * part
    for j in range(2):
        cols = slice((len(keys) - 2 + j) * LANES, (len(keys) - 1 + j) * LANES)
        top, low = mm(gt[:two], xb[0, :, cols]), mm(gt[two:], xb[1, :, cols])
        far[2 * j][...] = top[:mid].astype(BF)
        far[2 * j + 1][: two - mid] = top[mid:].astype(BF)
        far[2 * j + 1][two - mid :] = low.astype(BF)
    group = rows // 16
    for m, value in enumerate((dgate, dup)):
        rowbuf[...] = value.astype(BF)
        for g in range(16):
            to = g // 2 * 4 * group + g % 2 * group
            at = pl.multiple_of(sc[2 + g] * group, group)
            dgu[m, to : to + group] = rowbuf[pl.ds(at, group)]
        for g in range(8):
            to = g * 4 * group + 2 * group
            at = pl.multiple_of(rows + sc[18 + g] * 2 * group, 2 * group)
            dgu[m, to : to + 2 * group] = rowbuf[pl.ds(at, 2 * group)]


def rest_kernel(keys, parts, term_keys, part, sc, gt, dgu, x, dy, xp, *refs):
    n_out = len(term_keys) + 6
    chunks, (keep, send, *refs) = refs[:-n_out], refs[-n_out:]
    outs, (buf, xb, w_sems, x_sems) = refs[: len(term_keys)], refs[len(term_keys) :]
    rows = x.shape[0]
    waits = load_chunks(parts, [offset(sc, *key) for key in keys], part, chunks, buf, w_sems)
    loads = []
    for i, (k, s) in enumerate(term_keys):
        cols, to = pl.ds(offset(sc, k, s), LANES), pl.ds(i * LANES, LANES)
        mine = [
            pltpu.make_async_copy(x.at[:, cols], xb.at[0, pl.ds(0, rows), to], x_sems.at[i, 0]),
            pltpu.make_async_copy(dy.at[:, cols], xb.at[1, pl.ds(0, rows), to], x_sems.at[i, 1]),
            pltpu.make_async_copy(xp.at[:, :, cols], xb.at[:, pl.ds(rows, rows), to], x_sems.at[i, 2]),
        ]
        for copy in mine:
            copy.start()
        loads.append(mine)
    clear_pad(buf, part)
    for mine in waits:
        for copy in mine:
            copy.wait()
    step = 4 * LANES
    for at in range(0, keep.shape[1], step):
        cols = slice(at, at + step)
        dx = mm(dgu[0], buf[:LANES, cols]) + mm(dgu[1], buf[LANES : 2 * LANES, cols])
        keep[:, cols] = dx[:rows].astype(BF)
        send[:, cols] = dx[rows:].astype(BF)
    two = 2 * part
    for i in range(0, len(term_keys), 2):
        for copy in loads[i] + loads[i + 1]:
            copy.wait()
        cols = slice(i * LANES, (i + 2) * LANES)
        top = mm(gt[:two], xb[0, :, cols]).astype(BF)
        low = mm(gt[two:], xb[1, :, cols]).astype(BF)
        for j in range(2):
            outs[i + j][:two] = top[:, j * LANES : (j + 1) * LANES]
            outs[i + j][two:] = low[:, j * LANES : (j + 1) * LANES]


def halves(array, index):
    rows = array.shape[0] // 2
    return (
        lax.dynamic_slice_in_dim(array, index * rows, rows, 0),
        lax.dynamic_slice_in_dim(array, (1 - index) * rows, rows, 0),
    )


def params(mib):
    return pltpu.CompilerParams(vmem_limit_bytes=mib * 1024 * 1024)


def local(inputs, out_grad, w_gate, w_up, w_down):
    rows, width = inputs.shape[1:]
    part = w_down.shape[0] // 2
    dp, mp = lax.axis_index("dp"), lax.axis_index("mp")
    yl, z = dp // NZ, dp % NZ
    yh, x, c = mp // 8, mp // 2 % NX, mp % 2
    group = rows // 16
    x_own, dy_own = inputs[0], out_grad[0]

    order = []
    for dc in range(2):
        sign = 1 - 2 * (c ^ dc)
        for dx in range(NX):
            for dh in range(2):
                order.append((yh ^ dh) * 8 + (x - sign * dx + NX) % NX * 2 + (c ^ dc))
    stands = [dc * NX + (NX - (1 - 2 * (c ^ dc)) * dx) % NX for dc in range(2) for dx in range(NX)]
    sc = jnp.stack([z, yl, *order, *stands]).astype(jnp.int32)

    wts = [halves(w, yl) for w in (w_gate.T, w_up.T, w_down)]
    own = jnp.concatenate([w[0] for w in wts])
    other = jnp.concatenate([w[1] for w in wts])
    mid = own.shape[0] // 2

    def rows_at(array, index):
        return lax.dynamic_slice_in_dim(array, index * group, group, 0)

    def piece(array):
        return jnp.concatenate([rows_at(array, mp), rows_at(array, mp ^ 8)])

    n = own.shape[0]
    up, down = pz(own, 1), pz(own, -1)
    other = pyl(other)
    chunks = {
        (0, 0): [(own, 0, 0, n)],
        (0, 7): [(up, 0, 0, n)],
        (0, 1): [(down, 0, 0, n)],
        (1, 0): [(other, 0, 0, n)],
    }
    first = jnp.stack([piece(after(x_own, own)), piece(after(dy_own, own))])
    first = pyl(after(first, up, down))
    up, down = jnp.concatenate([other, up]), jnp.concatenate([down, other])
    for step in (1, 2):
        up, down = pz(up, 1), pz(down, -1)
        chunks[1, NZ - step], chunks[0, NZ - step - 1] = [(up, 0, 0, n)], [(up, n, 0, n)]
        chunks[0, step + 1], chunks[1, step] = [(down, 0, 0, n)], [(down, n, 0, n)]
        up, down, first = after_all(up, down, first)
        if step == 1:
            left, right = pxs(first, 1), pxs(first, -1)
    up_s, down_s, left_s, right_s = after_all(up, down, left, right)
    far_x, far_dy = pxs(left_s[0], 1), pxs(right_s[1], -1)
    swap = pc(jnp.stack([first, right_s, left_s]))
    up, down = pz(up_s[: n + mid], 1), pz(down_s[mid:], -1)
    chunks[1, 5], chunks[1, 3] = [(up, 0, 0, n)], [(down, n - mid, 0, n)]
    chunks[0, 4] = [(up, n, 0, mid), (down, 0, mid, n - mid)]
    up, down, far_x, far_dy = after_all(up, down, far_x, far_dy)
    two_off = jnp.stack([far_x, far_dy])
    swap_two = pc(two_off)
    up, down = pz(up[:mid], 1), pz(down[n:], -1)
    chunks[1, 4] = [(up, 0, 0, mid), (down, 0, mid, n - mid)]
    pieces = [first[None], right[None], two_off[None], left[None], swap, swap_two[None]]
    piece_at = [(0, 0), (1, 0), (2, 0), (3, 0), (4, 0), (4, 1), (5, 0), (4, 2)]

    late = [(0, 4), (1, 4)]
    early = [key for key in chunks if key not in late]

    def listed(keys):
        refs, where = [], []
        for key in keys:
            parts = []
            for array, *rest in chunks[key]:
                at = [i for i, a in enumerate(refs) if a is array]
                if not at:
                    refs.append(array)
                parts.append((at[0] if at else len(refs) - 1, *rest))
            where.append(tuple(parts))
        return tuple(where), refs

    parts, refs = listed(early)
    acc, xp = pl.pallas_call(
        functools.partial(early_kernel, early, late, parts, len(pieces), piece_at, part),
        out_shape=(
            jax.ShapeDtypeStruct((2 * rows, 3 * LANES), F32),
            jax.ShapeDtypeStruct((2, rows, width), BF),
        ),
        in_specs=[SMEM] + [ANY] * (2 + len(pieces) + len(refs)),
        out_specs=(VMEM, ANY),
        scratch_shapes=[
            pltpu.VMEM((2, 2 * rows, width), BF),
            pltpu.VMEM((3 * LANES, width), BF),
            pltpu.SemaphoreType.DMA((copies_of(parts, part),)),
            pltpu.SemaphoreType.DMA((2 + 2 * NX,)),
            pltpu.SemaphoreType.DMA,
        ],
        compiler_params=params(32),
        cost_estimate=COST,
        name="early",
    )(sc, x_own, dy_own, *pieces, *refs)

    parts, refs = listed(late)
    full = jax.ShapeDtypeStruct((3 * part, LANES), BF)
    half = jax.ShapeDtypeStruct((mid, LANES), BF)
    gt, dgu, *far = pl.pallas_call(
        functools.partial(late_kernel, late, parts, part),
        out_shape=(
            jax.ShapeDtypeStruct((3 * part, 2 * rows), BF),
            jax.ShapeDtypeStruct((2, 2 * rows, LANES), BF),
            half, half, half, half,
        ),
        in_specs=[SMEM, VMEM] + [ANY] * 3 + [VMEM] * len(refs),
        out_specs=(VMEM,) * 6,
        scratch_shapes=[
            pltpu.VMEM((2 * rows, LANES), BF),
            pltpu.VMEM((2, 2 * rows, len(late) * LANES), BF),
            pltpu.VMEM((3 * LANES, len(late) * LANES), BF),
            pltpu.SemaphoreType.DMA((len(late), 3)),
        ],
        compiler_params=params(32),
        cost_estimate=COST,
        name="late",
    )(sc, acc, x_own, dy_own, xp, *refs)

    term = {}

    def send_on(k, s, up, down):
        if s == 3:
            up = jnp.concatenate([term[k, 3][:mid].astype(F32) + up, term[k, 3][mid:].astype(F32)])
            down = jnp.concatenate([term[k, 5][:mid].astype(F32), term[k, 5][mid:].astype(F32) + down])
        else:
            up, down = term[k, s].astype(F32) + up, term[k, NZ - s].astype(F32) + down
        return up.astype(BF), down.astype(BF)

    def ring(up, down):
        return pz(up, 1), pz(down, -1)

    p = ring(far[2], far[3])
    o = ring(far[0], far[1])

    keys = list(chunks)
    parts, refs = listed(keys)
    term_keys = [(k, s) for s in (3, 5, 2, 6, 1, 7, 0) for k in (1, 0)]
    keep, send, *got = pl.pallas_call(
        functools.partial(rest_kernel, keys, parts, term_keys, part),
        out_shape=(jax.ShapeDtypeStruct((rows, width), BF),) * 2 + (full,) * len(term_keys),
        in_specs=[SMEM, VMEM, VMEM] + [ANY] * (3 + len(refs)),
        out_specs=(VMEM,) * (2 + len(term_keys)),
        scratch_shapes=[
            pltpu.VMEM((3 * LANES, width), BF),
            pltpu.VMEM((2, 2 * rows, len(term_keys) * LANES), BF),
            pltpu.SemaphoreType.DMA((copies_of(parts, part),)),
            pltpu.SemaphoreType.DMA((len(term_keys), 3)),
        ],
        compiler_params=params(40),
        cost_estimate=COST,
        name="rest",
    )(sc, after(gt, *far), dgu, x_own, dy_own, xp, *refs)
    term.update(zip(term_keys, got))
    sent = pc(send)

    p_in = send_on(1, 3, *p)
    p = ring(*p_in)
    o_in = send_on(0, 3, *o)
    o = ring(*o_in)

    quarter = rows // NX
    sent = after(sent, *o_in)
    mine = [keep[i * quarter : (i + 1) * quarter] for i in range(NX)]
    theirs = [sent[i * quarter : (i + 1) * quarter] for i in range(NX)]

    def pair(i):
        return mine[i].astype(F32) + theirs[i].astype(F32)

    acc = px(pair(3).astype(BF), -1)
    p_in = send_on(1, 2, *p)
    p = ring(*p_in)
    o_in = send_on(0, 2, *o)
    o = ring(*o_in)
    acc = px((pair(2) + after(acc, *p_in)).astype(BF), -1)
    acc = px((pair(1) + after(acc, *o_in)).astype(BF), -1)

    p_in = send_on(1, 1, *p)
    p = ring(*p_in)
    o_in = send_on(0, 1, *o)
    o = ring(*o_in)
    acc = pair(0) + after(acc, *p_in)
    half_rows = quarter // 2
    acc_b = acc[half_rows:].astype(BF)
    got = pyl(acc_b)

    sum_other = (term[1, 0].astype(F32) + p[0].astype(F32) + p[1].astype(F32)).astype(BF)
    got = after(got, sum_other)
    sum_other = pyl(sum_other)
    acc = acc[:half_rows] + got
    acc_b = acc[group:].astype(BF)
    got = pyh(acc_b)
    o = after(tuple(o), acc_b)
    sum_own = (term[0, 0].astype(F32) + o[0].astype(F32) + o[1].astype(F32)).astype(BF)
    in_grad = (acc[:group] + got).astype(BF).reshape(1, group, width)

    def whole(index):
        mine = sum_own[index * part : (index + 1) * part]
        theirs = sum_other[index * part : (index + 1) * part]
        return jnp.where(yl == 0, jnp.concatenate([mine, theirs]), jnp.concatenate([theirs, mine]))

    return in_grad, whole(0).T, whole(1).T, whole(2)


def solution(mesh):
    placed = (P("dp", None, None), P("dp", None, None), P("dp", "mp"), P("dp", "mp"), P("mp", "dp"))
    return jax.shard_map(
        local,
        mesh=mesh,
        in_specs=placed,
        out_specs=(P("dp", "mp", None), P("dp", "mp"), P("dp", "mp"), P("mp", "dp")),
        check_vma=False,
    )
```

```python
import functools

import jax
import jax.numpy as jnp
from jax import lax
from jax.experimental import pallas as pl
from jax.experimental.pallas import tpu as pltpu
from jax.sharding import PartitionSpec as P

BF = jnp.bfloat16
F32 = jnp.float32
NX, NZ = 4, 8
LANES = 256
ANY = pl.BlockSpec(memory_space=pl.ANY)
VMEM = pl.BlockSpec(memory_space=pltpu.VMEM)
COST = pl.CostEstimate(flops=1, bytes_accessed=1, transcendentals=0)
SMEM = pl.BlockSpec(memory_space=pltpu.SMEM)


def mm(left, right):
    return lax.dot_general(left, right, (((1,), (0,)), ((), ())), preferred_element_type=F32)


def mm_t(left, right):
    return lax.dot_general(left, right, (((1,), (1,)), ((), ())), preferred_element_type=F32)


def pz(value, step):
    pairs = [(y * NZ + z, y * NZ + (z + step) % NZ) for y in range(2) for z in range(NZ)]
    return lax.ppermute(value, "dp", pairs)


def pyl(value):
    return lax.ppermute(value, "dp", [(i, (i + NZ) % (2 * NZ)) for i in range(2 * NZ)])


def px(value, step):
    pairs = [
        (y * 8 + x * 2 + c, y * 8 + (x + (-step if c else step)) % NX * 2 + c)
        for y in range(2) for x in range(NX) for c in range(2)
    ]
    return lax.ppermute(value, "mp", pairs)


def pxs(value, step):
    pairs = [
        (y * 8 + x * 2 + c, y * 8 + (x + step) % NX * 2 + c)
        for y in range(2) for x in range(NX) for c in range(2)
    ]
    return lax.ppermute(value, "mp", pairs)


def pc(value):
    return lax.ppermute(value, "mp", [(i, i ^ 1) for i in range(16)])


def pyh(value):
    return lax.ppermute(value, "mp", [(i, i ^ 8) for i in range(16)])


def after(value, *others):
    return lax.optimization_barrier((value, *others))[0]


def after_all(*values):
    return lax.optimization_barrier(values)


def col_block(sc, k, s):
    yl = 1 - sc[1] if k else sc[1]
    return yl * NZ + lax.rem(sc[0] + s, NZ)


def offset(sc, k, s):
    return pl.multiple_of(col_block(sc, k, s) * LANES, LANES)


def spread(row, count, part):
    out, end = [], row + count
    while row < end:
        m = row // part
        n = min(end, (m + 1) * part) - row
        out.append((row, n, m * LANES + row - m * part))
        row += n
    return out


def load_chunks(where, places, part, refs, buf, sems):
    waits, sem = [], 0
    for parts, place in zip(where, places):
        mine = []
        for at, row, start, count in parts:
            for first, n, to in spread(start, count, part):
                copy = pltpu.make_async_copy(
                    refs[at].at[pl.ds(row + first - start, n)],
                    buf.at[pl.ds(to, n), pl.ds(place, LANES)],
                    sems.at[sem],
                )
                copy.start()
                mine.append(copy)
                sem += 1
        waits.append(mine)
    return waits


def copies_of(where, part):
    return sum(len(spread(start, count, part)) for parts in where for _, _, start, count in parts)


def clear_pad(buf, part):
    for m in range(3):
        buf[m * LANES + part : (m + 1) * LANES] = jnp.zeros((LANES - part, buf.shape[1]), BF)


def early_kernel(keys, missing, parts, n_pieces, piece_at, part, sc, x, dy, *refs):
    pieces, chunks = refs[:n_pieces], refs[n_pieces:-7]
    acc, xp, xs, buf, w_sems, x_sems, out_sem = refs[-7:]
    rows = x.shape[0]
    loads = [
        pltpu.make_async_copy(x, xs.at[0, pl.ds(0, rows)], x_sems.at[0]),
        pltpu.make_async_copy(dy, xs.at[1, pl.ds(0, rows)], x_sems.at[1]),
    ]
    row = rows
    pieces = [pieces[i].at[j] for i, j in piece_at]
    for i, piece in enumerate(pieces):
        n = piece.shape[1]
        loads.append(pltpu.make_async_copy(piece, xs.at[:, pl.ds(row, n)], x_sems.at[2 + i]))
        row += n
    for copy in loads:
        copy.start()
    waits = load_chunks(parts, [offset(sc, *key) for key in keys], part, chunks, buf, w_sems)
    clear_pad(buf, part)
    for key in missing:
        buf[:, pl.ds(offset(sc, *key), LANES)] = jnp.zeros((buf.shape[0], LANES), BF)
    for copy in loads:
        copy.wait()
    store = pltpu.make_async_copy(xs.at[:, pl.ds(rows, rows)], xp, out_sem)
    store.start()
    for mine in waits:
        for copy in mine:
            copy.wait()
    acc[:, : 2 * LANES] = mm_t(xs[0], buf[: 2 * LANES])
    acc[:, 2 * LANES :] = mm_t(xs[1], buf[2 * LANES :])
    store.wait()


def late_kernel(keys, parts, part, sc, acc, x, dy, xp, *refs):
    chunks = refs[:-10]
    gt, dgu, *far = refs[-10:-4]
    rowbuf, xb, buf, x_sems = refs[-4:]
    rows = x.shape[0]
    loads = []
    for i, (k, s) in enumerate(keys):
        cols, to = pl.ds(offset(sc, k, s), LANES), pl.ds(i * LANES, LANES)
        loads += [
            pltpu.make_async_copy(x.at[:, cols], xb.at[0, pl.ds(0, rows), to], x_sems.at[i, 0]),
            pltpu.make_async_copy(dy.at[:, cols], xb.at[1, pl.ds(0, rows), to], x_sems.at[i, 1]),
            pltpu.make_async_copy(xp.at[:, :, cols], xb.at[:, pl.ds(rows, rows), to], x_sems.at[i, 2]),
        ]
    for copy in loads:
        copy.start()
    clear_pad(buf, part)
    for i, pieces in enumerate(parts):
        for at, row, start, count in pieces:
            for first, n, to in spread(start, count, part):
                row_at = row + first - start
                buf[to : to + n, i * LANES : (i + 1) * LANES] = chunks[at][row_at : row_at + n]
    for copy in loads:
        copy.wait()
    both = acc[:, : 2 * LANES] + mm_t(xb[0], buf[: 2 * LANES])
    dhid = acc[:, 2 * LANES :] + mm_t(xb[1], buf[2 * LANES :])
    gate, up_val = both[:, :LANES], both[:, LANES:]
    sig = 1.0 / (1.0 + jnp.exp(-gate))
    silu = gate * sig
    hidden = silu * up_val
    dup = dhid * silu
    dgate = dhid * up_val * sig * (1.0 + gate * (1.0 - sig))
    for m, value in enumerate((dgate, dup, hidden)):
        gt[m * part : (m + 1) * part] = value.T[:part].astype(BF)
    mid = 3 * part // 2
    two = 2 * part
    for j in range(2):
        cols = slice((len(keys) - 2 + j) * LANES, (len(keys) - 1 + j) * LANES)
        top, low = mm(gt[:two], xb[0, :, cols]), mm(gt[two:], xb[1, :, cols])
        far[2 * j][...] = top[:mid].astype(BF)
        far[2 * j + 1][: two - mid] = top[mid:].astype(BF)
        far[2 * j + 1][two - mid :] = low.astype(BF)
    group = rows // 16
    for m, value in enumerate((dgate, dup)):
        rowbuf[...] = value.astype(BF)
        for g in range(16):
            to = g // 2 * 4 * group + g % 2 * group
            at = pl.multiple_of(sc[2 + g] * group, group)
            dgu[m, to : to + group] = rowbuf[pl.ds(at, group)]
        for g in range(8):
            to = g * 4 * group + 2 * group
            at = pl.multiple_of(rows + sc[18 + g] * 2 * group, 2 * group)
            dgu[m, to : to + 2 * group] = rowbuf[pl.ds(at, 2 * group)]


def rest_kernel(keys, parts, term_keys, part, sc, gt, dgu, x, dy, xp, *refs):
    n_out = len(term_keys) + 6
    chunks, (keep, send, *refs) = refs[:-n_out], refs[-n_out:]
    outs, (buf, xb, w_sems, x_sems) = refs[: len(term_keys)], refs[len(term_keys) :]
    rows = x.shape[0]
    waits = load_chunks(parts, [offset(sc, *key) for key in keys], part, chunks, buf, w_sems)
    slots = xb.shape[2] // (2 * LANES)

    def load(i):
        mine = []
        for j in range(2):
            k, s = term_keys[i + j]
            place = (i // 2 % slots) * 2 + j
            cols, to = pl.ds(offset(sc, k, s), LANES), pl.ds(place * LANES, LANES)
            mine += [
                pltpu.make_async_copy(x.at[:, cols], xb.at[0, pl.ds(0, rows), to], x_sems.at[place, 0]),
                pltpu.make_async_copy(dy.at[:, cols], xb.at[1, pl.ds(0, rows), to], x_sems.at[place, 1]),
                pltpu.make_async_copy(xp.at[:, :, cols], xb.at[:, pl.ds(rows, rows), to], x_sems.at[place, 2]),
            ]
        for copy in mine:
            copy.start()
        return mine

    loads = [load(2 * i) for i in range(slots)]
    clear_pad(buf, part)
    for mine in waits:
        for copy in mine:
            copy.wait()
    step = 4 * LANES
    for at in range(0, keep.shape[1], step):
        cols = slice(at, at + step)
        dx = mm(dgu[0], buf[:LANES, cols]) + mm(dgu[1], buf[LANES : 2 * LANES, cols])
        keep[:, cols] = dx[:rows].astype(BF)
        send[:, cols] = dx[rows:].astype(BF)
    two = 2 * part
    for i in range(0, len(term_keys), 2):
        for copy in loads[i // 2]:
            copy.wait()
        place = (i // 2 % slots) * 2 * LANES
        cols = slice(place, place + 2 * LANES)
        top = mm(gt[:two], xb[0, :, cols]).astype(BF)
        low = mm(gt[two:], xb[1, :, cols]).astype(BF)
        for j in range(2):
            outs[i + j][:two] = top[:, j * LANES : (j + 1) * LANES]
            outs[i + j][two:] = low[:, j * LANES : (j + 1) * LANES]
        if i + 2 * slots < len(term_keys):
            loads.append(load(i + 2 * slots))


def halves(array, index):
    rows = array.shape[0] // 2
    return (
        lax.dynamic_slice_in_dim(array, index * rows, rows, 0),
        lax.dynamic_slice_in_dim(array, (1 - index) * rows, rows, 0),
    )


def params(mib):
    return pltpu.CompilerParams(vmem_limit_bytes=mib * 1024 * 1024)


def local(inputs, out_grad, w_gate, w_up, w_down):
    rows, width = inputs.shape[1:]
    part = w_down.shape[0] // 2
    dp, mp = lax.axis_index("dp"), lax.axis_index("mp")
    yl, z = dp // NZ, dp % NZ
    yh, x, c = mp // 8, mp // 2 % NX, mp % 2
    group = rows // 16
    x_own, dy_own = inputs[0], out_grad[0]

    order = []
    for dc in range(2):
        sign = 1 - 2 * (c ^ dc)
        for dx in range(NX):
            for dh in range(2):
                order.append((yh ^ dh) * 8 + (x - sign * dx + NX) % NX * 2 + (c ^ dc))
    stands = [dc * NX + (NX - (1 - 2 * (c ^ dc)) * dx) % NX for dc in range(2) for dx in range(NX)]
    sc = jnp.stack([z, yl, *order, *stands]).astype(jnp.int32)

    wts = [halves(w, yl) for w in (w_gate.T, w_up.T, w_down)]
    own = jnp.concatenate([w[0] for w in wts])
    other = jnp.concatenate([w[1] for w in wts])
    mid = own.shape[0] // 2

    def rows_at(array, index):
        return lax.dynamic_slice_in_dim(array, index * group, group, 0)

    def piece(array):
        return jnp.concatenate([rows_at(array, mp), rows_at(array, mp ^ 8)])

    n = own.shape[0]
    up, down = pz(own, 1), pz(own, -1)
    other = pyl(other)
    chunks = {
        (0, 0): [(own, 0, 0, n)],
        (0, 7): [(up, 0, 0, n)],
        (0, 1): [(down, 0, 0, n)],
        (1, 0): [(other, 0, 0, n)],
    }
    first = jnp.stack([piece(after(x_own, own)), piece(after(dy_own, own))])
    first = pyl(after(first, up, down))
    up, down = jnp.concatenate([other, up]), jnp.concatenate([down, other])
    for step in (1, 2):
        up, down = pz(up, 1), pz(down, -1)
        chunks[1, NZ - step], chunks[0, NZ - step - 1] = [(up, 0, 0, n)], [(up, n, 0, n)]
        chunks[0, step + 1], chunks[1, step] = [(down, 0, 0, n)], [(down, n, 0, n)]
        up, down, first = after_all(up, down, first)
        if step == 1:
            left, right = pxs(first, 1), pxs(first, -1)
    far_x, far_dy = pxs(left[0], 1), pxs(right[1], -1)
    two_off = jnp.stack([far_x, far_dy])
    up, down, *sides = after_all(up, down, first, right, two_off, left)
    swap = pc(jnp.stack(sides))
    up, down = pz(up[: n + mid], 1), pz(down[mid:], -1)
    chunks[1, 5], chunks[1, 3] = [(up, 0, 0, n)], [(down, n - mid, 0, n)]
    chunks[0, 4] = [(up, n, 0, mid), (down, 0, mid, n - mid)]
    up, down = after_all(up, down)
    up, down = pz(up[:mid], 1), pz(down[n:], -1)
    chunks[1, 4] = [(up, 0, 0, mid), (down, 0, mid, n - mid)]
    pieces = [first[None], right[None], two_off[None], left[None], swap]
    piece_at = [(0, 0), (1, 0), (2, 0), (3, 0), (4, 0), (4, 1), (4, 2), (4, 3)]

    late = [(0, 4), (1, 4)]
    early = [key for key in chunks if key not in late]

    def listed(keys):
        refs, where = [], []
        for key in keys:
            parts = []
            for array, *rest in chunks[key]:
                at = [i for i, a in enumerate(refs) if a is array]
                if not at:
                    refs.append(array)
                parts.append((at[0] if at else len(refs) - 1, *rest))
            where.append(tuple(parts))
        return tuple(where), refs

    parts, refs = listed(early)
    acc, xp = pl.pallas_call(
        functools.partial(early_kernel, early, late, parts, len(pieces), piece_at, part),
        out_shape=(
            jax.ShapeDtypeStruct((2 * rows, 3 * LANES), F32),
            jax.ShapeDtypeStruct((2, rows, width), BF),
        ),
        in_specs=[SMEM] + [ANY] * (2 + len(pieces) + len(refs)),
        out_specs=(VMEM, ANY),
        scratch_shapes=[
            pltpu.VMEM((2, 2 * rows, width), BF),
            pltpu.VMEM((3 * LANES, width), BF),
            pltpu.SemaphoreType.DMA((copies_of(parts, part),)),
            pltpu.SemaphoreType.DMA((2 + 2 * NX,)),
            pltpu.SemaphoreType.DMA,
        ],
        compiler_params=params(22),
        cost_estimate=COST,
        name="early",
    )(sc, x_own, dy_own, *pieces, *refs)

    parts, refs = listed(late)
    full = jax.ShapeDtypeStruct((3 * part, LANES), BF)
    half = jax.ShapeDtypeStruct((mid, LANES), BF)
    gt, dgu, *far = pl.pallas_call(
        functools.partial(late_kernel, late, parts, part),
        out_shape=(
            jax.ShapeDtypeStruct((3 * part, 2 * rows), BF),
            jax.ShapeDtypeStruct((2, 2 * rows, LANES), BF),
            half, half, half, half,
        ),
        in_specs=[SMEM, VMEM] + [ANY] * 3 + [VMEM] * len(refs),
        out_specs=(VMEM,) * 6,
        scratch_shapes=[
            pltpu.VMEM((2 * rows, LANES), BF),
            pltpu.VMEM((2, 2 * rows, len(late) * LANES), BF),
            pltpu.VMEM((3 * LANES, len(late) * LANES), BF),
            pltpu.SemaphoreType.DMA((len(late), 3)),
        ],
        compiler_params=params(18),
        cost_estimate=COST,
        name="late",
    )(sc, acc, x_own, dy_own, xp, *refs)

    term = {}

    def send_on(k, s, up, down):
        if s == 3:
            up = jnp.concatenate([term[k, 3][:mid].astype(F32) + up, term[k, 3][mid:].astype(F32)])
            down = jnp.concatenate([term[k, 5][:mid].astype(F32), term[k, 5][mid:].astype(F32) + down])
        else:
            up, down = term[k, s].astype(F32) + up, term[k, NZ - s].astype(F32) + down
        return up.astype(BF), down.astype(BF)

    def ring(up, down):
        return pz(up, 1), pz(down, -1)

    p = ring(far[2], far[3])
    o = ring(far[0], far[1])

    keys = list(chunks)
    parts, refs = listed(keys)
    term_keys = [(k, s) for s in (3, 5, 2, 6, 1, 7, 0) for k in (1, 0)]
    keep, send, *got = pl.pallas_call(
        functools.partial(rest_kernel, keys, parts, term_keys, part),
        out_shape=(jax.ShapeDtypeStruct((rows, width), BF),) * 2 + (full,) * len(term_keys),
        in_specs=[SMEM, VMEM, VMEM] + [ANY] * (3 + len(refs)),
        out_specs=(VMEM,) * (2 + len(term_keys)),
        scratch_shapes=[
            pltpu.VMEM((3 * LANES, width), BF),
            pltpu.VMEM((2, 2 * rows, 6 * LANES), BF),
            pltpu.SemaphoreType.DMA((copies_of(parts, part),)),
            pltpu.SemaphoreType.DMA((6, 3)),
        ],
        compiler_params=params(26),
        cost_estimate=COST,
        name="rest",
    )(sc, after(gt, *far), dgu, x_own, dy_own, xp, *refs)
    term.update(zip(term_keys, got))

    *p, o_up, o_down = after_all(*p, *o)
    o = o_up, o_down
    p_in = send_on(1, 3, *p)
    p = ring(*p_in)
    sent = pc(after(send, *p_in))
    o_in = send_on(0, 3, *o)
    o = ring(*o_in)

    quarter = rows // NX
    sent = after(sent, *o_in)
    mine = [keep[i * quarter : (i + 1) * quarter] for i in range(NX)]
    theirs = [sent[i * quarter : (i + 1) * quarter] for i in range(NX)]

    def pair(i):
        return mine[i].astype(F32) + theirs[i].astype(F32)

    acc = px(pair(3).astype(BF), -1)
    p_in = send_on(1, 2, *p)
    p = ring(*p_in)
    o_in = send_on(0, 2, *o)
    o = ring(*o_in)
    acc = px((pair(2) + after(acc, *p_in)).astype(BF), -1)
    acc = px((pair(1) + after(acc, *o_in)).astype(BF), -1)

    p_in = send_on(1, 1, *p)
    p = ring(*p_in)
    o_in = send_on(0, 1, *o)
    o = ring(*o_in)
    acc = pair(0) + after(acc, *p_in)
    half_rows = quarter // 2
    acc_b = acc[half_rows:].astype(BF)
    got = pyl(acc_b)

    sum_other = (term[1, 0].astype(F32) + p[0].astype(F32) + p[1].astype(F32)).astype(BF)
    got = after(got, sum_other)
    sum_other = pyl(sum_other)
    acc = acc[:half_rows] + got
    acc_b = acc[group:].astype(BF)
    got = pyh(acc_b)
    o = after(tuple(o), acc_b)
    sum_own = (term[0, 0].astype(F32) + o[0].astype(F32) + o[1].astype(F32)).astype(BF)
    in_grad = (acc[:group] + got).astype(BF).reshape(1, group, width)

    def whole(index):
        mine = sum_own[index * part : (index + 1) * part]
        theirs = sum_other[index * part : (index + 1) * part]
        return jnp.where(yl == 0, jnp.concatenate([mine, theirs]), jnp.concatenate([theirs, mine]))

    return in_grad, whole(0).T, whole(1).T, whole(2)


def solution(mesh):
    placed = (P("dp", None, None), P("dp", None, None), P("dp", "mp"), P("dp", "mp"), P("mp", "dp"))
    return jax.shard_map(
        local,
        mesh=mesh,
        in_specs=placed,
        out_specs=(P("dp", "mp", None), P("dp", "mp"), P("dp", "mp"), P("mp", "dp")),
        check_vma=False,
    )
```

```python
import functools

import jax
import jax.numpy as jnp
from jax import lax
from jax.experimental import pallas as pl
from jax.experimental.pallas import tpu as pltpu
from jax.sharding import PartitionSpec as P

BF = jnp.bfloat16
F32 = jnp.float32
NX, NZ = 4, 8
LANES = 256
ANY = pl.BlockSpec(memory_space=pl.ANY)
HBM = pl.BlockSpec(memory_space=pltpu.HBM)
VMEM = pl.BlockSpec(memory_space=pltpu.VMEM)
COST = pl.CostEstimate(flops=1, bytes_accessed=1, transcendentals=0)
SMEM = pl.BlockSpec(memory_space=pltpu.SMEM)


def mm(left, right):
    return lax.dot_general(left, right, (((1,), (0,)), ((), ())), preferred_element_type=F32)


def mm_t(left, right):
    return lax.dot_general(left, right, (((1,), (1,)), ((), ())), preferred_element_type=F32)


def pz(value, step):
    pairs = [(y * NZ + z, y * NZ + (z + step) % NZ) for y in range(2) for z in range(NZ)]
    return lax.ppermute(value, "dp", pairs)


def pyl(value):
    return lax.ppermute(value, "dp", [(i, (i + NZ) % (2 * NZ)) for i in range(2 * NZ)])


def px(value, step):
    pairs = [
        (y * 8 + x * 2 + c, y * 8 + (x + (-step if c else step)) % NX * 2 + c)
        for y in range(2) for x in range(NX) for c in range(2)
    ]
    return lax.ppermute(value, "mp", pairs)


def pxs(value, step):
    pairs = [
        (y * 8 + x * 2 + c, y * 8 + (x + step) % NX * 2 + c)
        for y in range(2) for x in range(NX) for c in range(2)
    ]
    return lax.ppermute(value, "mp", pairs)


def pc(value):
    return lax.ppermute(value, "mp", [(i, i ^ 1) for i in range(16)])


def pyh(value):
    return lax.ppermute(value, "mp", [(i, i ^ 8) for i in range(16)])


def pboth(value):
    n = 2 * NZ
    pairs = [(m * n + d, (m ^ 8) * n + (d + NZ) % n) for m in range(16) for d in range(n)]
    return lax.ppermute(value, ("mp", "dp"), pairs)


def after(value, *others):
    return lax.optimization_barrier((value, *others))[0]


def after_all(*values):
    return lax.optimization_barrier(values)


def col_block(sc, k, s):
    yl = 1 - sc[1] if k else sc[1]
    return yl * NZ + lax.rem(sc[0] + s, NZ)


def offset(sc, k, s):
    return pl.multiple_of(col_block(sc, k, s) * LANES, LANES)


def spread(row, count, part):
    out, end = [], row + count
    while row < end:
        m = row // part
        n = min(end, (m + 1) * part) - row
        out.append((row, n, m * LANES + row - m * part))
        row += n
    return out


def load_chunks(where, places, part, refs, buf, sems):
    waits, sem = [], 0
    for parts, place in zip(where, places):
        mine = []
        for at, row, start, count in parts:
            for first, n, to in spread(start, count, part):
                copy = pltpu.make_async_copy(
                    refs[at].at[pl.ds(row + first - start, n)],
                    buf.at[pl.ds(to, n), pl.ds(place, LANES)],
                    sems.at[sem],
                )
                copy.start()
                mine.append(copy)
                sem += 1
        waits.append(mine)
    return waits


def copies_of(where, part):
    return sum(len(spread(start, count, part)) for parts in where for _, _, start, count in parts)


def clear_pad(buf, part):
    for m in range(3):
        buf[m * LANES + part : (m + 1) * LANES] = jnp.zeros((LANES - part, buf.shape[1]), BF)


def early_kernel(keys, missing, parts, n_pieces, piece_at, part, sc, x, dy, *refs):
    pieces, chunks = refs[:n_pieces], refs[n_pieces:-7]
    acc, xp, xs, buf, w_sems, x_sems, out_sem = refs[-7:]
    rows = x.shape[0]
    loads = [
        pltpu.make_async_copy(x, xs.at[0, pl.ds(0, rows)], x_sems.at[0]),
        pltpu.make_async_copy(dy, xs.at[1, pl.ds(0, rows)], x_sems.at[1]),
    ]
    row = rows
    pieces = [pieces[i].at[j] for i, j in piece_at]
    for i, piece in enumerate(pieces):
        n = piece.shape[1]
        loads.append(pltpu.make_async_copy(piece, xs.at[:, pl.ds(row, n)], x_sems.at[2 + i]))
        row += n
    for copy in loads:
        copy.start()
    waits = load_chunks(parts, [offset(sc, *key) for key in keys], part, chunks, buf, w_sems)
    clear_pad(buf, part)
    for key in missing:
        buf[:, pl.ds(offset(sc, *key), LANES)] = jnp.zeros((buf.shape[0], LANES), BF)
    for copy in loads:
        copy.wait()
    store = pltpu.make_async_copy(xs.at[:, pl.ds(rows, rows)], xp, out_sem)
    store.start()
    for mine in waits:
        for copy in mine:
            copy.wait()
    acc[:, : 2 * LANES] = mm_t(xs[0], buf[: 2 * LANES])
    acc[:, 2 * LANES :] = mm_t(xs[1], buf[2 * LANES :])
    store.wait()


def late_kernel(keys, parts, part, sc, acc, x, dy, xp, *refs):
    chunks = refs[:-10]
    gt, dgu, *far = refs[-10:-4]
    rowbuf, xb, buf, x_sems = refs[-4:]
    rows = x.shape[0]
    loads = []
    for i, (k, s) in enumerate(keys):
        cols, to = pl.ds(offset(sc, k, s), LANES), pl.ds(i * LANES, LANES)
        loads += [
            pltpu.make_async_copy(x.at[:, cols], xb.at[0, pl.ds(0, rows), to], x_sems.at[i, 0]),
            pltpu.make_async_copy(dy.at[:, cols], xb.at[1, pl.ds(0, rows), to], x_sems.at[i, 1]),
            pltpu.make_async_copy(xp.at[:, :, cols], xb.at[:, pl.ds(rows, rows), to], x_sems.at[i, 2]),
        ]
    for copy in loads:
        copy.start()
    clear_pad(buf, part)
    for i, pieces in enumerate(parts):
        for at, row, start, count in pieces:
            for first, n, to in spread(start, count, part):
                row_at = row + first - start
                buf[to : to + n, i * LANES : (i + 1) * LANES] = chunks[at][row_at : row_at + n]
    for copy in loads:
        copy.wait()
    both = acc[:, : 2 * LANES] + mm_t(xb[0], buf[: 2 * LANES])
    dhid = acc[:, 2 * LANES :] + mm_t(xb[1], buf[2 * LANES :])
    gate, up_val = both[:, :LANES], both[:, LANES:]
    sig = 1.0 / (1.0 + jnp.exp(-gate))
    silu = gate * sig
    hidden = silu * up_val
    dup = dhid * silu
    dgate = dhid * up_val * sig * (1.0 + gate * (1.0 - sig))
    for m, value in enumerate((dgate, dup, hidden)):
        gt[m * part : (m + 1) * part] = value.T[:part].astype(BF)
    mid = 3 * part // 2
    two = 2 * part
    for j in range(2):
        cols = slice((len(keys) - 2 + j) * LANES, (len(keys) - 1 + j) * LANES)
        top, low = mm(gt[:two], xb[0, :, cols]), mm(gt[two:], xb[1, :, cols])
        far[2 * j][...] = top[:mid].astype(BF)
        far[2 * j + 1][: two - mid] = top[mid:].astype(BF)
        far[2 * j + 1][two - mid :] = low.astype(BF)
    group = rows // 16
    for m, value in enumerate((dgate, dup)):
        rowbuf[...] = value.astype(BF)
        for g in range(16):
            to = g // 2 * 4 * group + g % 2 * group
            at = pl.multiple_of(sc[2 + g] * group, group)
            dgu[m, to : to + group] = rowbuf[pl.ds(at, group)]
        for g in range(8):
            to = g * 4 * group + 2 * group
            at = pl.multiple_of(rows + sc[18 + g] * 2 * group, 2 * group)
            dgu[m, to : to + 2 * group] = rowbuf[pl.ds(at, 2 * group)]


def rest_kernel(keys, parts, term_keys, part, sc, gt, dgu, x, dy, xp, *refs):
    n_out = len(term_keys) + 6
    chunks, (keep, send, *refs) = refs[:-n_out], refs[-n_out:]
    outs, (buf, xb, w_sems, x_sems) = refs[: len(term_keys)], refs[len(term_keys) :]
    rows = x.shape[0]
    waits = load_chunks(parts, [offset(sc, *key) for key in keys], part, chunks, buf, w_sems)
    slots = xb.shape[2] // (2 * LANES)

    def load(i):
        mine = []
        for j in range(2):
            k, s = term_keys[i + j]
            place = (i // 2 % slots) * 2 + j
            cols, to = pl.ds(offset(sc, k, s), LANES), pl.ds(place * LANES, LANES)
            mine += [
                pltpu.make_async_copy(x.at[:, cols], xb.at[0, pl.ds(0, rows), to], x_sems.at[place, 0]),
                pltpu.make_async_copy(dy.at[:, cols], xb.at[1, pl.ds(0, rows), to], x_sems.at[place, 1]),
                pltpu.make_async_copy(xp.at[:, :, cols], xb.at[:, pl.ds(rows, rows), to], x_sems.at[place, 2]),
            ]
        for copy in mine:
            copy.start()
        return mine

    loads = [load(2 * i) for i in range(slots)]
    clear_pad(buf, part)
    for mine in waits:
        for copy in mine:
            copy.wait()
    step = 4 * LANES
    for at in range(0, keep.shape[1], step):
        cols = slice(at, at + step)
        dx = mm(dgu[0], buf[:LANES, cols]) + mm(dgu[1], buf[LANES : 2 * LANES, cols])
        keep[:, cols] = dx[:rows].astype(BF)
        send[:, cols] = dx[rows:].astype(BF)
    two = 2 * part
    for i in range(0, len(term_keys), 2):
        for copy in loads[i // 2]:
            copy.wait()
        place = (i // 2 % slots) * 2 * LANES
        cols = slice(place, place + 2 * LANES)
        top = mm(gt[:two], xb[0, :, cols]).astype(BF)
        low = mm(gt[two:], xb[1, :, cols]).astype(BF)
        for j in range(2):
            outs[i + j][:two] = top[:, j * LANES : (j + 1) * LANES]
            outs[i + j][two:] = low[:, j * LANES : (j + 1) * LANES]
        if i + 2 * slots < len(term_keys):
            loads.append(load(i + 2 * slots))


def halves(array, index):
    rows = array.shape[0] // 2
    return (
        lax.dynamic_slice_in_dim(array, index * rows, rows, 0),
        lax.dynamic_slice_in_dim(array, (1 - index) * rows, rows, 0),
    )


def params(mib):
    return pltpu.CompilerParams(vmem_limit_bytes=mib * 1024 * 1024)


def local(inputs, out_grad, w_gate, w_up, w_down):
    rows, width = inputs.shape[1:]
    part = w_down.shape[0] // 2
    dp, mp = lax.axis_index("dp"), lax.axis_index("mp")
    yl, z = dp // NZ, dp % NZ
    yh, x, c = mp // 8, mp // 2 % NX, mp % 2
    group = rows // 16
    x_own, dy_own = inputs[0], out_grad[0]

    order = []
    for dc in range(2):
        sign = 1 - 2 * (c ^ dc)
        for dx in range(NX):
            for dh in range(2):
                order.append((yh ^ dh) * 8 + (x - sign * dx + NX) % NX * 2 + (c ^ dc))
    stands = [dc * NX + (NX - (1 - 2 * (c ^ dc)) * dx) % NX for dc in range(2) for dx in range(NX)]
    sc = jnp.stack([z, yl, *order, *stands]).astype(jnp.int32)

    wts = [halves(w, yl) for w in (w_gate.T, w_up.T, w_down)]
    own = jnp.concatenate([w[0] for w in wts])
    other = jnp.concatenate([w[1] for w in wts])
    mid = own.shape[0] // 2

    def rows_at(array, index):
        return lax.dynamic_slice_in_dim(array, index * group, group, 0)

    def piece(array):
        return jnp.concatenate([rows_at(array, mp), rows_at(array, mp ^ 8)])

    n = own.shape[0]
    up, down = pz(own, 1), pz(own, -1)
    other = pyl(other)
    chunks = {
        (0, 0): [(own, 0, 0, n)],
        (0, 7): [(up, 0, 0, n)],
        (0, 1): [(down, 0, 0, n)],
        (1, 0): [(other, 0, 0, n)],
    }
    first = jnp.stack([piece(after(x_own, own)), piece(after(dy_own, own))])
    first = pyl(after(first, up, down))
    up, down = jnp.concatenate([other, up]), jnp.concatenate([down, other])
    for step in (1, 2):
        up, down = pz(up, 1), pz(down, -1)
        chunks[1, NZ - step], chunks[0, NZ - step - 1] = [(up, 0, 0, n)], [(up, n, 0, n)]
        chunks[0, step + 1], chunks[1, step] = [(down, 0, 0, n)], [(down, n, 0, n)]
        up, down, first = after_all(up, down, first)
        if step == 1:
            left, right = pxs(first, 1), pxs(first, -1)
    far_x, far_dy = pxs(left[0], 1), pxs(right[1], -1)
    two_off = jnp.stack([far_x, far_dy])
    up, down, *sides = after_all(up, down, first, right, two_off, left)
    swap = pc(jnp.stack(sides))
    up, down = pz(up[: n + mid], 1), pz(down[mid:], -1)
    chunks[1, 5], chunks[1, 3] = [(up, 0, 0, n)], [(down, n - mid, 0, n)]
    chunks[0, 4] = [(up, n, 0, mid), (down, 0, mid, n - mid)]
    up, down = after_all(up, down)
    up, down = pz(up[:mid], 1), pz(down[n:], -1)
    chunks[1, 4] = [(up, 0, 0, mid), (down, 0, mid, n - mid)]
    pieces = [first[None], right[None], two_off[None], left[None], swap]
    piece_at = [(0, 0), (1, 0), (2, 0), (3, 0), (4, 0), (4, 1), (4, 2), (4, 3)]

    late = [(0, 4), (1, 4)]
    early = [key for key in chunks if key not in late]

    def listed(keys):
        refs, where = [], []
        for key in keys:
            parts = []
            for array, *rest in chunks[key]:
                at = [i for i, a in enumerate(refs) if a is array]
                if not at:
                    refs.append(array)
                parts.append((at[0] if at else len(refs) - 1, *rest))
            where.append(tuple(parts))
        return tuple(where), refs

    parts, refs = listed(early)
    acc, xp = pl.pallas_call(
        functools.partial(early_kernel, early, late, parts, len(pieces), piece_at, part),
        out_shape=(
            jax.ShapeDtypeStruct((2 * rows, 3 * LANES), F32),
            jax.ShapeDtypeStruct((2, rows, width), BF),
        ),
        in_specs=[SMEM] + [HBM] * (2 + len(pieces) + len(refs)),
        out_specs=(VMEM, ANY),
        scratch_shapes=[
            pltpu.VMEM((2, 2 * rows, width), BF),
            pltpu.VMEM((3 * LANES, width), BF),
            pltpu.SemaphoreType.DMA((copies_of(parts, part),)),
            pltpu.SemaphoreType.DMA((2 + 2 * NX,)),
            pltpu.SemaphoreType.DMA,
        ],
        compiler_params=params(22),
        cost_estimate=COST,
        name="early",
    )(sc, x_own, dy_own, *pieces, *refs)

    parts, refs = listed(late)
    full = jax.ShapeDtypeStruct((3 * part, LANES), BF)
    half = jax.ShapeDtypeStruct((mid, LANES), BF)
    gt, dgu, *far = pl.pallas_call(
        functools.partial(late_kernel, late, parts, part),
        out_shape=(
            jax.ShapeDtypeStruct((3 * part, 2 * rows), BF),
            jax.ShapeDtypeStruct((2, 2 * rows, LANES), BF),
            half, half, half, half,
        ),
        in_specs=[SMEM, VMEM] + [ANY] * 3 + [VMEM] * len(refs),
        out_specs=(VMEM,) * 6,
        scratch_shapes=[
            pltpu.VMEM((2 * rows, LANES), BF),
            pltpu.VMEM((2, 2 * rows, len(late) * LANES), BF),
            pltpu.VMEM((3 * LANES, len(late) * LANES), BF),
            pltpu.SemaphoreType.DMA((len(late), 3)),
        ],
        compiler_params=params(18),
        cost_estimate=COST,
        name="late",
    )(sc, acc, x_own, dy_own, xp, *refs)

    term = {}

    def send_on(k, s, up, down):
        if s == 3:
            up = jnp.concatenate([term[k, 3][:mid].astype(F32) + up, term[k, 3][mid:].astype(F32)])
            down = jnp.concatenate([term[k, 5][:mid].astype(F32), term[k, 5][mid:].astype(F32) + down])
        else:
            up, down = term[k, s].astype(F32) + up, term[k, NZ - s].astype(F32) + down
        return up.astype(BF), down.astype(BF)

    def ring(up, down):
        return pz(up, 1), pz(down, -1)

    p = ring(far[2], far[3])
    o = ring(far[0], far[1])

    keys = list(chunks)
    parts, refs = listed(keys)
    term_keys = [(k, s) for s in (3, 5, 2, 6, 1, 7, 0) for k in (1, 0)]
    keep, send, *got = pl.pallas_call(
        functools.partial(rest_kernel, keys, parts, term_keys, part),
        out_shape=(jax.ShapeDtypeStruct((rows, width), BF),) * 2 + (full,) * len(term_keys),
        in_specs=[SMEM, VMEM, VMEM] + [ANY] * 3 + [HBM] * len(refs),
        out_specs=(VMEM,) * (2 + len(term_keys)),
        scratch_shapes=[
            pltpu.VMEM((3 * LANES, width), BF),
            pltpu.VMEM((2, 2 * rows, 6 * LANES), BF),
            pltpu.SemaphoreType.DMA((copies_of(parts, part),)),
            pltpu.SemaphoreType.DMA((6, 3)),
        ],
        compiler_params=params(26),
        cost_estimate=COST,
        name="rest",
    )(sc, after(gt, *far), dgu, x_own, dy_own, xp, *refs)
    term.update(zip(term_keys, got))

    *p, o_up, o_down = after_all(*p, *o)
    o = o_up, o_down
    p_in = send_on(1, 3, *p)
    p = ring(*p_in)
    sent = pc(after(send, *p_in))
    o_in = send_on(0, 3, *o)
    o = ring(*o_in)

    quarter = rows // NX
    sent = after(sent, *o_in)
    mine = [keep[i * quarter : (i + 1) * quarter] for i in range(NX)]
    theirs = [sent[i * quarter : (i + 1) * quarter] for i in range(NX)]

    def pair(i):
        return mine[i].astype(F32) + theirs[i].astype(F32)

    acc = px(pair(3).astype(BF), -1)
    p_in = send_on(1, 2, *p)
    p = ring(*p_in)
    o_in = send_on(0, 2, *o)
    o = ring(*o_in)
    acc = px((pair(2) + after(acc, *p_in)).astype(BF), -1)
    acc = px((pair(1) + after(acc, *o_in)).astype(BF), -1)

    p_in = send_on(1, 1, *p)
    p = ring(*p_in)
    o_in = send_on(0, 1, *o)
    o = ring(*o_in)
    acc = pair(0) + after(acc, *p_in)
    part_b = [acc[i * group : (i + 1) * group].astype(BF) for i in range(1, 4)]
    got = [pyh(part_b[0]), pyl(part_b[1]), pboth(part_b[2])]

    sum_other = (term[1, 0].astype(F32) + p[0].astype(F32) + p[1].astype(F32)).astype(BF)
    sum_other = pyl(sum_other)
    o = after(tuple(o), *part_b)
    sum_own = (term[0, 0].astype(F32) + o[0].astype(F32) + o[1].astype(F32)).astype(BF)
    in_grad = (acc[:group] + got[0] + got[1] + got[2]).astype(BF).reshape(1, group, width)

    def whole(index):
        mine = sum_own[index * part : (index + 1) * part]
        theirs = sum_other[index * part : (index + 1) * part]
        return jnp.where(yl == 0, jnp.concatenate([mine, theirs]), jnp.concatenate([theirs, mine]))

    return in_grad, whole(0).T, whole(1).T, whole(2)


def solution(mesh):
    placed = (P("dp", None, None), P("dp", None, None), P("dp", "mp"), P("dp", "mp"), P("mp", "dp"))
    return jax.shard_map(
        local,
        mesh=mesh,
        in_specs=placed,
        out_specs=(P("dp", "mp", None), P("dp", "mp"), P("dp", "mp"), P("mp", "dp")),
        check_vma=False,
    )
```

```python
import functools

import jax
import jax.numpy as jnp
from jax import lax
from jax.experimental import pallas as pl
from jax.experimental.pallas import tpu as pltpu
from jax.sharding import PartitionSpec as P

BF = jnp.bfloat16
F32 = jnp.float32
NX, NZ = 4, 8
LANES = 256
ANY = pl.BlockSpec(memory_space=pl.ANY)
HBM = pl.BlockSpec(memory_space=pltpu.HBM)
VMEM = pl.BlockSpec(memory_space=pltpu.VMEM)
COST = pl.CostEstimate(flops=1, bytes_accessed=1, transcendentals=0)
SMEM = pl.BlockSpec(memory_space=pltpu.SMEM)


def mm(left, right):
    return lax.dot_general(left, right, (((1,), (0,)), ((), ())), preferred_element_type=F32)


def mm_t(left, right):
    return lax.dot_general(left, right, (((1,), (1,)), ((), ())), preferred_element_type=F32)


def pz(value, step):
    pairs = [(y * NZ + z, y * NZ + (z + step) % NZ) for y in range(2) for z in range(NZ)]
    return lax.ppermute(value, "dp", pairs)


def pyl(value):
    return lax.ppermute(value, "dp", [(i, (i + NZ) % (2 * NZ)) for i in range(2 * NZ)])


def px(value, step):
    pairs = [
        (y * 8 + x * 2 + c, y * 8 + (x + (-step if c else step)) % NX * 2 + c)
        for y in range(2) for x in range(NX) for c in range(2)
    ]
    return lax.ppermute(value, "mp", pairs)


def pxs(value, step):
    pairs = [
        (y * 8 + x * 2 + c, y * 8 + (x + step) % NX * 2 + c)
        for y in range(2) for x in range(NX) for c in range(2)
    ]
    return lax.ppermute(value, "mp", pairs)


def pc(value):
    return lax.ppermute(value, "mp", [(i, i ^ 1) for i in range(16)])


def pyh(value):
    return lax.ppermute(value, "mp", [(i, i ^ 8) for i in range(16)])


def pboth(value):
    n = 2 * NZ
    pairs = [(m * n + d, (m ^ 8) * n + (d + NZ) % n) for m in range(16) for d in range(n)]
    return lax.ppermute(value, ("mp", "dp"), pairs)


def after(value, *others):
    return lax.optimization_barrier((value, *others))[0]


def after_all(*values):
    return lax.optimization_barrier(values)


def col_block(sc, k, s):
    yl = 1 - sc[1] if k else sc[1]
    return yl * NZ + lax.rem(sc[0] + s, NZ)


def offset(sc, k, s):
    return pl.multiple_of(col_block(sc, k, s) * LANES, LANES)


def spread(row, count, part):
    out, end = [], row + count
    while row < end:
        m = row // part
        n = min(end, (m + 1) * part) - row
        out.append((row, n, m * LANES + row - m * part))
        row += n
    return out


def load_chunks(where, places, part, refs, buf, sems):
    waits, sem = [], 0
    for parts, place in zip(where, places):
        mine = []
        for at, row, start, count in parts:
            for first, n, to in spread(start, count, part):
                copy = pltpu.make_async_copy(
                    refs[at].at[pl.ds(row + first - start, n)],
                    buf.at[pl.ds(to, n), pl.ds(place, LANES)],
                    sems.at[sem],
                )
                copy.start()
                mine.append(copy)
                sem += 1
        waits.append(mine)
    return waits


def copies_of(where, part):
    return sum(len(spread(start, count, part)) for parts in where for _, _, start, count in parts)


def clear_pad(buf, part):
    for m in range(3):
        buf[m * LANES + part : (m + 1) * LANES] = jnp.zeros((LANES - part, buf.shape[1]), BF)


def early_kernel(keys, missing, parts, n_pieces, piece_at, part, sc, x, dy, *refs):
    pieces, chunks = refs[:n_pieces], refs[n_pieces:-7]
    acc, xp, xs, buf, w_sems, x_sems, out_sem = refs[-7:]
    rows = x.shape[0]
    loads = [
        pltpu.make_async_copy(x, xs.at[0, pl.ds(0, rows)], x_sems.at[0]),
        pltpu.make_async_copy(dy, xs.at[1, pl.ds(0, rows)], x_sems.at[1]),
    ]
    row = rows
    pieces = [pieces[i].at[j] for i, j in piece_at]
    for i, piece in enumerate(pieces):
        n = piece.shape[1]
        loads.append(pltpu.make_async_copy(piece, xs.at[:, pl.ds(row, n)], x_sems.at[2 + i]))
        row += n
    for copy in loads:
        copy.start()
    waits = load_chunks(parts, [offset(sc, *key) for key in keys], part, chunks, buf, w_sems)
    clear_pad(buf, part)
    for key in missing:
        buf[:, pl.ds(offset(sc, *key), LANES)] = jnp.zeros((buf.shape[0], LANES), BF)
    for copy in loads:
        copy.wait()
    store = pltpu.make_async_copy(xs.at[:, pl.ds(rows, rows)], xp, out_sem)
    store.start()
    for mine in waits:
        for copy in mine:
            copy.wait()
    acc[:, : 2 * LANES] = mm_t(xs[0], buf[: 2 * LANES])
    acc[:, 2 * LANES :] = mm_t(xs[1], buf[2 * LANES :])
    store.wait()


def put_terms(outs, part, top, low):
    two, n = 2 * part, 3 * part
    top, low = top.astype(BF), low.astype(BF)
    for j, out in enumerate(outs):
        for k in range(2):
            cols = slice((2 * j + k) * LANES, (2 * j + k + 1) * LANES)
            out[k * n : k * n + two] = top[:, cols]
            out[k * n + two : (k + 1) * n] = low[:, cols]


def late_kernel(keys, parts, term_keys, part, sc, acc, x, dy, xp, *refs):
    n_out = 8 + len(term_keys) // 2
    chunks = refs[:-n_out]
    gt, dgu, *outs = refs[-n_out:-4]
    far, outs = outs[:2], outs[2:]
    rowbuf, xb, buf, x_sems = refs[-4:]
    rows = x.shape[0]
    loads = []
    for i, (k, s) in enumerate(keys + term_keys):
        cols, to = pl.ds(offset(sc, k, s), LANES), pl.ds(i * LANES, LANES)
        loads += [
            pltpu.make_async_copy(x.at[:, cols], xb.at[0, pl.ds(0, rows), to], x_sems.at[i, 0]),
            pltpu.make_async_copy(dy.at[:, cols], xb.at[1, pl.ds(0, rows), to], x_sems.at[i, 1]),
            pltpu.make_async_copy(xp.at[:, :, cols], xb.at[:, pl.ds(rows, rows), to], x_sems.at[i, 2]),
        ]
    for copy in loads:
        copy.start()
    clear_pad(buf, part)
    for i, pieces in enumerate(parts):
        for at, row, start, count in pieces:
            for first, n, to in spread(start, count, part):
                row_at = row + first - start
                buf[to : to + n, i * LANES : (i + 1) * LANES] = chunks[at][row_at : row_at + n]
    for copy in loads[: 3 * len(keys)]:
        copy.wait()
    used = len(keys) * LANES
    both = acc[:, : 2 * LANES] + mm_t(xb[0, :, :used], buf[: 2 * LANES])
    dhid = acc[:, 2 * LANES :] + mm_t(xb[1, :, :used], buf[2 * LANES :])
    gate, up_val = both[:, :LANES], both[:, LANES:]
    sig = 1.0 / (1.0 + jnp.exp(-gate))
    silu = gate * sig
    hidden = silu * up_val
    dup = dhid * silu
    dgate = dhid * up_val * sig * (1.0 + gate * (1.0 - sig))
    for m, value in enumerate((dgate, dup, hidden)):
        gt[m * part : (m + 1) * part] = value.T[:part].astype(BF)
    mid = 3 * part // 2
    two = 2 * part
    up, down = far
    for j in range(2):
        cols = slice(j * LANES, (j + 1) * LANES)
        top, low = mm(gt[:two], xb[0, :, cols]), mm(gt[two:], xb[1, :, cols])
        at = j * mid
        up[at : at + mid] = top[:mid].astype(BF)
        down[at : at + two - mid] = top[mid:].astype(BF)
        down[at + two - mid : at + mid] = low.astype(BF)
    for copy in loads[3 * len(keys) :]:
        copy.wait()
    put_terms(outs, part, mm(gt[:two], xb[0, :, used:]), mm(gt[two:], xb[1, :, used:]))
    group = rows // 16
    for m, value in enumerate((dgate, dup)):
        rowbuf[...] = value.astype(BF)
        for g in range(16):
            to = g // 2 * 4 * group + g % 2 * group
            at = pl.multiple_of(sc[2 + g] * group, group)
            dgu[m, to : to + group] = rowbuf[pl.ds(at, group)]
        for g in range(8):
            to = g * 4 * group + 2 * group
            at = pl.multiple_of(rows + sc[18 + g] * 2 * group, 2 * group)
            dgu[m, to : to + 2 * group] = rowbuf[pl.ds(at, 2 * group)]


def dx_kernel(keys, parts, part, sc, dgu, *refs):
    chunks, (keep, send, buf, w_sems) = refs[:-4], refs[-4:]
    rows = keep.shape[0]
    waits = load_chunks(parts, [offset(sc, *key) for key in keys], part, chunks, buf, w_sems)
    clear_pad(buf, part)
    for mine in waits:
        for copy in mine:
            copy.wait()
    step = 4 * LANES
    for at in range(0, keep.shape[1], step):
        cols = slice(at, at + step)
        dx = mm(dgu[0], buf[:LANES, cols]) + mm(dgu[1], buf[LANES : 2 * LANES, cols])
        keep[:, cols] = dx[:rows].astype(BF)
        send[:, cols] = dx[rows:].astype(BF)


def terms_kernel(keys, part, sc, gt, x, dy, xp, *refs):
    outs, (xb, x_sems) = refs[:-2], refs[-2:]
    rows = x.shape[0]
    loads = []
    for i, (k, s) in enumerate(keys):
        cols, to = pl.ds(offset(sc, k, s), LANES), pl.ds(i * LANES, LANES)
        mine = [
            pltpu.make_async_copy(x.at[:, cols], xb.at[0, pl.ds(0, rows), to], x_sems.at[i, 0]),
            pltpu.make_async_copy(dy.at[:, cols], xb.at[1, pl.ds(0, rows), to], x_sems.at[i, 1]),
            pltpu.make_async_copy(xp.at[:, :, cols], xb.at[:, pl.ds(rows, rows), to], x_sems.at[i, 2]),
        ]
        for copy in mine:
            copy.start()
        loads.append(mine)
    two = 2 * part
    for i in range(0, len(keys), 2):
        for copy in loads[i] + loads[i + 1]:
            copy.wait()
        cols = slice(i * LANES, (i + 2) * LANES)
        put_terms(outs[i // 2 : i // 2 + 1], part, mm(gt[:two], xb[0, :, cols]), mm(gt[two:], xb[1, :, cols]))


def halves(array, index):
    rows = array.shape[0] // 2
    return (
        lax.dynamic_slice_in_dim(array, index * rows, rows, 0),
        lax.dynamic_slice_in_dim(array, (1 - index) * rows, rows, 0),
    )


def params(mib):
    return pltpu.CompilerParams(vmem_limit_bytes=mib * 1024 * 1024)


def local(inputs, out_grad, w_gate, w_up, w_down):
    rows, width = inputs.shape[1:]
    part = w_down.shape[0] // 2
    dp, mp = lax.axis_index("dp"), lax.axis_index("mp")
    yl, z = dp // NZ, dp % NZ
    yh, x, c = mp // 8, mp // 2 % NX, mp % 2
    group = rows // 16
    x_own, dy_own = inputs[0], out_grad[0]

    order = []
    for dc in range(2):
        sign = 1 - 2 * (c ^ dc)
        for dx in range(NX):
            for dh in range(2):
                order.append((yh ^ dh) * 8 + (x - sign * dx + NX) % NX * 2 + (c ^ dc))
    stands = [dc * NX + (NX - (1 - 2 * (c ^ dc)) * dx) % NX for dc in range(2) for dx in range(NX)]
    sc = jnp.stack([z, yl, *order, *stands]).astype(jnp.int32)

    wts = [halves(w, yl) for w in (w_gate.T, w_up.T, w_down)]
    own = jnp.concatenate([w[0] for w in wts])
    other = jnp.concatenate([w[1] for w in wts])
    mid = own.shape[0] // 2

    def rows_at(array, index):
        return lax.dynamic_slice_in_dim(array, index * group, group, 0)

    def piece(array):
        return jnp.concatenate([rows_at(array, mp), rows_at(array, mp ^ 8)])

    n = own.shape[0]
    up, down = pz(own, 1), pz(own, -1)
    other = pyl(other)
    chunks = {
        (0, 0): [(own, 0, 0, n)],
        (0, 7): [(up, 0, 0, n)],
        (0, 1): [(down, 0, 0, n)],
        (1, 0): [(other, 0, 0, n)],
    }
    first = jnp.stack([piece(after(x_own, own)), piece(after(dy_own, own))])
    first = pyl(after(first, up, down))
    up, down = jnp.concatenate([other, up]), jnp.concatenate([down, other])
    for step in (1, 2):
        up, down = pz(up, 1), pz(down, -1)
        chunks[1, NZ - step], chunks[0, NZ - step - 1] = [(up, 0, 0, n)], [(up, n, 0, n)]
        chunks[0, step + 1], chunks[1, step] = [(down, 0, 0, n)], [(down, n, 0, n)]
        up, down, first = after_all(up, down, first)
        if step == 1:
            left, right = pxs(first, 1), pxs(first, -1)
    far_x, far_dy = pxs(left[0], 1), pxs(right[1], -1)
    two_off = jnp.stack([far_x, far_dy])
    up, down, *sides = after_all(up, down, first, right, two_off, left)
    swap = pc(jnp.stack(sides))
    up, down = pz(up[: n + mid], 1), pz(down[mid:], -1)
    chunks[1, 5], chunks[1, 3] = [(up, 0, 0, n)], [(down, n - mid, 0, n)]
    chunks[0, 4] = [(up, n, 0, mid), (down, 0, mid, n - mid)]
    up, down = after_all(up, down)
    up, down = pz(up[:mid], 1), pz(down[n:], -1)
    chunks[1, 4] = [(up, 0, 0, mid), (down, 0, mid, n - mid)]
    pieces = [first[None], right[None], two_off[None], left[None], swap]
    piece_at = [(0, 0), (1, 0), (2, 0), (3, 0), (4, 0), (4, 1), (4, 2), (4, 3)]

    late = [(1, 4), (0, 4)]
    early = [key for key in chunks if key not in late]

    def listed(keys):
        refs, where = [], []
        for key in keys:
            parts = []
            for array, *rest in chunks[key]:
                at = [i for i, a in enumerate(refs) if a is array]
                if not at:
                    refs.append(array)
                parts.append((at[0] if at else len(refs) - 1, *rest))
            where.append(tuple(parts))
        return tuple(where), refs

    parts, refs = listed(early)
    acc, xp = pl.pallas_call(
        functools.partial(early_kernel, early, late, parts, len(pieces), piece_at, part),
        out_shape=(
            jax.ShapeDtypeStruct((2 * rows, 3 * LANES), F32),
            jax.ShapeDtypeStruct((2, rows, width), BF),
        ),
        in_specs=[SMEM] + [HBM] * (2 + len(pieces) + len(refs)),
        out_specs=(VMEM, ANY),
        scratch_shapes=[
            pltpu.VMEM((2, 2 * rows, width), BF),
            pltpu.VMEM((3 * LANES, width), BF),
            pltpu.SemaphoreType.DMA((copies_of(parts, part),)),
            pltpu.SemaphoreType.DMA((2 + 2 * NX,)),
            pltpu.SemaphoreType.DMA,
        ],
        compiler_params=params(58),
        cost_estimate=COST,
        name="early",
    )(sc, x_own, dy_own, *pieces, *refs)

    parts, refs = listed(late)
    full = jax.ShapeDtypeStruct((3 * part, LANES), BF)
    double = jax.ShapeDtypeStruct((6 * part, LANES), BF)
    late_terms = [(1, 3), (0, 3), (1, 5), (0, 5)]
    gt, dgu, *far = pl.pallas_call(
        functools.partial(late_kernel, late, parts, late_terms, part),
        out_shape=(
            jax.ShapeDtypeStruct((3 * part, 2 * rows), BF),
            jax.ShapeDtypeStruct((2, 2 * rows, LANES), BF),
            full, full, double, double,
        ),
        in_specs=[SMEM, VMEM] + [ANY] * 3 + [VMEM] * len(refs),
        out_specs=(VMEM,) * 6,
        scratch_shapes=[
            pltpu.VMEM((2 * rows, LANES), BF),
            pltpu.VMEM((2, 2 * rows, (len(late) + 4) * LANES), BF),
            pltpu.VMEM((3 * LANES, len(late) * LANES), BF),
            pltpu.SemaphoreType.DMA((len(late) + 4, 3)),
        ],
        compiler_params=params(22),
        cost_estimate=COST,
        name="late",
    )(sc, acc, x_own, dy_own, xp, *refs)
    far, got = far[:2], far[2:]

    term = dict(zip((3, 5), got))

    def ring(up, down):
        return pz(up, 1), pz(down, -1)

    up, down = ring(*far)

    keys = list(chunks)
    parts, refs = listed(keys)
    keep, send = pl.pallas_call(
        functools.partial(dx_kernel, keys, parts, part),
        out_shape=(jax.ShapeDtypeStruct((rows, width), BF),) * 2,
        in_specs=[SMEM, VMEM] + [HBM] * len(refs),
        out_specs=(VMEM, VMEM),
        scratch_shapes=[
            pltpu.VMEM((3 * LANES, width), BF),
            pltpu.SemaphoreType.DMA((copies_of(parts, part),)),
        ],
        compiler_params=params(58),
        cost_estimate=COST,
        name="dx",
    )(sc, dgu, *refs)
    sent = pc(send)

    up, down, _ = after_all(up, down, send)

    def joined(whole, halves, first):
        rows_of = [whole[i * mid : (i + 1) * mid].astype(F32) for i in range(4)]
        for i in range(2):
            rows_of[2 * i + first] += halves[i * mid : (i + 1) * mid]
        return jnp.concatenate([r.astype(BF) for r in rows_of])

    up, down = joined(term[3], up, 0), joined(term[5], down, 1)
    gt_later = after(gt, up, down)
    up, down = ring(up, down)
    distances = (2, 6, 1, 7, 0)
    keys = [(k, s) for s in distances for k in (1, 0)]
    got = pl.pallas_call(
        functools.partial(terms_kernel, keys, part),
        out_shape=(double,) * len(distances),
        in_specs=[SMEM, VMEM] + [ANY] * 3,
        out_specs=(VMEM,) * len(distances),
        scratch_shapes=[
            pltpu.VMEM((2, 2 * rows, len(keys) * LANES), BF),
            pltpu.SemaphoreType.DMA((len(keys), 3)),
        ],
        compiler_params=params(20),
        cost_estimate=COST,
        name="terms",
    )(sc, gt_later, x_own, dy_own, xp)
    term.update(zip(distances, got))

    up, down, sent = after_all(up, down, sent)
    up, down = (term[2].astype(F32) + up).astype(BF), (term[6].astype(F32) + down).astype(BF)
    up, down = ring(up, down)
    quarter = rows // NX

    def pair(i):
        rows_of = slice(i * quarter, (i + 1) * quarter)
        return keep[rows_of].astype(F32) + sent[rows_of].astype(F32)

    acc = px(pair(3).astype(BF), -1)
    acc = px((pair(2) + acc).astype(BF), -1)

    up, down, acc = after_all(up, down, acc)
    ends = []
    for k in range(2):
        rows_of = slice(k * n, (k + 1) * n)
        ends.append(
            ring(
                (term[1][rows_of].astype(F32) + up[rows_of]).astype(BF),
                (term[7][rows_of].astype(F32) + down[rows_of]).astype(BF),
            )
        )
    acc = px((pair(1) + acc).astype(BF), -1)
    p, o = ends
    acc, *p = after_all(pair(0) + acc, *p)
    part_b = [acc[i * group : (i + 1) * group].astype(BF) for i in range(1, 4)]
    got = [pyh(part_b[0]), pyl(part_b[1]), pboth(part_b[2])]

    sum_other = (term[0][:n].astype(F32) + p[0].astype(F32) + p[1].astype(F32)).astype(BF)
    o = after(tuple(o), sum_other)
    sum_other = pyl(sum_other)
    sum_own = (term[0][n:].astype(F32) + o[0].astype(F32) + o[1].astype(F32)).astype(BF)
    in_grad = (acc[:group] + got[0] + got[1] + got[2]).astype(BF).reshape(1, group, width)

    def whole(index):
        mine = sum_own[index * part : (index + 1) * part]
        theirs = sum_other[index * part : (index + 1) * part]
        return jnp.where(yl == 0, jnp.concatenate([mine, theirs]), jnp.concatenate([theirs, mine]))

    return in_grad, whole(0).T, whole(1).T, whole(2)


def solution(mesh):
    placed = (P("dp", None, None), P("dp", None, None), P("dp", "mp"), P("dp", "mp"), P("mp", "dp"))
    return jax.shard_map(
        local,
        mesh=mesh,
        in_specs=placed,
        out_specs=(P("dp", "mp", None), P("dp", "mp"), P("dp", "mp"), P("mp", "dp")),
        check_vma=False,
    )
```

```python
import functools

import jax
import jax.numpy as jnp
from jax import lax
from jax.experimental import pallas as pl
from jax.experimental.pallas import tpu as pltpu
from jax.sharding import PartitionSpec as P

BF = jnp.bfloat16
F32 = jnp.float32
NX, NZ = 4, 8
LANES = 256
ANY = pl.BlockSpec(memory_space=pl.ANY)
HBM = pl.BlockSpec(memory_space=pltpu.HBM)
VMEM = pl.BlockSpec(memory_space=pltpu.VMEM)
COST = pl.CostEstimate(flops=1, bytes_accessed=1, transcendentals=0)
SMEM = pl.BlockSpec(memory_space=pltpu.SMEM)


def mm(left, right):
    return lax.dot_general(left, right, (((1,), (0,)), ((), ())), preferred_element_type=F32)


def mm_t(left, right):
    return lax.dot_general(left, right, (((1,), (1,)), ((), ())), preferred_element_type=F32)


def pz(value, step):
    pairs = [(y * NZ + z, y * NZ + (z + step) % NZ) for y in range(2) for z in range(NZ)]
    return lax.ppermute(value, "dp", pairs)


def pyl(value):
    return lax.ppermute(value, "dp", [(i, (i + NZ) % (2 * NZ)) for i in range(2 * NZ)])


def px(value, step):
    pairs = [
        (y * 8 + x * 2 + c, y * 8 + (x + (-step if c else step)) % NX * 2 + c)
        for y in range(2) for x in range(NX) for c in range(2)
    ]
    return lax.ppermute(value, "mp", pairs)


def pxs(value, step):
    pairs = [
        (y * 8 + x * 2 + c, y * 8 + (x + step) % NX * 2 + c)
        for y in range(2) for x in range(NX) for c in range(2)
    ]
    return lax.ppermute(value, "mp", pairs)


def pc(value):
    return lax.ppermute(value, "mp", [(i, i ^ 1) for i in range(16)])


def pyh(value):
    return lax.ppermute(value, "mp", [(i, i ^ 8) for i in range(16)])


def pboth(value):
    n = 2 * NZ
    pairs = [(m * n + d, (m ^ 8) * n + (d + NZ) % n) for m in range(16) for d in range(n)]
    return lax.ppermute(value, ("mp", "dp"), pairs)


def after(value, *others):
    return lax.optimization_barrier((value, *others))[0]


def after_all(*values):
    return lax.optimization_barrier(values)


def col_block(sc, k, s):
    yl = 1 - sc[1] if k else sc[1]
    return yl * NZ + lax.rem(sc[0] + s, NZ)


def offset(sc, k, s):
    return pl.multiple_of(col_block(sc, k, s) * LANES, LANES)


def spread(row, count, part):
    out, end = [], row + count
    while row < end:
        m = row // part
        n = min(end, (m + 1) * part) - row
        out.append((row, n, m * LANES + row - m * part))
        row += n
    return out


def load_chunks(where, places, part, refs, buf, sems):
    waits, sem = [], 0
    for parts, place in zip(where, places):
        mine = []
        for at, row, start, count in parts:
            for first, n, to in spread(start, count, part):
                copy = pltpu.make_async_copy(
                    refs[at].at[pl.ds(row + first - start, n)],
                    buf.at[pl.ds(to, n), pl.ds(place, LANES)],
                    sems.at[sem],
                )
                copy.start()
                mine.append(copy)
                sem += 1
        waits.append(mine)
    return waits


def copies_of(where, part):
    return sum(len(spread(start, count, part)) for parts in where for _, _, start, count in parts)


def clear_pad(buf, part):
    for m in range(3):
        buf[m * LANES + part : (m + 1) * LANES] = jnp.zeros((LANES - part, buf.shape[1]), BF)


def early_kernel(keys, missing, parts, n_pieces, piece_at, part, sc, x, dy, *refs):
    pieces, chunks = refs[:n_pieces], refs[n_pieces:-7]
    acc, xp, xs, buf, w_sems, x_sems, out_sem = refs[-7:]
    rows = x.shape[0]
    loads = [
        pltpu.make_async_copy(x, xs.at[0, pl.ds(0, rows)], x_sems.at[0]),
        pltpu.make_async_copy(dy, xs.at[1, pl.ds(0, rows)], x_sems.at[1]),
    ]
    row = rows
    pieces = [pieces[i].at[j] for i, j in piece_at]
    for i, piece in enumerate(pieces):
        n = piece.shape[1]
        loads.append(pltpu.make_async_copy(piece, xs.at[:, pl.ds(row, n)], x_sems.at[2 + i]))
        row += n
    for copy in loads:
        copy.start()
    waits = load_chunks(parts, [offset(sc, *key) for key in keys], part, chunks, buf, w_sems)
    clear_pad(buf, part)
    for key in missing:
        buf[:, pl.ds(offset(sc, *key), LANES)] = jnp.zeros((buf.shape[0], LANES), BF)
    for copy in loads:
        copy.wait()
    store = pltpu.make_async_copy(xs.at[:, pl.ds(rows, rows)], xp, out_sem)
    store.start()
    for mine in waits:
        for copy in mine:
            copy.wait()
    acc[:, : 2 * LANES] = mm_t(xs[0], buf[: 2 * LANES])
    acc[:, 2 * LANES :] = mm_t(xs[1], buf[2 * LANES :])
    store.wait()


def put_terms(outs, part, top, low):
    two, n = 2 * part, 3 * part
    top, low = top.astype(BF), low.astype(BF)
    for j, out in enumerate(outs):
        for k in range(2):
            cols = slice((2 * j + k) * LANES, (2 * j + k + 1) * LANES)
            out[k * n : k * n + two] = top[:, cols]
            out[k * n + two : (k + 1) * n] = low[:, cols]


def late_kernel(keys, parts, term_keys, part, sc, acc, x, dy, xp, *refs):
    n_out = 8 + len(term_keys) // 2
    chunks = refs[:-n_out]
    gt, dgu, *outs = refs[-n_out:-4]
    far, outs = outs[:2], outs[2:]
    rowbuf, xb, buf, x_sems = refs[-4:]
    rows = x.shape[0]
    loads = []
    for i, (k, s) in enumerate(keys + term_keys):
        cols, to = pl.ds(offset(sc, k, s), LANES), pl.ds(i * LANES, LANES)
        loads += [
            pltpu.make_async_copy(x.at[:, cols], xb.at[0, pl.ds(0, rows), to], x_sems.at[i, 0]),
            pltpu.make_async_copy(dy.at[:, cols], xb.at[1, pl.ds(0, rows), to], x_sems.at[i, 1]),
            pltpu.make_async_copy(xp.at[:, :, cols], xb.at[:, pl.ds(rows, rows), to], x_sems.at[i, 2]),
        ]
    for copy in loads:
        copy.start()
    clear_pad(buf, part)
    for i, pieces in enumerate(parts):
        for at, row, start, count in pieces:
            for first, n, to in spread(start, count, part):
                row_at = row + first - start
                buf[to : to + n, i * LANES : (i + 1) * LANES] = chunks[at][row_at : row_at + n]
    for copy in loads[: 3 * len(keys)]:
        copy.wait()
    used = len(keys) * LANES
    both = acc[:, : 2 * LANES] + mm_t(xb[0, :, :used], buf[: 2 * LANES])
    dhid = acc[:, 2 * LANES :] + mm_t(xb[1, :, :used], buf[2 * LANES :])
    gate, up_val = both[:, :LANES], both[:, LANES:]
    sig = 1.0 / (1.0 + jnp.exp(-gate))
    silu = gate * sig
    hidden = silu * up_val
    dup = dhid * silu
    dgate = dhid * up_val * sig * (1.0 + gate * (1.0 - sig))
    for m, value in enumerate((dgate, dup, hidden)):
        gt[m * part : (m + 1) * part] = value.T[:part].astype(BF)
    mid = 3 * part // 2
    two = 2 * part
    up, down = far
    for j in range(2):
        cols = slice(j * LANES, (j + 1) * LANES)
        top, low = mm(gt[:two], xb[0, :, cols]), mm(gt[two:], xb[1, :, cols])
        at = j * mid
        up[at : at + mid] = top[:mid].astype(BF)
        down[at : at + two - mid] = top[mid:].astype(BF)
        down[at + two - mid : at + mid] = low.astype(BF)
    for copy in loads[3 * len(keys) :]:
        copy.wait()
    put_terms(outs, part, mm(gt[:two], xb[0, :, used:]), mm(gt[two:], xb[1, :, used:]))
    group = rows // 16
    for m, value in enumerate((dgate, dup)):
        rowbuf[...] = value.astype(BF)
        for g in range(16):
            to = g // 2 * 4 * group + g % 2 * group
            at = pl.multiple_of(sc[2 + g] * group, group)
            dgu[m, to : to + group] = rowbuf[pl.ds(at, group)]
        for g in range(8):
            to = g * 4 * group + 2 * group
            at = pl.multiple_of(rows + sc[18 + g] * 2 * group, 2 * group)
            dgu[m, to : to + 2 * group] = rowbuf[pl.ds(at, 2 * group)]


def dx_kernel(keys, parts, part, sc, dgu, *refs):
    chunks, (keep, send, buf, w_sems) = refs[:-4], refs[-4:]
    rows = keep.shape[0]
    waits = load_chunks(parts, [offset(sc, *key) for key in keys], part, chunks, buf, w_sems)
    clear_pad(buf, part)
    for mine in waits:
        for copy in mine:
            copy.wait()
    step = 4 * LANES
    for at in range(0, keep.shape[1], step):
        cols = slice(at, at + step)
        dx = mm(dgu[0], buf[:LANES, cols]) + mm(dgu[1], buf[LANES : 2 * LANES, cols])
        keep[:, cols] = dx[:rows].astype(BF)
        send[:, cols] = dx[rows:].astype(BF)


def terms_kernel(keys, part, sc, gt, x, dy, xp, *refs):
    outs, (xb, x_sems) = refs[:-2], refs[-2:]
    rows = x.shape[0]
    loads = []
    for i, (k, s) in enumerate(keys):
        cols, to = pl.ds(offset(sc, k, s), LANES), pl.ds(i * LANES, LANES)
        mine = [
            pltpu.make_async_copy(x.at[:, cols], xb.at[0, pl.ds(0, rows), to], x_sems.at[i, 0]),
            pltpu.make_async_copy(dy.at[:, cols], xb.at[1, pl.ds(0, rows), to], x_sems.at[i, 1]),
            pltpu.make_async_copy(xp.at[:, :, cols], xb.at[:, pl.ds(rows, rows), to], x_sems.at[i, 2]),
        ]
        for copy in mine:
            copy.start()
        loads.append(mine)
    two = 2 * part
    for i in range(0, len(keys), 2):
        for copy in loads[i] + loads[i + 1]:
            copy.wait()
        cols = slice(i * LANES, (i + 2) * LANES)
        put_terms(outs[i // 2 : i // 2 + 1], part, mm(gt[:two], xb[0, :, cols]), mm(gt[two:], xb[1, :, cols]))


def halves(array, index):
    rows = array.shape[0] // 2
    return (
        lax.dynamic_slice_in_dim(array, index * rows, rows, 0),
        lax.dynamic_slice_in_dim(array, (1 - index) * rows, rows, 0),
    )


def params(mib):
    return pltpu.CompilerParams(vmem_limit_bytes=mib * 1024 * 1024)


def local(inputs, out_grad, w_gate, w_up, w_down):
    rows, width = inputs.shape[1:]
    part = w_down.shape[0] // 2
    dp, mp = lax.axis_index("dp"), lax.axis_index("mp")
    yl, z = dp // NZ, dp % NZ
    yh, x, c = mp // 8, mp // 2 % NX, mp % 2
    group = rows // 16
    x_own, dy_own = inputs[0], out_grad[0]

    slot = lax.iota(jnp.int32, 26)
    at = slot - 2
    dc, dx, dh = at // 8, at // 2 % NX, at % 2
    ordered = (yh ^ dh) * 8 + (x - (1 - 2 * (c ^ dc)) * dx + NX) % NX * 2 + (c ^ dc)
    at = slot - 18
    dc, dx = at // NX % 2, at % NX
    stands = dc * NX + (NX - (1 - 2 * (c ^ dc)) * dx) % NX
    sc = jnp.where(slot < 2, jnp.where(slot == 0, z, yl), jnp.where(slot < 18, ordered, stands)).astype(jnp.int32)

    wts = [halves(w, yl) for w in (w_gate.T, w_up.T, w_down)]
    own = jnp.concatenate([w[0] for w in wts])
    other = jnp.concatenate([w[1] for w in wts])
    mid = own.shape[0] // 2

    def rows_at(array, index):
        return lax.dynamic_slice_in_dim(array, index * group, group, 0)

    def piece(array):
        return jnp.concatenate([rows_at(array, mp), rows_at(array, mp ^ 8)])

    n = own.shape[0]
    up, down = pz(own, 1), pz(own, -1)
    other = pyl(other)
    chunks = {
        (0, 0): [(own, 0, 0, n)],
        (0, 7): [(up, 0, 0, n)],
        (0, 1): [(down, 0, 0, n)],
        (1, 0): [(other, 0, 0, n)],
    }
    first = jnp.stack([piece(after(x_own, own)), piece(after(dy_own, own))])
    first = pyl(after(first, up, down))
    up, down = jnp.concatenate([other, up]), jnp.concatenate([down, other])
    for step in (1, 2):
        up, down = pz(up, 1), pz(down, -1)
        chunks[1, NZ - step], chunks[0, NZ - step - 1] = [(up, 0, 0, n)], [(up, n, 0, n)]
        chunks[0, step + 1], chunks[1, step] = [(down, 0, 0, n)], [(down, n, 0, n)]
        up, down = after_all(up, down)
        if step == 1:
            left, right = pxs(first, 1), pxs(first, -1)
            left_s, right_s, first_s, _, _ = after_all(left, right, first, up, down)
            far_x, far_dy = pxs(left_s[0], 1), pxs(right_s[1], -1)
            swap = pc(jnp.stack([first_s, right_s, left_s]))
    far_x, far_dy, _, _ = after_all(far_x, far_dy, up, down)
    two_off = jnp.stack([far_x, far_dy])
    swap_two = pc(two_off)
    up, down = pz(up[: n + mid], 1), pz(down[mid:], -1)
    chunks[1, 5], chunks[1, 3] = [(up, 0, 0, n)], [(down, n - mid, 0, n)]
    chunks[0, 4] = [(up, n, 0, mid), (down, 0, mid, n - mid)]
    pieces = [first[None], right[None], two_off[None], left[None], swap, swap_two[None]]
    piece_at = [(0, 0), (1, 0), (2, 0), (3, 0), (4, 0), (4, 1), (5, 0), (4, 2)]

    late = [(1, 4), (0, 4), (1, 3), (1, 5)]
    early = [key for key in chunks if key not in late]

    def listed(keys):
        refs, where = [], []
        for key in keys:
            parts = []
            for array, *rest in chunks[key]:
                at = [i for i, a in enumerate(refs) if a is array]
                if not at:
                    refs.append(array)
                parts.append((at[0] if at else len(refs) - 1, *rest))
            where.append(tuple(parts))
        return tuple(where), refs

    parts, refs = listed(early)
    acc, xp = pl.pallas_call(
        functools.partial(early_kernel, early, late, parts, len(pieces), piece_at, part),
        out_shape=(
            jax.ShapeDtypeStruct((2 * rows, 3 * LANES), F32),
            jax.ShapeDtypeStruct((2, rows, width), BF),
        ),
        in_specs=[SMEM] + [HBM] * (2 + len(pieces) + len(refs)),
        out_specs=(VMEM, ANY),
        scratch_shapes=[
            pltpu.VMEM((2, 2 * rows, width), BF),
            pltpu.VMEM((3 * LANES, width), BF),
            pltpu.SemaphoreType.DMA((copies_of(parts, part),)),
            pltpu.SemaphoreType.DMA((2 + 2 * NX,)),
            pltpu.SemaphoreType.DMA,
        ],
        compiler_params=params(22),
        cost_estimate=COST,
        name="early",
    )(sc, x_own, dy_own, *pieces, *refs)

    up, down, acc, xp = after_all(up, down, acc, xp)
    up, down = pz(up[:mid], 1), pz(down[n:], -1)
    chunks[1, 4] = [(up, 0, 0, mid), (down, 0, mid, n - mid)]

    parts, refs = listed(late)
    full = jax.ShapeDtypeStruct((3 * part, LANES), BF)
    double = jax.ShapeDtypeStruct((6 * part, LANES), BF)
    late_terms = [(1, 3), (0, 3), (1, 5), (0, 5)]
    gt, dgu, *far = pl.pallas_call(
        functools.partial(late_kernel, late, parts, late_terms, part),
        out_shape=(
            jax.ShapeDtypeStruct((3 * part, 2 * rows), BF),
            jax.ShapeDtypeStruct((2, 2 * rows, LANES), BF),
            full, full, double, double,
        ),
        in_specs=[SMEM, VMEM] + [ANY] * 3 + [VMEM] * len(refs),
        out_specs=(VMEM,) * 6,
        scratch_shapes=[
            pltpu.VMEM((2 * rows, LANES), BF),
            pltpu.VMEM((2, 2 * rows, (len(late) + 4) * LANES), BF),
            pltpu.VMEM((3 * LANES, len(late) * LANES), BF),
            pltpu.SemaphoreType.DMA((len(late) + 4, 3)),
        ],
        compiler_params=params(22),
        cost_estimate=COST,
        name="late",
    )(sc, acc, x_own, dy_own, xp, *refs)
    far, got = far[:2], far[2:]

    term = dict(zip((3, 5), got))

    def ring(up, down):
        return pz(up, 1), pz(down, -1)

    up, down = ring(*far)

    keys = list(chunks)
    parts, refs = listed(keys)
    keep, send = pl.pallas_call(
        functools.partial(dx_kernel, keys, parts, part),
        out_shape=(jax.ShapeDtypeStruct((rows, width), BF),) * 2,
        in_specs=[SMEM, VMEM] + [HBM] * len(refs),
        out_specs=(VMEM, VMEM),
        scratch_shapes=[
            pltpu.VMEM((3 * LANES, width), BF),
            pltpu.SemaphoreType.DMA((copies_of(parts, part),)),
        ],
        compiler_params=params(20),
        cost_estimate=COST,
        name="dx",
    )(sc, dgu, *refs)

    up, down, send = after_all(up, down, send)
    sent = pc(send)

    def joined(whole, halves, first):
        rows_of = [whole[i * mid : (i + 1) * mid].astype(F32) for i in range(4)]
        for i in range(2):
            rows_of[2 * i + first] += halves[i * mid : (i + 1) * mid]
        return jnp.concatenate([r.astype(BF) for r in rows_of])

    up, down = joined(term[3], up, 0), joined(term[5], down, 1)
    gt_later = after(gt, up, down)
    up, down = ring(up, down)
    distances = (2, 6, 1, 7, 0)
    keys = [(k, s) for s in distances for k in (1, 0)]
    got = pl.pallas_call(
        functools.partial(terms_kernel, keys, part),
        out_shape=(double,) * len(distances),
        in_specs=[SMEM, VMEM] + [ANY] * 3,
        out_specs=(VMEM,) * len(distances),
        scratch_shapes=[
            pltpu.VMEM((2, 2 * rows, len(keys) * LANES), BF),
            pltpu.SemaphoreType.DMA((len(keys), 3)),
        ],
        compiler_params=params(20),
        cost_estimate=COST,
        name="terms",
    )(sc, gt_later, x_own, dy_own, xp)
    term.update(zip(distances, got))

    quarter = rows // NX

    def pair(i):
        rows_of = slice(i * quarter, (i + 1) * quarter)
        return keep[rows_of].astype(F32) + sent[rows_of].astype(F32)

    acc = px(pair(3).astype(BF), -1)

    up, down, acc = after_all(up, down, acc)
    up, down = (term[2].astype(F32) + up).astype(BF), (term[6].astype(F32) + down).astype(BF)
    up, down = ring(up, down)
    acc = px((pair(2) + acc).astype(BF), -1)

    acc = (pair(1) + acc).astype(BF)
    up, down, acc = after_all(up, down, acc)
    acc = px(acc, -1)
    ends = []
    for k in range(2):
        rows_of = slice(k * n, (k + 1) * n)
        ends.append(
            (
                (term[1][rows_of].astype(F32) + up[rows_of]).astype(BF),
                (term[7][rows_of].astype(F32) + down[rows_of]).astype(BF),
            )
        )
        if k == 0:
            up, down, _, _ = after_all(up, down, *ends[0])
    acc = pair(0) + after(acc, *ends[0])
    p, o = ring(*ends[0]), ring(*ends[1])
    part_b = [acc[i * group : (i + 1) * group].astype(BF) for i in range(1, 4)]
    got = [pyh(part_b[0]), pyl(part_b[1]), pboth(part_b[2])]

    sum_other = (term[0][:n].astype(F32) + p[0].astype(F32) + p[1].astype(F32)).astype(BF)
    o = after(tuple(o), sum_other)
    sum_other = pyl(sum_other)
    o = after(tuple(o), *part_b)
    sum_own = (term[0][n:].astype(F32) + o[0].astype(F32) + o[1].astype(F32)).astype(BF)
    in_grad = (acc[:group] + got[0] + got[1] + got[2]).astype(BF).reshape(1, group, width)

    def whole(index):
        mine = sum_own[index * part : (index + 1) * part]
        theirs = sum_other[index * part : (index + 1) * part]
        return jnp.where(yl == 0, jnp.concatenate([mine, theirs]), jnp.concatenate([theirs, mine]))

    return in_grad, whole(0).T, whole(1).T, whole(2)


def solution(mesh):
    placed = (P("dp", None, None), P("dp", None, None), P("dp", "mp"), P("dp", "mp"), P("mp", "dp"))
    return jax.shard_map(
        local,
        mesh=mesh,
        in_specs=placed,
        out_specs=(P("dp", "mp", None), P("dp", "mp"), P("dp", "mp"), P("mp", "dp")),
        check_vma=False,
    )
```

```python
import functools

import jax
import jax.numpy as jnp
from jax import lax
from jax.experimental import pallas as pl
from jax.experimental.pallas import tpu as pltpu
from jax.sharding import PartitionSpec as P

BF = jnp.bfloat16
F32 = jnp.float32
NX, NZ = 4, 8
LANES = 256
ANY = pl.BlockSpec(memory_space=pl.ANY)
HBM = pl.BlockSpec(memory_space=pltpu.HBM)
VMEM = pl.BlockSpec(memory_space=pltpu.VMEM)
COST = pl.CostEstimate(flops=1, bytes_accessed=1, transcendentals=0)
SMEM = pl.BlockSpec(memory_space=pltpu.SMEM)


def mm(left, right):
    return lax.dot_general(left, right, (((1,), (0,)), ((), ())), preferred_element_type=F32)


def mm_t(left, right):
    return lax.dot_general(left, right, (((1,), (1,)), ((), ())), preferred_element_type=F32)


def pz(value, step):
    pairs = [(y * NZ + z, y * NZ + (z + step) % NZ) for y in range(2) for z in range(NZ)]
    return lax.ppermute(value, "dp", pairs)


def pyl(value):
    return lax.ppermute(value, "dp", [(i, (i + NZ) % (2 * NZ)) for i in range(2 * NZ)])


def px(value, step):
    pairs = [
        (y * 8 + x * 2 + c, y * 8 + (x + (-step if c else step)) % NX * 2 + c)
        for y in range(2) for x in range(NX) for c in range(2)
    ]
    return lax.ppermute(value, "mp", pairs)


def pxs(value, step):
    pairs = [
        (y * 8 + x * 2 + c, y * 8 + (x + step) % NX * 2 + c)
        for y in range(2) for x in range(NX) for c in range(2)
    ]
    return lax.ppermute(value, "mp", pairs)


def pc(value):
    return lax.ppermute(value, "mp", [(i, i ^ 1) for i in range(16)])


def pyh(value):
    return lax.ppermute(value, "mp", [(i, i ^ 8) for i in range(16)])


def pboth(value):
    n = 2 * NZ
    pairs = [(m * n + d, (m ^ 8) * n + (d + NZ) % n) for m in range(16) for d in range(n)]
    return lax.ppermute(value, ("mp", "dp"), pairs)


def after(value, *others):
    return lax.optimization_barrier((value, *others))[0]


def after_all(*values):
    return lax.optimization_barrier(values)


def col_block(sc, k, s):
    yl = 1 - sc[1] if k else sc[1]
    return yl * NZ + lax.rem(sc[0] + s, NZ)


def offset(sc, k, s):
    return pl.multiple_of(col_block(sc, k, s) * LANES, LANES)


def spread(row, count, part):
    out, end = [], row + count
    while row < end:
        m = row // part
        n = min(end, (m + 1) * part) - row
        out.append((row, n, m * LANES + row - m * part))
        row += n
    return out


def load_chunks(where, places, part, refs, buf, sems):
    waits, sem = [], 0
    for parts, place in zip(where, places):
        mine = []
        for at, row, start, count in parts:
            for first, n, to in spread(start, count, part):
                copy = pltpu.make_async_copy(
                    refs[at].at[pl.ds(row + first - start, n)],
                    buf.at[pl.ds(to, n), pl.ds(place, LANES)],
                    sems.at[sem],
                )
                copy.start()
                mine.append(copy)
                sem += 1
        waits.append(mine)
    return waits


def copies_of(where, part):
    return sum(len(spread(start, count, part)) for parts in where for _, _, start, count in parts)


def clear_pad(buf, part):
    for m in range(3):
        buf[m * LANES + part : (m + 1) * LANES] = jnp.zeros((LANES - part, buf.shape[1]), BF)


def early_kernel(keys, missing, parts, n_pieces, piece_at, part, sc, x, dy, *refs):
    pieces, chunks = refs[:n_pieces], refs[n_pieces:-7]
    acc, xp, xs, buf, w_sems, x_sems, out_sem = refs[-7:]
    rows = x.shape[0]
    loads = [
        pltpu.make_async_copy(x, xs.at[0, pl.ds(0, rows)], x_sems.at[0]),
        pltpu.make_async_copy(dy, xs.at[1, pl.ds(0, rows)], x_sems.at[1]),
    ]
    row = rows
    pieces = [pieces[i].at[j] for i, j in piece_at]
    for i, piece in enumerate(pieces):
        n = piece.shape[1]
        loads.append(pltpu.make_async_copy(piece, xs.at[:, pl.ds(row, n)], x_sems.at[2 + i]))
        row += n
    for copy in loads:
        copy.start()
    waits = load_chunks(parts, [offset(sc, *key) for key in keys], part, chunks, buf, w_sems)
    clear_pad(buf, part)
    for key in missing:
        buf[:, pl.ds(offset(sc, *key), LANES)] = jnp.zeros((buf.shape[0], LANES), BF)
    for copy in loads:
        copy.wait()
    store = pltpu.make_async_copy(xs.at[:, pl.ds(rows, rows)], xp, out_sem)
    store.start()
    for mine in waits:
        for copy in mine:
            copy.wait()
    acc[:, : 2 * LANES] = mm_t(xs[0], buf[: 2 * LANES])
    acc[:, 2 * LANES :] = mm_t(xs[1], buf[2 * LANES :])
    store.wait()


def put_terms(outs, part, top, low):
    two, n = 2 * part, 3 * part
    top, low = top.astype(BF), low.astype(BF)
    for j, out in enumerate(outs):
        for k in range(2):
            cols = slice((2 * j + k) * LANES, (2 * j + k + 1) * LANES)
            out[k * n : k * n + two] = top[:, cols]
            out[k * n + two : (k + 1) * n] = low[:, cols]


def late_kernel(keys, parts, term_keys, part, sc, acc, x, dy, xp, *refs):
    n_out = 8 + len(term_keys) // 2
    chunks = refs[:-n_out]
    gt, dgu, *outs = refs[-n_out:-4]
    far, outs = outs[:2], outs[2:]
    rowbuf, xb, buf, x_sems = refs[-4:]
    rows = x.shape[0]
    loads = []
    for i, (k, s) in enumerate(keys + term_keys):
        cols, to = pl.ds(offset(sc, k, s), LANES), pl.ds(i * LANES, LANES)
        loads += [
            pltpu.make_async_copy(x.at[:, cols], xb.at[0, pl.ds(0, rows), to], x_sems.at[i, 0]),
            pltpu.make_async_copy(dy.at[:, cols], xb.at[1, pl.ds(0, rows), to], x_sems.at[i, 1]),
            pltpu.make_async_copy(xp.at[:, :, cols], xb.at[:, pl.ds(rows, rows), to], x_sems.at[i, 2]),
        ]
    for copy in loads:
        copy.start()
    clear_pad(buf, part)
    for i, pieces in enumerate(parts):
        for at, row, start, count in pieces:
            for first, n, to in spread(start, count, part):
                row_at = row + first - start
                buf[to : to + n, i * LANES : (i + 1) * LANES] = chunks[at][row_at : row_at + n]
    for copy in loads[: 3 * len(keys)]:
        copy.wait()
    used = len(keys) * LANES
    both = acc[:, : 2 * LANES] + mm_t(xb[0, :, :used], buf[: 2 * LANES])
    dhid = acc[:, 2 * LANES :] + mm_t(xb[1, :, :used], buf[2 * LANES :])
    gate, up_val = both[:, :LANES], both[:, LANES:]
    sig = 1.0 / (1.0 + jnp.exp(-gate))
    silu = gate * sig
    hidden = silu * up_val
    dup = dhid * silu
    dgate = dhid * up_val * sig * (1.0 + gate * (1.0 - sig))
    for m, value in enumerate((dgate, dup, hidden)):
        gt[m * part : (m + 1) * part] = value.T[:part].astype(BF)
    mid = 3 * part // 2
    two = 2 * part
    up, down = far
    for j in range(2):
        cols = slice(j * LANES, (j + 1) * LANES)
        top, low = mm(gt[:two], xb[0, :, cols]), mm(gt[two:], xb[1, :, cols])
        at = j * mid
        up[at : at + mid] = top[:mid].astype(BF)
        down[at : at + two - mid] = top[mid:].astype(BF)
        down[at + two - mid : at + mid] = low.astype(BF)
    for copy in loads[3 * len(keys) :]:
        copy.wait()
    put_terms(outs, part, mm(gt[:two], xb[0, :, used:]), mm(gt[two:], xb[1, :, used:]))
    group = rows // 16
    for m, value in enumerate((dgate, dup)):
        rowbuf[...] = value.astype(BF)
        for g in range(16):
            to = g // 2 * 4 * group + g % 2 * group
            at = pl.multiple_of(sc[2 + g] * group, group)
            dgu[m, to : to + group] = rowbuf[pl.ds(at, group)]
        for g in range(8):
            to = g * 4 * group + 2 * group
            at = pl.multiple_of(rows + sc[18 + g] * 2 * group, 2 * group)
            dgu[m, to : to + 2 * group] = rowbuf[pl.ds(at, 2 * group)]


def dx_kernel(keys, parts, part, sc, dgu, *refs):
    chunks, (keep, send, buf, w_sems) = refs[:-4], refs[-4:]
    rows = keep.shape[0]
    waits = load_chunks(parts, [offset(sc, *key) for key in keys], part, chunks, buf, w_sems)
    clear_pad(buf, part)
    for mine in waits:
        for copy in mine:
            copy.wait()
    step = 4 * LANES
    for at in range(0, keep.shape[1], step):
        cols = slice(at, at + step)
        dx = mm(dgu[0], buf[:LANES, cols]) + mm(dgu[1], buf[LANES : 2 * LANES, cols])
        keep[:, cols] = dx[:rows].astype(BF)
        send[:, cols] = dx[rows:].astype(BF)


def terms_kernel(keys, part, sc, gt, x, dy, xp, *refs):
    outs, (xb, x_sems) = refs[:-2], refs[-2:]
    rows = x.shape[0]
    loads = []
    for i, (k, s) in enumerate(keys):
        cols, to = pl.ds(offset(sc, k, s), LANES), pl.ds(i * LANES, LANES)
        mine = [
            pltpu.make_async_copy(x.at[:, cols], xb.at[0, pl.ds(0, rows), to], x_sems.at[i, 0]),
            pltpu.make_async_copy(dy.at[:, cols], xb.at[1, pl.ds(0, rows), to], x_sems.at[i, 1]),
            pltpu.make_async_copy(xp.at[:, :, cols], xb.at[:, pl.ds(rows, rows), to], x_sems.at[i, 2]),
        ]
        for copy in mine:
            copy.start()
        loads.append(mine)
    two = 2 * part
    for i in range(0, len(keys), 2):
        for copy in loads[i] + loads[i + 1]:
            copy.wait()
        cols = slice(i * LANES, (i + 2) * LANES)
        put_terms(outs[i // 2 : i // 2 + 1], part, mm(gt[:two], xb[0, :, cols]), mm(gt[two:], xb[1, :, cols]))


def params(mib):
    return pltpu.CompilerParams(vmem_limit_bytes=mib * 1024 * 1024)


def local(inputs, out_grad, w_gate, w_up, w_down):
    rows, width = inputs.shape[1:]
    part = w_down.shape[0] // 2
    dp, mp = lax.axis_index("dp"), lax.axis_index("mp")
    yl, z = dp // NZ, dp % NZ
    yh, x, c = mp // 8, mp // 2 % NX, mp % 2
    group = rows // 16
    x_own, dy_own = inputs[0], out_grad[0]

    slot = lax.iota(jnp.int32, 26)
    at = slot - 2
    dc, dx, dh = at // 8, at // 2 % NX, at % 2
    ordered = (yh ^ dh) * 8 + (x - (1 - 2 * (c ^ dc)) * dx + NX) % NX * 2 + (c ^ dc)
    at = slot - 18
    dc, dx = at // NX % 2, at % NX
    stands = dc * NX + (NX - (1 - 2 * (c ^ dc)) * dx) % NX
    sc = jnp.where(slot < 2, jnp.where(slot == 0, z, yl), jnp.where(slot < 18, ordered, stands)).astype(jnp.int32)

    u32 = jnp.uint32
    low = jnp.broadcast_to(yl == 0, (8, 128))
    starts = [(yl * part).astype(u32), ((1 - yl) * part).astype(u32), (mp * group).astype(u32), ((mp ^ 8) * group).astype(u32)]
    w_gate, w_up, w_down, x_own, dy_own, sc, low, *starts = after_all(
        w_gate, w_up, w_down, x_own, dy_own, sc, low, *starts
    )

    def rows_from(array, start, count):
        return lax.dynamic_slice(array, (start, u32(0)), (count, array.shape[1]))

    own, other = (
        jnp.concatenate([rows_from(w, starts[i], part) for w in (w_gate.T, w_up.T, w_down)]) for i in range(2)
    )
    mid = own.shape[0] // 2

    def piece(array):
        return jnp.concatenate([rows_from(array, starts[i], group) for i in (2, 3)])

    n = own.shape[0]
    up, down = pz(own, 1), pz(own, -1)
    other = pyl(other)
    chunks = {
        (0, 0): [(own, 0, 0, n)],
        (0, 7): [(up, 0, 0, n)],
        (0, 1): [(down, 0, 0, n)],
        (1, 0): [(other, 0, 0, n)],
    }
    first = jnp.stack([piece(after(x_own, own)), piece(after(dy_own, own))])
    first = pyl(after(first, up, down))
    up, down = jnp.concatenate([other, up]), jnp.concatenate([down, other])
    for step in (1, 2):
        up, down = pz(up, 1), pz(down, -1)
        chunks[1, NZ - step], chunks[0, NZ - step - 1] = [(up, 0, 0, n)], [(up, n, 0, n)]
        chunks[0, step + 1], chunks[1, step] = [(down, 0, 0, n)], [(down, n, 0, n)]
        up, down = after_all(up, down)
        if step == 1:
            left, right = pxs(first, 1), pxs(first, -1)
            left_s, right_s, first_s, _, _ = after_all(left, right, first, up, down)
            far_x, far_dy = pxs(left_s[0], 1), pxs(right_s[1], -1)
            swap = pc(jnp.stack([first_s, right_s, left_s]))
    far_x, far_dy, _, _ = after_all(far_x, far_dy, up, down)
    two_off = jnp.stack([far_x, far_dy])
    swap_two = pc(two_off)
    up, down = pz(up[: n + mid], 1), pz(down[mid:], -1)
    chunks[1, 5], chunks[1, 3] = [(up, 0, 0, n)], [(down, n - mid, 0, n)]
    chunks[0, 4] = [(up, n, 0, mid), (down, 0, mid, n - mid)]
    pieces = [first[None], right[None], two_off[None], left[None], swap, swap_two[None]]
    piece_at = [(0, 0), (1, 0), (2, 0), (3, 0), (4, 0), (4, 1), (5, 0), (4, 2)]

    late = [(1, 4), (0, 4), (1, 3), (1, 5)]
    early = [key for key in chunks if key not in late]

    def listed(keys):
        refs, where = [], []
        for key in keys:
            parts = []
            for array, *rest in chunks[key]:
                at = [i for i, a in enumerate(refs) if a is array]
                if not at:
                    refs.append(array)
                parts.append((at[0] if at else len(refs) - 1, *rest))
            where.append(tuple(parts))
        return tuple(where), refs

    parts, refs = listed(early)
    acc, xp = pl.pallas_call(
        functools.partial(early_kernel, early, late, parts, len(pieces), piece_at, part),
        out_shape=(
            jax.ShapeDtypeStruct((2 * rows, 3 * LANES), F32),
            jax.ShapeDtypeStruct((2, rows, width), BF),
        ),
        in_specs=[SMEM] + [HBM] * (2 + len(pieces) + len(refs)),
        out_specs=(VMEM, ANY),
        scratch_shapes=[
            pltpu.VMEM((2, 2 * rows, width), BF),
            pltpu.VMEM((3 * LANES, width), BF),
            pltpu.SemaphoreType.DMA((copies_of(parts, part),)),
            pltpu.SemaphoreType.DMA((2 + 2 * NX,)),
            pltpu.SemaphoreType.DMA,
        ],
        compiler_params=params(22),
        cost_estimate=COST,
        name="early",
    )(sc, x_own, dy_own, *pieces, *refs)

    up, down, acc, xp = after_all(up, down, acc, xp)
    up, down = pz(up[:mid], 1), pz(down[n:], -1)
    chunks[1, 4] = [(up, 0, 0, mid), (down, 0, mid, n - mid)]

    parts, refs = listed(late)
    full = jax.ShapeDtypeStruct((3 * part, LANES), BF)
    double = jax.ShapeDtypeStruct((6 * part, LANES), BF)
    late_terms = [(1, 3), (0, 3), (1, 5), (0, 5)]
    gt, dgu, *far = pl.pallas_call(
        functools.partial(late_kernel, late, parts, late_terms, part),
        out_shape=(
            jax.ShapeDtypeStruct((3 * part, 2 * rows), BF),
            jax.ShapeDtypeStruct((2, 2 * rows, LANES), BF),
            full, full, double, double,
        ),
        in_specs=[SMEM, VMEM] + [ANY] * 3 + [VMEM] * len(refs),
        out_specs=(VMEM,) * 6,
        scratch_shapes=[
            pltpu.VMEM((2 * rows, LANES), BF),
            pltpu.VMEM((2, 2 * rows, (len(late) + 4) * LANES), BF),
            pltpu.VMEM((3 * LANES, len(late) * LANES), BF),
            pltpu.SemaphoreType.DMA((len(late) + 4, 3)),
        ],
        compiler_params=params(22),
        cost_estimate=COST,
        name="late",
    )(sc, acc, x_own, dy_own, xp, *refs)
    far, got = far[:2], far[2:]

    term = dict(zip((3, 5), got))

    def ring(up, down):
        return pz(up, 1), pz(down, -1)

    up, down = ring(*far)

    keys = list(chunks)
    parts, refs = listed(keys)
    keep, send = pl.pallas_call(
        functools.partial(dx_kernel, keys, parts, part),
        out_shape=(jax.ShapeDtypeStruct((rows, width), BF),) * 2,
        in_specs=[SMEM, VMEM] + [HBM] * len(refs),
        out_specs=(VMEM, VMEM),
        scratch_shapes=[
            pltpu.VMEM((3 * LANES, width), BF),
            pltpu.SemaphoreType.DMA((copies_of(parts, part),)),
        ],
        compiler_params=params(20),
        cost_estimate=COST,
        name="dx",
    )(sc, dgu, *refs)

    up, down, send = after_all(up, down, send)
    sent = pc(send)

    def joined(whole, halves, first):
        rows_of = [whole[i * mid : (i + 1) * mid].astype(F32) for i in range(4)]
        for i in range(2):
            rows_of[2 * i + first] += halves[i * mid : (i + 1) * mid]
        return jnp.concatenate([r.astype(BF) for r in rows_of])

    up, down = joined(term[3], up, 0), joined(term[5], down, 1)
    gt_later = after(gt, up, down)
    up, down = ring(up, down)
    distances = (2, 6, 1, 7, 0)
    keys = [(k, s) for s in distances for k in (1, 0)]
    got = pl.pallas_call(
        functools.partial(terms_kernel, keys, part),
        out_shape=(double,) * len(distances),
        in_specs=[SMEM, VMEM] + [ANY] * 3,
        out_specs=(VMEM,) * len(distances),
        scratch_shapes=[
            pltpu.VMEM((2, 2 * rows, len(keys) * LANES), BF),
            pltpu.SemaphoreType.DMA((len(keys), 3)),
        ],
        compiler_params=params(20),
        cost_estimate=COST,
        name="terms",
    )(sc, gt_later, x_own, dy_own, xp)
    term.update(zip(distances, got))

    quarter = rows // NX

    def pair(i):
        rows_of = slice(i * quarter, (i + 1) * quarter)
        return keep[rows_of].astype(F32) + sent[rows_of].astype(F32)

    acc = px(pair(3).astype(BF), -1)

    up, down, acc = after_all(up, down, acc)
    up, down = (term[2].astype(F32) + up).astype(BF), (term[6].astype(F32) + down).astype(BF)
    up, down = ring(up, down)
    acc = px((pair(2) + acc).astype(BF), -1)

    acc = (pair(1) + acc).astype(BF)
    up, down, acc = after_all(up, down, acc)
    acc = px(acc, -1)
    ends = []
    for k in range(2):
        rows_of = slice(k * n, (k + 1) * n)
        ends.append(
            (
                (term[1][rows_of].astype(F32) + up[rows_of]).astype(BF),
                (term[7][rows_of].astype(F32) + down[rows_of]).astype(BF),
            )
        )
        if k == 0:
            up, down, _, _ = after_all(up, down, *ends[0])
    acc = pair(0) + after(acc, *ends[0])
    p, o = ring(*ends[0]), ring(*ends[1])
    part_b = [acc[i * group : (i + 1) * group].astype(BF) for i in range(1, 4)]
    got = [pyh(part_b[0]), pyl(part_b[1]), pboth(part_b[2])]

    p = after(tuple(p), *part_b)
    sum_other = (term[0][:n].astype(F32) + p[0].astype(F32) + p[1].astype(F32)).astype(BF)
    o = after(tuple(o), sum_other)
    sum_other = pyl(sum_other)
    sum_own = (term[0][n:].astype(F32) + o[0].astype(F32) + o[1].astype(F32)).astype(BF)
    in_grad = (acc[:group] + got[0] + got[1] + got[2]).astype(BF).reshape(1, group, width)

    def whole(index):
        mine = sum_own[index * part : (index + 1) * part]
        theirs = sum_other[index * part : (index + 1) * part]
        return jnp.where(low[:1, :1], jnp.concatenate([mine, theirs]), jnp.concatenate([theirs, mine]))

    return in_grad, whole(0).T, whole(1).T, whole(2)


def solution(mesh):
    placed = (P("dp", None, None), P("dp", None, None), P("dp", "mp"), P("dp", "mp"), P("mp", "dp"))
    return jax.shard_map(
        local,
        mesh=mesh,
        in_specs=placed,
        out_specs=(P("dp", "mp", None), P("dp", "mp"), P("dp", "mp"), P("mp", "dp")),
        check_vma=False,
    )
```

```python
import functools

import jax
import jax.numpy as jnp
from jax import lax
from jax.experimental import pallas as pl
from jax.experimental.pallas import tpu as pltpu
from jax.sharding import PartitionSpec as P

BF = jnp.bfloat16
F32 = jnp.float32
NX, NZ = 4, 8
LANES = 256
ANY = pl.BlockSpec(memory_space=pl.ANY)
HBM = pl.BlockSpec(memory_space=pltpu.HBM)
VMEM = pl.BlockSpec(memory_space=pltpu.VMEM)
COST = pl.CostEstimate(flops=1, bytes_accessed=1, transcendentals=0)
SMEM = pl.BlockSpec(memory_space=pltpu.SMEM)


def mm(left, right):
    return lax.dot_general(left, right, (((1,), (0,)), ((), ())), preferred_element_type=F32)


def mm_t(left, right):
    return lax.dot_general(left, right, (((1,), (1,)), ((), ())), preferred_element_type=F32)


def pz(value, step):
    pairs = [(y * NZ + z, y * NZ + (z + step) % NZ) for y in range(2) for z in range(NZ)]
    return lax.ppermute(value, "dp", pairs)


def pyl(value):
    return lax.ppermute(value, "dp", [(i, (i + NZ) % (2 * NZ)) for i in range(2 * NZ)])


def px(value, step):
    pairs = [
        (y * 8 + x * 2 + c, y * 8 + (x + (-step if c else step)) % NX * 2 + c)
        for y in range(2) for x in range(NX) for c in range(2)
    ]
    return lax.ppermute(value, "mp", pairs)


def pxs(value, step):
    pairs = [
        (y * 8 + x * 2 + c, y * 8 + (x + step) % NX * 2 + c)
        for y in range(2) for x in range(NX) for c in range(2)
    ]
    return lax.ppermute(value, "mp", pairs)


def pc(value):
    return lax.ppermute(value, "mp", [(i, i ^ 1) for i in range(16)])


def pyh(value):
    return lax.ppermute(value, "mp", [(i, i ^ 8) for i in range(16)])


def pboth(value):
    n = 2 * NZ
    pairs = [(m * n + d, (m ^ 8) * n + (d + NZ) % n) for m in range(16) for d in range(n)]
    return lax.ppermute(value, ("mp", "dp"), pairs)


def after(value, *others):
    return lax.optimization_barrier((value, *others))[0]


def after_all(*values):
    return lax.optimization_barrier(values)


def col_block(sc, k, s):
    yl = 1 - sc[1] if k else sc[1]
    return yl * NZ + lax.rem(sc[0] + s, NZ)


def offset(sc, k, s):
    return pl.multiple_of(col_block(sc, k, s) * LANES, LANES)


def spread(row, count, part):
    out, end = [], row + count
    while row < end:
        m = row // part
        n = min(end, (m + 1) * part) - row
        out.append((row, n, m * LANES + row - m * part))
        row += n
    return out


def load_chunks(where, places, part, refs, buf, sems):
    waits, sem = [], 0
    for parts, place in zip(where, places):
        mine = []
        for at, row, start, count in parts:
            for first, n, to in spread(start, count, part):
                copy = pltpu.make_async_copy(
                    refs[at].at[pl.ds(row + first - start, n)],
                    buf.at[pl.ds(to, n), pl.ds(place, LANES)],
                    sems.at[sem],
                )
                copy.start()
                mine.append(copy)
                sem += 1
        waits.append(mine)
    return waits


def copies_of(where, part):
    return sum(len(spread(start, count, part)) for parts in where for _, _, start, count in parts)


def clear_pad(buf, part):
    for m in range(3):
        buf[m * LANES + part : (m + 1) * LANES] = jnp.zeros((LANES - part, buf.shape[1]), BF)


def early_kernel(keys, missing, parts, n_pieces, piece_at, part, sc, x, dy, *refs):
    pieces, chunks = refs[:n_pieces], refs[n_pieces:-7]
    acc, xp, xs, buf, w_sems, x_sems, out_sem = refs[-7:]
    rows = x.shape[0]
    loads = [
        pltpu.make_async_copy(x, xs.at[0, pl.ds(0, rows)], x_sems.at[0]),
        pltpu.make_async_copy(dy, xs.at[1, pl.ds(0, rows)], x_sems.at[1]),
    ]
    row = rows
    pieces = [pieces[i].at[j] for i, j in piece_at]
    for i, piece in enumerate(pieces):
        n = piece.shape[1]
        loads.append(pltpu.make_async_copy(piece, xs.at[:, pl.ds(row, n)], x_sems.at[2 + i]))
        row += n
    for copy in loads:
        copy.start()
    waits = load_chunks(parts, [offset(sc, *key) for key in keys], part, chunks, buf, w_sems)
    clear_pad(buf, part)
    for key in missing:
        buf[:, pl.ds(offset(sc, *key), LANES)] = jnp.zeros((buf.shape[0], LANES), BF)
    for copy in loads:
        copy.wait()
    store = pltpu.make_async_copy(xs.at[:, pl.ds(rows, rows)], xp, out_sem)
    store.start()
    for mine in waits:
        for copy in mine:
            copy.wait()
    acc[:, : 2 * LANES] = mm_t(xs[0], buf[: 2 * LANES])
    acc[:, 2 * LANES :] = mm_t(xs[1], buf[2 * LANES :])
    store.wait()


def put_terms(outs, part, top, low):
    two, n = 2 * part, 3 * part
    top, low = top.astype(BF), low.astype(BF)
    for j, out in enumerate(outs):
        for k in range(2):
            cols = slice((2 * j + k) * LANES, (2 * j + k + 1) * LANES)
            out[k * n : k * n + two] = top[:, cols]
            out[k * n + two : (k + 1) * n] = low[:, cols]


def late_kernel(keys, parts, term_keys, part, sc, acc, x, dy, xp, *refs):
    n_out = 8 + len(term_keys) // 2
    chunks = refs[:-n_out]
    gt, dgu, *outs = refs[-n_out:-4]
    far, outs = outs[:2], outs[2:]
    rowbuf, xb, buf, x_sems = refs[-4:]
    rows = x.shape[0]
    loads = []
    for i, (k, s) in enumerate(keys + term_keys):
        cols, to = pl.ds(offset(sc, k, s), LANES), pl.ds(i * LANES, LANES)
        loads += [
            pltpu.make_async_copy(x.at[:, cols], xb.at[0, pl.ds(0, rows), to], x_sems.at[i, 0]),
            pltpu.make_async_copy(dy.at[:, cols], xb.at[1, pl.ds(0, rows), to], x_sems.at[i, 1]),
            pltpu.make_async_copy(xp.at[:, :, cols], xb.at[:, pl.ds(rows, rows), to], x_sems.at[i, 2]),
        ]
    for copy in loads:
        copy.start()
    clear_pad(buf, part)
    for i, pieces in enumerate(parts):
        for at, row, start, count in pieces:
            for first, n, to in spread(start, count, part):
                row_at = row + first - start
                buf[to : to + n, i * LANES : (i + 1) * LANES] = chunks[at][row_at : row_at + n]
    for copy in loads[: 3 * len(keys)]:
        copy.wait()
    used = len(keys) * LANES
    both = acc[:, : 2 * LANES] + mm_t(xb[0, :, :used], buf[: 2 * LANES])
    dhid = acc[:, 2 * LANES :] + mm_t(xb[1, :, :used], buf[2 * LANES :])
    gate, up_val = both[:, :LANES], both[:, LANES:]
    sig = 1.0 / (1.0 + jnp.exp(-gate))
    silu = gate * sig
    hidden = silu * up_val
    dup = dhid * silu
    dgate = dhid * up_val * sig * (1.0 + gate * (1.0 - sig))
    for m, value in enumerate((dgate, dup, hidden)):
        gt[m * part : (m + 1) * part] = value.T[:part].astype(BF)
    mid = 3 * part // 2
    two = 2 * part
    up, down = far
    for j in range(2):
        cols = slice(j * LANES, (j + 1) * LANES)
        top, low = mm(gt[:two], xb[0, :, cols]), mm(gt[two:], xb[1, :, cols])
        at = j * mid
        up[at : at + mid] = top[:mid].astype(BF)
        down[at : at + two - mid] = top[mid:].astype(BF)
        down[at + two - mid : at + mid] = low.astype(BF)
    for copy in loads[3 * len(keys) :]:
        copy.wait()
    put_terms(outs, part, mm(gt[:two], xb[0, :, used:]), mm(gt[two:], xb[1, :, used:]))
    group = rows // 16
    for m, value in enumerate((dgate, dup)):
        rowbuf[...] = value.astype(BF)
        for g in range(16):
            to = g // 2 * 4 * group + g % 2 * group
            at = pl.multiple_of(sc[2 + g] * group, group)
            dgu[m, to : to + group] = rowbuf[pl.ds(at, group)]
        for g in range(8):
            to = g * 4 * group + 2 * group
            at = pl.multiple_of(rows + sc[18 + g] * 2 * group, 2 * group)
            dgu[m, to : to + 2 * group] = rowbuf[pl.ds(at, 2 * group)]


def dx_kernel(keys, parts, part, sc, dgu, *refs):
    chunks, (keep, send, buf, w_sems) = refs[:-4], refs[-4:]
    rows = keep.shape[0]
    waits = load_chunks(parts, [offset(sc, *key) for key in keys], part, chunks, buf, w_sems)
    clear_pad(buf, part)
    for mine in waits:
        for copy in mine:
            copy.wait()
    step = 4 * LANES
    for at in range(0, keep.shape[1], step):
        cols = slice(at, at + step)
        dx = mm(dgu[0], buf[:LANES, cols]) + mm(dgu[1], buf[LANES : 2 * LANES, cols])
        keep[:, cols] = dx[:rows].astype(BF)
        send[:, cols] = dx[rows:].astype(BF)


def terms_kernel(keys, part, sc, gt, x, dy, xp, *refs):
    outs, (xb, x_sems) = refs[:-2], refs[-2:]
    rows = x.shape[0]
    loads = []
    for i, (k, s) in enumerate(keys):
        cols, to = pl.ds(offset(sc, k, s), LANES), pl.ds(i * LANES, LANES)
        mine = [
            pltpu.make_async_copy(x.at[:, cols], xb.at[0, pl.ds(0, rows), to], x_sems.at[i, 0]),
            pltpu.make_async_copy(dy.at[:, cols], xb.at[1, pl.ds(0, rows), to], x_sems.at[i, 1]),
            pltpu.make_async_copy(xp.at[:, :, cols], xb.at[:, pl.ds(rows, rows), to], x_sems.at[i, 2]),
        ]
        for copy in mine:
            copy.start()
        loads.append(mine)
    two = 2 * part
    for i in range(0, len(keys), 2):
        for copy in loads[i] + loads[i + 1]:
            copy.wait()
        cols = slice(i * LANES, (i + 2) * LANES)
        put_terms(outs[i // 2 : i // 2 + 1], part, mm(gt[:two], xb[0, :, cols]), mm(gt[two:], xb[1, :, cols]))


def cut_kernel(part, sc, *refs):
    weights, (own, other, sems) = refs[:3], refs[3:]
    copies = []
    for m, w in enumerate(weights):
        for i, out in enumerate((own, other)):
            start = pl.multiple_of((1 - sc[1] if i else sc[1]) * part, part)
            copies.append(
                pltpu.make_async_copy(w.at[pl.ds(start, part)], out.at[pl.ds(m * part, part)], sems.at[m, i])
            )
    for copy in copies:
        copy.start()
    for copy in copies:
        copy.wait()


def join_kernel(part, sc, own, other, *outs):
    mine, theirs = pl.multiple_of(sc[1] * part, part), pl.multiple_of((1 - sc[1]) * part, part)
    for m, out in enumerate(outs):
        out[pl.ds(mine, part)] = own[m * part : (m + 1) * part]
        out[pl.ds(theirs, part)] = other[m * part : (m + 1) * part]


def params(mib):
    return pltpu.CompilerParams(vmem_limit_bytes=mib * 1024 * 1024)


def local(inputs, out_grad, w_gate, w_up, w_down):
    rows, width = inputs.shape[1:]
    part = w_down.shape[0] // 2
    dp, mp = lax.axis_index("dp"), lax.axis_index("mp")
    yl, z = dp // NZ, dp % NZ
    yh, x, c = mp // 8, mp // 2 % NX, mp % 2
    group = rows // 16
    x_own, dy_own = inputs[0], out_grad[0]

    slot = lax.iota(jnp.int32, 26)
    at = slot - 2
    dc, dx, dh = at // 8, at // 2 % NX, at % 2
    ordered = (yh ^ dh) * 8 + (x - (1 - 2 * (c ^ dc)) * dx + NX) % NX * 2 + (c ^ dc)
    at = slot - 18
    dc, dx = at // NX % 2, at % NX
    stands = dc * NX + (NX - (1 - 2 * (c ^ dc)) * dx) % NX
    sc = jnp.where(slot < 2, jnp.where(slot == 0, z, yl), jnp.where(slot < 18, ordered, stands)).astype(jnp.int32)

    u32 = jnp.uint32
    w_gate, w_up, w_down, x_own, dy_own, sc, *starts = after_all(
        w_gate, w_up, w_down, x_own, dy_own, sc, (mp * group).astype(u32), ((mp ^ 8) * group).astype(u32)
    )

    own, other = pl.pallas_call(
        functools.partial(cut_kernel, part),
        out_shape=(jax.ShapeDtypeStruct((3 * part, LANES), BF),) * 2,
        in_specs=[SMEM] + [ANY] * 3,
        out_specs=(ANY,) * 2,
        scratch_shapes=[pltpu.SemaphoreType.DMA((3, 2))],
        compiler_params=params(59),
        cost_estimate=COST,
        name="cut",
    )(sc, w_gate.T, w_up.T, w_down)
    mid = own.shape[0] // 2

    def piece(array):
        cut = [lax.dynamic_slice(array, (start, u32(0)), (group, array.shape[1])) for start in starts]
        return jnp.concatenate(cut)

    n = own.shape[0]
    up, down = pz(own, 1), pz(own, -1)
    other = pyl(other)
    chunks = {
        (0, 0): [(own, 0, 0, n)],
        (0, 7): [(up, 0, 0, n)],
        (0, 1): [(down, 0, 0, n)],
        (1, 0): [(other, 0, 0, n)],
    }
    first = jnp.stack([piece(after(x_own, own)), piece(after(dy_own, own))])
    first = pyl(after(first, up, down))
    up, down = jnp.concatenate([other, up]), jnp.concatenate([down, other])
    for step in (1, 2):
        up, down = pz(up, 1), pz(down, -1)
        chunks[1, NZ - step], chunks[0, NZ - step - 1] = [(up, 0, 0, n)], [(up, n, 0, n)]
        chunks[0, step + 1], chunks[1, step] = [(down, 0, 0, n)], [(down, n, 0, n)]
        up, down = after_all(up, down)
        if step == 1:
            left, right = pxs(first, 1), pxs(first, -1)
            left_s, right_s, first_s, _, _ = after_all(left, right, first, up, down)
            far_x, far_dy = pxs(left_s[0], 1), pxs(right_s[1], -1)
            swap = pc(jnp.stack([first_s, right_s, left_s]))
    up, down = up[: n + mid], down[mid:]
    far_x, far_dy, _, _ = after_all(far_x, far_dy, up, down)
    two_off = jnp.stack([far_x, far_dy])
    swap_two = pc(two_off)
    up, down = pz(up, 1), pz(down, -1)
    chunks[1, 5], chunks[1, 3] = [(up, 0, 0, n)], [(down, n - mid, 0, n)]
    chunks[0, 4] = [(up, n, 0, mid), (down, 0, mid, n - mid)]
    pieces = [first[None], right[None], two_off[None], left[None], swap, swap_two[None]]
    piece_at = [(0, 0), (1, 0), (2, 0), (3, 0), (4, 0), (4, 1), (5, 0), (4, 2)]

    late = [(1, 4), (0, 4), (1, 3), (1, 5)]
    early = [key for key in chunks if key not in late]

    def listed(keys):
        refs, where = [], []
        for key in keys:
            parts = []
            for array, *rest in chunks[key]:
                at = [i for i, a in enumerate(refs) if a is array]
                if not at:
                    refs.append(array)
                parts.append((at[0] if at else len(refs) - 1, *rest))
            where.append(tuple(parts))
        return tuple(where), refs

    parts, refs = listed(early)
    acc, xp = pl.pallas_call(
        functools.partial(early_kernel, early, late, parts, len(pieces), piece_at, part),
        out_shape=(
            jax.ShapeDtypeStruct((2 * rows, 3 * LANES), F32),
            jax.ShapeDtypeStruct((2, rows, width), BF),
        ),
        in_specs=[SMEM] + [HBM] * (2 + len(pieces) + len(refs)),
        out_specs=(VMEM, ANY),
        scratch_shapes=[
            pltpu.VMEM((2, 2 * rows, width), BF),
            pltpu.VMEM((3 * LANES, width), BF),
            pltpu.SemaphoreType.DMA((copies_of(parts, part),)),
            pltpu.SemaphoreType.DMA((2 + 2 * NX,)),
            pltpu.SemaphoreType.DMA,
        ],
        compiler_params=params(22),
        cost_estimate=COST,
        name="early",
    )(sc, x_own, dy_own, *pieces, *refs)

    up, down, acc, xp = after_all(up, down, acc, xp)
    up, down = pz(up[:mid], 1), pz(down[n:], -1)
    chunks[1, 4] = [(up, 0, 0, mid), (down, 0, mid, n - mid)]

    parts, refs = listed(late)
    full = jax.ShapeDtypeStruct((3 * part, LANES), BF)
    double = jax.ShapeDtypeStruct((6 * part, LANES), BF)
    late_terms = [(1, 3), (0, 3), (1, 5), (0, 5)]
    gt, dgu, *far = pl.pallas_call(
        functools.partial(late_kernel, late, parts, late_terms, part),
        out_shape=(
            jax.ShapeDtypeStruct((3 * part, 2 * rows), BF),
            jax.ShapeDtypeStruct((2, 2 * rows, LANES), BF),
            full, full, double, double,
        ),
        in_specs=[SMEM, VMEM] + [ANY] * 3 + [VMEM] * len(refs),
        out_specs=(VMEM,) * 6,
        scratch_shapes=[
            pltpu.VMEM((2 * rows, LANES), BF),
            pltpu.VMEM((2, 2 * rows, (len(late) + 4) * LANES), BF),
            pltpu.VMEM((3 * LANES, len(late) * LANES), BF),
            pltpu.SemaphoreType.DMA((len(late) + 4, 3)),
        ],
        compiler_params=params(22),
        cost_estimate=COST,
        name="late",
    )(sc, acc, x_own, dy_own, xp, *refs)
    far, got = far[:2], far[2:]

    term = dict(zip((3, 5), got))

    def ring(up, down):
        return pz(up, 1), pz(down, -1)

    up, down = ring(*far)

    keys = list(chunks)
    parts, refs = listed(keys)
    keep, send = pl.pallas_call(
        functools.partial(dx_kernel, keys, parts, part),
        out_shape=(jax.ShapeDtypeStruct((rows, width), BF),) * 2,
        in_specs=[SMEM, VMEM] + [HBM] * len(refs),
        out_specs=(VMEM, VMEM),
        scratch_shapes=[
            pltpu.VMEM((3 * LANES, width), BF),
            pltpu.SemaphoreType.DMA((copies_of(parts, part),)),
        ],
        compiler_params=params(20),
        cost_estimate=COST,
        name="dx",
    )(sc, dgu, *refs)

    up, down, send = after_all(up, down, send)
    sent = pc(send)

    def joined(whole, halves, first):
        rows_of = [whole[i * mid : (i + 1) * mid].astype(F32) for i in range(4)]
        for i in range(2):
            rows_of[2 * i + first] += halves[i * mid : (i + 1) * mid]
        return jnp.concatenate([r.astype(BF) for r in rows_of])

    up, down = joined(term[3], up, 0), joined(term[5], down, 1)
    gt_later = after(gt, up, down)
    up, down = ring(up, down)
    distances = (2, 6, 1, 7, 0)
    keys = [(k, s) for s in distances for k in (1, 0)]
    got = pl.pallas_call(
        functools.partial(terms_kernel, keys, part),
        out_shape=(double,) * len(distances),
        in_specs=[SMEM, VMEM] + [ANY] * 3,
        out_specs=(VMEM,) * len(distances),
        scratch_shapes=[
            pltpu.VMEM((2, 2 * rows, len(keys) * LANES), BF),
            pltpu.SemaphoreType.DMA((len(keys), 3)),
        ],
        compiler_params=params(20),
        cost_estimate=COST,
        name="terms",
    )(sc, gt_later, x_own, dy_own, xp)
    term.update(zip(distances, got))

    quarter = rows // NX

    def pair(i):
        rows_of = slice(i * quarter, (i + 1) * quarter)
        return keep[rows_of].astype(F32) + sent[rows_of].astype(F32)

    acc = px(pair(3).astype(BF), -1)

    up, down, acc = after_all(up, down, acc)
    up, down = (term[2].astype(F32) + up).astype(BF), (term[6].astype(F32) + down).astype(BF)
    up, down = ring(up, down)
    acc = px((pair(2) + acc).astype(BF), -1)

    acc = (pair(1) + acc).astype(BF)
    up, down, acc = after_all(up, down, acc)
    acc = px(acc, -1)
    ends = []
    for k in range(2):
        rows_of = slice(k * n, (k + 1) * n)
        ends.append(
            (
                (term[1][rows_of].astype(F32) + up[rows_of]).astype(BF),
                (term[7][rows_of].astype(F32) + down[rows_of]).astype(BF),
            )
        )
        if k == 0:
            up, down, _, _ = after_all(up, down, *ends[0])
    acc = pair(0) + after(acc, *ends[0])
    p, o = ring(*ends[0]), ring(*ends[1])
    part_b = [acc[i * group : (i + 1) * group].astype(BF) for i in range(1, 4)]
    sum_other = (term[0][:n].astype(F32) + p[0].astype(F32) + p[1].astype(F32)).astype(BF)
    *part_b, _ = after_all(*part_b, sum_other)
    got = [pyh(part_b[0]), pyl(part_b[1]), pboth(part_b[2])]
    o = after(tuple(o), sum_other)
    sum_other = pyl(sum_other)
    sum_own = (term[0][n:].astype(F32) + o[0].astype(F32) + o[1].astype(F32)).astype(BF)
    in_grad = (acc[:group] + got[0] + got[1] + got[2]).astype(BF).reshape(1, group, width)

    gate_grad, up_grad, down_grad = pl.pallas_call(
        functools.partial(join_kernel, part),
        out_shape=(jax.ShapeDtypeStruct((2 * part, LANES), BF),) * 3,
        in_specs=[SMEM, VMEM, VMEM],
        out_specs=(VMEM,) * 3,
        compiler_params=params(8),
        cost_estimate=COST,
        name="join",
    )(sc, sum_own, sum_other)
    return in_grad, gate_grad.T, up_grad.T, down_grad


def solution(mesh):
    placed = (P("dp", None, None), P("dp", None, None), P("dp", "mp"), P("dp", "mp"), P("mp", "dp"))
    return jax.shard_map(
        local,
        mesh=mesh,
        in_specs=placed,
        out_specs=(P("dp", "mp", None), P("dp", "mp"), P("dp", "mp"), P("mp", "dp")),
        check_vma=False,
    )
```

```python
import functools

import jax
import jax.numpy as jnp
from jax import lax
from jax.experimental import pallas as pl
from jax.experimental.pallas import tpu as pltpu
from jax.sharding import PartitionSpec as P

BF = jnp.bfloat16
F32 = jnp.float32
NX, NZ = 4, 8
LANES = 256
ANY = pl.BlockSpec(memory_space=pl.ANY)
HBM = pl.BlockSpec(memory_space=pltpu.HBM)
VMEM = pl.BlockSpec(memory_space=pltpu.VMEM)
COST = pl.CostEstimate(flops=1, bytes_accessed=1, transcendentals=0)
SMEM = pl.BlockSpec(memory_space=pltpu.SMEM)


def mm(left, right):
    return lax.dot_general(left, right, (((1,), (0,)), ((), ())), preferred_element_type=F32)


def mm_t(left, right):
    return lax.dot_general(left, right, (((1,), (1,)), ((), ())), preferred_element_type=F32)


def pz(value, step):
    pairs = [(y * NZ + z, y * NZ + (z + step) % NZ) for y in range(2) for z in range(NZ)]
    return lax.ppermute(value, "dp", pairs)


def pyl(value):
    return lax.ppermute(value, "dp", [(i, (i + NZ) % (2 * NZ)) for i in range(2 * NZ)])


def px(value, step):
    pairs = [
        (y * 8 + x * 2 + c, y * 8 + (x + (-step if c else step)) % NX * 2 + c)
        for y in range(2) for x in range(NX) for c in range(2)
    ]
    return lax.ppermute(value, "mp", pairs)


def pxs(value, step):
    pairs = [
        (y * 8 + x * 2 + c, y * 8 + (x + step) % NX * 2 + c)
        for y in range(2) for x in range(NX) for c in range(2)
    ]
    return lax.ppermute(value, "mp", pairs)


def pc(value):
    return lax.ppermute(value, "mp", [(i, i ^ 1) for i in range(16)])


def pyh(value):
    return lax.ppermute(value, "mp", [(i, i ^ 8) for i in range(16)])


def pboth(value):
    n = 2 * NZ
    pairs = [(m * n + d, (m ^ 8) * n + (d + NZ) % n) for m in range(16) for d in range(n)]
    return lax.ppermute(value, ("mp", "dp"), pairs)


def after(value, *others):
    return lax.optimization_barrier((value, *others))[0]


def after_all(*values):
    return lax.optimization_barrier(values)


def col_block(sc, k, s):
    yl = 1 - sc[1] if k else sc[1]
    return yl * NZ + lax.rem(sc[0] + s, NZ)


def offset(sc, k, s):
    return pl.multiple_of(col_block(sc, k, s) * LANES, LANES)


def spread(row, count, part):
    out, end = [], row + count
    while row < end:
        m = row // part
        n = min(end, (m + 1) * part) - row
        out.append((row, n, m * LANES + row - m * part))
        row += n
    return out


def load_chunks(where, places, part, refs, buf, sems):
    waits, sem = [], 0
    for parts, place in zip(where, places):
        mine = []
        for at, row, start, count in parts:
            for first, n, to in spread(start, count, part):
                copy = pltpu.make_async_copy(
                    refs[at].at[pl.ds(row + first - start, n)],
                    buf.at[pl.ds(to, n), pl.ds(place, LANES)],
                    sems.at[sem],
                )
                copy.start()
                mine.append(copy)
                sem += 1
        waits.append(mine)
    return waits


def copies_of(where, part):
    return sum(len(spread(start, count, part)) for parts in where for _, _, start, count in parts)


def clear_pad(buf, part):
    for m in range(3):
        buf[m * LANES + part : (m + 1) * LANES] = jnp.zeros((LANES - part, buf.shape[1]), BF)


def early_kernel(keys, missing, parts, n_pieces, piece_at, part, sc, x, dy, *refs):
    pieces, chunks = refs[:n_pieces], refs[n_pieces:-7]
    acc, xp, xs, buf, w_sems, x_sems, out_sem = refs[-7:]
    rows = x.shape[0]
    loads = [
        pltpu.make_async_copy(x, xs.at[0, pl.ds(0, rows)], x_sems.at[0]),
        pltpu.make_async_copy(dy, xs.at[1, pl.ds(0, rows)], x_sems.at[1]),
    ]
    row = rows
    pieces = [pieces[i].at[j] for i, j in piece_at]
    for i, piece in enumerate(pieces):
        n = piece.shape[1]
        loads.append(pltpu.make_async_copy(piece, xs.at[:, pl.ds(row, n)], x_sems.at[2 + i]))
        row += n
    for copy in loads:
        copy.start()
    waits = load_chunks(parts, [offset(sc, *key) for key in keys], part, chunks, buf, w_sems)
    clear_pad(buf, part)
    for key in missing:
        buf[:, pl.ds(offset(sc, *key), LANES)] = jnp.zeros((buf.shape[0], LANES), BF)
    for copy in loads:
        copy.wait()
    store = pltpu.make_async_copy(xs.at[:, pl.ds(rows, rows)], xp, out_sem)
    store.start()
    for mine in waits:
        for copy in mine:
            copy.wait()
    acc[:, : 2 * LANES] = mm_t(xs[0], buf[: 2 * LANES])
    acc[:, 2 * LANES :] = mm_t(xs[1], buf[2 * LANES :])
    store.wait()


def put_terms(outs, part, top, low):
    two, n = 2 * part, 3 * part
    top, low = top.astype(BF), low.astype(BF)
    for j, out in enumerate(outs):
        for k in range(2):
            cols = slice((2 * j + k) * LANES, (2 * j + k + 1) * LANES)
            out[k * n : k * n + two] = top[:, cols]
            out[k * n + two : (k + 1) * n] = low[:, cols]


def late_kernel(keys, parts, term_keys, part, sc, acc, x, dy, xp, *refs):
    n_out = 8 + len(term_keys) // 2
    chunks = refs[:-n_out]
    gt, dgu, *outs = refs[-n_out:-4]
    far, outs = outs[:2], outs[2:]
    rowbuf, xb, buf, x_sems = refs[-4:]
    rows = x.shape[0]
    loads = []
    for i, (k, s) in enumerate(keys + term_keys):
        cols, to = pl.ds(offset(sc, k, s), LANES), pl.ds(i * LANES, LANES)
        loads += [
            pltpu.make_async_copy(x.at[:, cols], xb.at[0, pl.ds(0, rows), to], x_sems.at[i, 0]),
            pltpu.make_async_copy(dy.at[:, cols], xb.at[1, pl.ds(0, rows), to], x_sems.at[i, 1]),
            pltpu.make_async_copy(xp.at[:, :, cols], xb.at[:, pl.ds(rows, rows), to], x_sems.at[i, 2]),
        ]
    for copy in loads:
        copy.start()
    clear_pad(buf, part)
    for i, pieces in enumerate(parts):
        for at, row, start, count in pieces:
            for first, n, to in spread(start, count, part):
                row_at = row + first - start
                buf[to : to + n, i * LANES : (i + 1) * LANES] = chunks[at][row_at : row_at + n]
    for copy in loads[: 3 * len(keys)]:
        copy.wait()
    used = len(keys) * LANES
    both = acc[:, : 2 * LANES] + mm_t(xb[0, :, :used], buf[: 2 * LANES])
    dhid = acc[:, 2 * LANES :] + mm_t(xb[1, :, :used], buf[2 * LANES :])
    gate, up_val = both[:, :LANES], both[:, LANES:]
    sig = 1.0 / (1.0 + jnp.exp(-gate))
    silu = gate * sig
    hidden = silu * up_val
    dup = dhid * silu
    dgate = dhid * up_val * sig * (1.0 + gate * (1.0 - sig))
    for m, value in enumerate((dgate, dup, hidden)):
        gt[m * part : (m + 1) * part] = value.T[:part].astype(BF)
    mid = 3 * part // 2
    two = 2 * part
    up, down = far
    for j in range(2):
        cols = slice(j * LANES, (j + 1) * LANES)
        top, low = mm(gt[:two], xb[0, :, cols]), mm(gt[two:], xb[1, :, cols])
        at = j * mid
        up[at : at + mid] = top[:mid].astype(BF)
        down[at : at + two - mid] = top[mid:].astype(BF)
        down[at + two - mid : at + mid] = low.astype(BF)
    for copy in loads[3 * len(keys) :]:
        copy.wait()
    put_terms(outs, part, mm(gt[:two], xb[0, :, used:]), mm(gt[two:], xb[1, :, used:]))
    group = rows // 16
    for m, value in enumerate((dgate, dup)):
        rowbuf[...] = value.astype(BF)
        for g in range(16):
            to = g // 2 * 4 * group + g % 2 * group
            at = pl.multiple_of(sc[2 + g] * group, group)
            dgu[m, to : to + group] = rowbuf[pl.ds(at, group)]
        for g in range(8):
            to = g * 4 * group + 2 * group
            at = pl.multiple_of(rows + sc[18 + g] * 2 * group, 2 * group)
            dgu[m, to : to + 2 * group] = rowbuf[pl.ds(at, 2 * group)]


def dx_kernel(keys, parts, part, sc, dgu, *refs):
    chunks, (keep, send, buf, w_sems) = refs[:-4], refs[-4:]
    rows = keep.shape[0]
    waits = load_chunks(parts, [offset(sc, *key) for key in keys], part, chunks, buf, w_sems)
    clear_pad(buf, part)
    for mine in waits:
        for copy in mine:
            copy.wait()
    step = 4 * LANES
    for at in range(0, keep.shape[1], step):
        cols = slice(at, at + step)
        dx = mm(dgu[0], buf[:LANES, cols]) + mm(dgu[1], buf[LANES : 2 * LANES, cols])
        keep[:, cols] = dx[:rows].astype(BF)
        send[:, cols] = dx[rows:].astype(BF)


def terms_kernel(keys, part, sc, gt, x, dy, xp, *refs):
    outs, (xb, x_sems) = refs[:-2], refs[-2:]
    rows = x.shape[0]
    loads = []
    for i, (k, s) in enumerate(keys):
        cols, to = pl.ds(offset(sc, k, s), LANES), pl.ds(i * LANES, LANES)
        mine = [
            pltpu.make_async_copy(x.at[:, cols], xb.at[0, pl.ds(0, rows), to], x_sems.at[i, 0]),
            pltpu.make_async_copy(dy.at[:, cols], xb.at[1, pl.ds(0, rows), to], x_sems.at[i, 1]),
            pltpu.make_async_copy(xp.at[:, :, cols], xb.at[:, pl.ds(rows, rows), to], x_sems.at[i, 2]),
        ]
        for copy in mine:
            copy.start()
        loads.append(mine)
    two = 2 * part
    for i in range(0, len(keys), 2):
        for copy in loads[i] + loads[i + 1]:
            copy.wait()
        cols = slice(i * LANES, (i + 2) * LANES)
        put_terms(outs[i // 2 : i // 2 + 1], part, mm(gt[:two], xb[0, :, cols]), mm(gt[two:], xb[1, :, cols]))


def cut_kernel(part, sc, *refs):
    weights, (own, other, sems) = refs[:3], refs[3:]
    copies = []
    for m, w in enumerate(weights):
        for i, out in enumerate((own, other)):
            start = pl.multiple_of((1 - sc[1] if i else sc[1]) * part, part)
            copies.append(
                pltpu.make_async_copy(w.at[pl.ds(start, part)], out.at[pl.ds(m * part, part)], sems.at[m, i])
            )
    for copy in copies:
        copy.start()
    for copy in copies:
        copy.wait()


def join_kernel(part, sc, own, other, *outs):
    mine, theirs = pl.multiple_of(sc[1] * part, part), pl.multiple_of((1 - sc[1]) * part, part)
    for m, out in enumerate(outs):
        out[pl.ds(mine, part)] = own[m * part : (m + 1) * part]
        out[pl.ds(theirs, part)] = other[m * part : (m + 1) * part]


def params(mib):
    return pltpu.CompilerParams(vmem_limit_bytes=mib * 1024 * 1024)


def local(inputs, out_grad, w_gate, w_up, w_down):
    rows, width = inputs.shape[1:]
    part = w_down.shape[0] // 2
    dp, mp = lax.axis_index("dp"), lax.axis_index("mp")
    yl, z = dp // NZ, dp % NZ
    yh, x, c = mp // 8, mp // 2 % NX, mp % 2
    group = rows // 16
    x_own, dy_own = inputs[0], out_grad[0]

    slot = lax.iota(jnp.int32, 26)
    at = slot - 2
    dc, dx, dh = at // 8, at // 2 % NX, at % 2
    ordered = (yh ^ dh) * 8 + (x - (1 - 2 * (c ^ dc)) * dx + NX) % NX * 2 + (c ^ dc)
    at = slot - 18
    dc, dx = at // NX % 2, at % NX
    stands = dc * NX + (NX - (1 - 2 * (c ^ dc)) * dx) % NX
    sc = jnp.where(slot < 2, jnp.where(slot == 0, z, yl), jnp.where(slot < 18, ordered, stands)).astype(jnp.int32)

    u32 = jnp.uint32
    w_gate, w_up, w_down, x_own, dy_own, sc, *starts = after_all(
        w_gate, w_up, w_down, x_own, dy_own, sc, (mp * group).astype(u32), ((mp ^ 8) * group).astype(u32)
    )

    own, other = pl.pallas_call(
        functools.partial(cut_kernel, part),
        out_shape=(jax.ShapeDtypeStruct((3 * part, LANES), BF),) * 2,
        in_specs=[SMEM] + [ANY] * 3,
        out_specs=(VMEM,) * 2,
        scratch_shapes=[pltpu.SemaphoreType.DMA((3, 2))],
        compiler_params=params(59),
        cost_estimate=COST,
        name="cut",
    )(sc, w_gate.T, w_up.T, w_down)
    mid = own.shape[0] // 2

    def piece(array):
        cut = [lax.dynamic_slice(array, (start, u32(0)), (group, array.shape[1])) for start in starts]
        return jnp.concatenate(cut)

    n = own.shape[0]
    up, down = pz(own, 1), pz(own, -1)
    other = pyl(other)
    chunks = {
        (0, 0): [(own, 0, 0, n)],
        (0, 7): [(up, 0, 0, n)],
        (0, 1): [(down, 0, 0, n)],
        (1, 0): [(other, 0, 0, n)],
    }
    first = jnp.stack([piece(after(x_own, own)), piece(after(dy_own, own))])
    first = pyl(first)
    up, down = jnp.concatenate([other, up]), jnp.concatenate([down, other])
    for step in (1, 2):
        up, down = pz(up, 1), pz(down, -1)
        chunks[1, NZ - step], chunks[0, NZ - step - 1] = [(up, 0, 0, n)], [(up, n, 0, n)]
        chunks[0, step + 1], chunks[1, step] = [(down, 0, 0, n)], [(down, n, 0, n)]
        up, down = after_all(up, down)
        if step == 1:
            left, right = pxs(first, 1), pxs(first, -1)
            left_s, right_s, first_s, _, _ = after_all(left, right, first, up, down)
            far_x, far_dy = pxs(left_s[0], 1), pxs(right_s[1], -1)
            swap = pc(jnp.stack([first_s, right_s, left_s]))
    up, down = up[: n + mid], down[mid:]
    far_x, far_dy, _, _ = after_all(far_x, far_dy, up, down)
    two_off = jnp.stack([far_x, far_dy])
    swap_two = pc(two_off)
    up, down = pz(up, 1), pz(down, -1)
    chunks[1, 5], chunks[1, 3] = [(up, 0, 0, n)], [(down, n - mid, 0, n)]
    chunks[0, 4] = [(up, n, 0, mid), (down, 0, mid, n - mid)]
    pieces = [first[None], right[None], two_off[None], left[None], swap, swap_two[None]]
    piece_at = [(0, 0), (1, 0), (2, 0), (3, 0), (4, 0), (4, 1), (5, 0), (4, 2)]

    late = [(1, 4), (0, 4), (1, 3), (1, 5)]
    early = [key for key in chunks if key not in late]

    def listed(keys):
        refs, where = [], []
        for key in keys:
            parts = []
            for array, *rest in chunks[key]:
                at = [i for i, a in enumerate(refs) if a is array]
                if not at:
                    refs.append(array)
                parts.append((at[0] if at else len(refs) - 1, *rest))
            where.append(tuple(parts))
        return tuple(where), refs

    parts, refs = listed(early)
    acc, xp = pl.pallas_call(
        functools.partial(early_kernel, early, late, parts, len(pieces), piece_at, part),
        out_shape=(
            jax.ShapeDtypeStruct((2 * rows, 3 * LANES), F32),
            jax.ShapeDtypeStruct((2, rows, width), BF),
        ),
        in_specs=[SMEM] + [HBM] * (2 + len(pieces) + len(refs)),
        out_specs=(VMEM, ANY),
        scratch_shapes=[
            pltpu.VMEM((2, 2 * rows, width), BF),
            pltpu.VMEM((3 * LANES, width), BF),
            pltpu.SemaphoreType.DMA((copies_of(parts, part),)),
            pltpu.SemaphoreType.DMA((2 + 2 * NX,)),
            pltpu.SemaphoreType.DMA,
        ],
        compiler_params=params(22),
        cost_estimate=COST,
        name="early",
    )(sc, x_own, dy_own, *pieces, *refs)

    up, down, acc, xp = after_all(up, down, acc, xp)
    up, down = pz(up[:mid], 1), pz(down[n:], -1)
    chunks[1, 4] = [(up, 0, 0, mid), (down, 0, mid, n - mid)]

    parts, refs = listed(late)
    full = jax.ShapeDtypeStruct((3 * part, LANES), BF)
    double = jax.ShapeDtypeStruct((6 * part, LANES), BF)
    late_terms = [(1, 3), (0, 3), (1, 5), (0, 5)]
    gt, dgu, *far = pl.pallas_call(
        functools.partial(late_kernel, late, parts, late_terms, part),
        out_shape=(
            jax.ShapeDtypeStruct((3 * part, 2 * rows), BF),
            jax.ShapeDtypeStruct((2, 2 * rows, LANES), BF),
            full, full, double, double,
        ),
        in_specs=[SMEM, VMEM] + [ANY] * 3 + [VMEM] * len(refs),
        out_specs=(VMEM,) * 6,
        scratch_shapes=[
            pltpu.VMEM((2 * rows, LANES), BF),
            pltpu.VMEM((2, 2 * rows, (len(late) + 4) * LANES), BF),
            pltpu.VMEM((3 * LANES, len(late) * LANES), BF),
            pltpu.SemaphoreType.DMA((len(late) + 4, 3)),
        ],
        compiler_params=params(22),
        cost_estimate=COST,
        name="late",
    )(sc, acc, x_own, dy_own, xp, *refs)
    far, got = far[:2], far[2:]

    term = dict(zip((3, 5), got))

    def ring(up, down):
        return pz(up, 1), pz(down, -1)

    up, down = ring(*far)

    keys = list(chunks)
    parts, refs = listed(keys)
    keep, send = pl.pallas_call(
        functools.partial(dx_kernel, keys, parts, part),
        out_shape=(jax.ShapeDtypeStruct((rows, width), BF),) * 2,
        in_specs=[SMEM, VMEM] + [HBM] * len(refs),
        out_specs=(VMEM, VMEM),
        scratch_shapes=[
            pltpu.VMEM((3 * LANES, width), BF),
            pltpu.SemaphoreType.DMA((copies_of(parts, part),)),
        ],
        compiler_params=params(20),
        cost_estimate=COST,
        name="dx",
    )(sc, dgu, *refs)

    up, down, send = after_all(up, down, send)
    sent = pc(send)

    def joined(whole, halves, first):
        rows_of = [whole[i * mid : (i + 1) * mid].astype(F32) for i in range(4)]
        for i in range(2):
            rows_of[2 * i + first] += halves[i * mid : (i + 1) * mid]
        return jnp.concatenate([r.astype(BF) for r in rows_of])

    up, down = joined(term[3], up, 0), joined(term[5], down, 1)
    gt_later = after(gt, up, down)
    up, down = ring(up, down)
    distances = (2, 6, 1, 7, 0)
    keys = [(k, s) for s in distances for k in (1, 0)]
    got = pl.pallas_call(
        functools.partial(terms_kernel, keys, part),
        out_shape=(double,) * len(distances),
        in_specs=[SMEM, VMEM] + [ANY] * 3,
        out_specs=(VMEM,) * len(distances),
        scratch_shapes=[
            pltpu.VMEM((2, 2 * rows, len(keys) * LANES), BF),
            pltpu.SemaphoreType.DMA((len(keys), 3)),
        ],
        compiler_params=params(20),
        cost_estimate=COST,
        name="terms",
    )(sc, gt_later, x_own, dy_own, xp)
    term.update(zip(distances, got))

    quarter = rows // NX

    def pair(i):
        rows_of = slice(i * quarter, (i + 1) * quarter)
        return keep[rows_of].astype(F32) + sent[rows_of].astype(F32)

    acc = px(pair(3).astype(BF), -1)

    up, down, acc = after_all(up, down, acc)
    up, down = (term[2].astype(F32) + up).astype(BF), (term[6].astype(F32) + down).astype(BF)
    up, down = ring(up, down)
    acc = px((pair(2) + acc).astype(BF), -1)

    acc = px((pair(1) + acc).astype(BF), -1)
    up, down, acc = after_all(up, down, acc)

    def last(k, up, down):
        rows_of = slice(k * n, (k + 1) * n)
        return (
            (term[1][rows_of].astype(F32) + up[rows_of]).astype(BF),
            (term[7][rows_of].astype(F32) + down[rows_of]).astype(BF),
        )

    p_in = last(0, up, down)
    p = ring(*p_in)
    acc = pair(0) + after(acc, *p_in)
    part_b = [acc[i * group : (i + 1) * group].astype(BF) for i in range(1, 4)]
    got = [pyh(part_b[0]), pyl(part_b[1]), pboth(part_b[2])]
    in_grad = (acc[:group] + got[0] + got[1] + got[2]).astype(BF).reshape(1, group, width)
    up, down, *_ = after_all(up, down, *got)
    o = ring(*last(1, up, down))
    sum_other = (term[0][:n].astype(F32) + p[0].astype(F32) + p[1].astype(F32)).astype(BF)
    o = after(tuple(o), sum_other)
    sum_other = pyl(sum_other)
    sum_own = (term[0][n:].astype(F32) + o[0].astype(F32) + o[1].astype(F32)).astype(BF)

    gate_grad, up_grad, down_grad = pl.pallas_call(
        functools.partial(join_kernel, part),
        out_shape=(jax.ShapeDtypeStruct((2 * part, LANES), BF),) * 3,
        in_specs=[SMEM, VMEM, VMEM],
        out_specs=(VMEM,) * 3,
        compiler_params=params(8),
        cost_estimate=COST,
        name="join",
    )(sc, sum_own, sum_other)
    return in_grad, gate_grad.T, up_grad.T, down_grad


def solution(mesh):
    placed = (P("dp", None, None), P("dp", None, None), P("dp", "mp"), P("dp", "mp"), P("mp", "dp"))
    return jax.shard_map(
        local,
        mesh=mesh,
        in_specs=placed,
        out_specs=(P("dp", "mp", None), P("dp", "mp"), P("dp", "mp"), P("mp", "dp")),
        check_vma=False,
    )
```

```python
import functools

import jax
import jax.numpy as jnp
from jax import lax
from jax.experimental import pallas as pl
from jax.experimental.pallas import tpu as pltpu
from jax.sharding import PartitionSpec as P

BF = jnp.bfloat16
F32 = jnp.float32
NX, NZ = 4, 8
LANES = 256
ANY = pl.BlockSpec(memory_space=pl.ANY)
HBM = pl.BlockSpec(memory_space=pltpu.HBM)
VMEM = pl.BlockSpec(memory_space=pltpu.VMEM)
COST = pl.CostEstimate(flops=1, bytes_accessed=1, transcendentals=0)
SMEM = pl.BlockSpec(memory_space=pltpu.SMEM)


def mm(left, right):
    return lax.dot_general(left, right, (((1,), (0,)), ((), ())), preferred_element_type=F32)


def mm_t(left, right):
    return lax.dot_general(left, right, (((1,), (1,)), ((), ())), preferred_element_type=F32)


def pz(value, step):
    pairs = [(y * NZ + z, y * NZ + (z + step) % NZ) for y in range(2) for z in range(NZ)]
    return lax.ppermute(value, "dp", pairs)


def pyl(value):
    return lax.ppermute(value, "dp", [(i, (i + NZ) % (2 * NZ)) for i in range(2 * NZ)])


def px(value, step):
    pairs = [
        (y * 8 + x * 2 + c, y * 8 + (x + (-step if c else step)) % NX * 2 + c)
        for y in range(2) for x in range(NX) for c in range(2)
    ]
    return lax.ppermute(value, "mp", pairs)


def pxs(value, step):
    pairs = [
        (y * 8 + x * 2 + c, y * 8 + (x + step) % NX * 2 + c)
        for y in range(2) for x in range(NX) for c in range(2)
    ]
    return lax.ppermute(value, "mp", pairs)


def pc(value):
    return lax.ppermute(value, "mp", [(i, i ^ 1) for i in range(16)])


def pyh(value):
    return lax.ppermute(value, "mp", [(i, i ^ 8) for i in range(16)])


def pboth(value):
    n = 2 * NZ
    pairs = [(m * n + d, (m ^ 8) * n + (d + NZ) % n) for m in range(16) for d in range(n)]
    return lax.ppermute(value, ("mp", "dp"), pairs)


def after(value, *others):
    return lax.optimization_barrier((value, *others))[0]


def after_all(*values):
    return lax.optimization_barrier(values)


def col_block(sc, k, s):
    yl = 1 - sc[1] if k else sc[1]
    return yl * NZ + lax.rem(sc[0] + s, NZ)


def offset(sc, k, s):
    return pl.multiple_of(col_block(sc, k, s) * LANES, LANES)


def spread(row, count, part):
    out, end = [], row + count
    while row < end:
        m = row // part
        n = min(end, (m + 1) * part) - row
        out.append((row, n, m * LANES + row - m * part))
        row += n
    return out


def load_chunks(where, places, part, refs, buf, sems):
    waits, sem = [], 0
    for parts, place in zip(where, places):
        mine = []
        for at, row, start, count in parts:
            for first, n, to in spread(start, count, part):
                copy = pltpu.make_async_copy(
                    refs[at].at[pl.ds(row + first - start, n)],
                    buf.at[pl.ds(to, n), pl.ds(place, LANES)],
                    sems.at[sem],
                )
                copy.start()
                mine.append(copy)
                sem += 1
        waits.append(mine)
    return waits


def copies_of(where, part):
    return sum(len(spread(start, count, part)) for parts in where for _, _, start, count in parts)


def clear_pad(buf, part):
    for m in range(3):
        buf[m * LANES + part : (m + 1) * LANES] = jnp.zeros((LANES - part, buf.shape[1]), BF)


def early_kernel(keys, missing, parts, n_pieces, piece_at, part, sc, x, dy, *refs):
    pieces, chunks = refs[:n_pieces], refs[n_pieces:-7]
    acc, xp, xs, buf, w_sems, x_sems, out_sem = refs[-7:]
    rows = x.shape[0]
    loads = [
        pltpu.make_async_copy(x, xs.at[0, pl.ds(0, rows)], x_sems.at[0]),
        pltpu.make_async_copy(dy, xs.at[1, pl.ds(0, rows)], x_sems.at[1]),
    ]
    row = rows
    pieces = [pieces[i].at[j] for i, j in piece_at]
    for i, piece in enumerate(pieces):
        n = piece.shape[1]
        loads.append(pltpu.make_async_copy(piece, xs.at[:, pl.ds(row, n)], x_sems.at[2 + i]))
        row += n
    for copy in loads:
        copy.start()
    waits = load_chunks(parts, [offset(sc, *key) for key in keys], part, chunks, buf, w_sems)
    clear_pad(buf, part)
    for key in missing:
        buf[:, pl.ds(offset(sc, *key), LANES)] = jnp.zeros((buf.shape[0], LANES), BF)
    for copy in loads:
        copy.wait()
    store = pltpu.make_async_copy(xs.at[:, pl.ds(rows, rows)], xp, out_sem)
    store.start()
    for mine in waits:
        for copy in mine:
            copy.wait()
    acc[:, : 2 * LANES] = mm_t(xs[0], buf[: 2 * LANES])
    acc[:, 2 * LANES :] = mm_t(xs[1], buf[2 * LANES :])
    store.wait()


def put_terms(outs, part, top, low):
    two, n = 2 * part, 3 * part
    top, low = top.astype(BF), low.astype(BF)
    for j, out in enumerate(outs):
        for k in range(2):
            cols = slice((2 * j + k) * LANES, (2 * j + k + 1) * LANES)
            out[k * n : k * n + two] = top[:, cols]
            out[k * n + two : (k + 1) * n] = low[:, cols]


def late_kernel(keys, parts, term_keys, part, sc, acc, x, dy, xp, *refs):
    n_out = 8 + len(term_keys) // 2
    chunks = refs[:-n_out]
    gt, dgu, *outs = refs[-n_out:-4]
    far, outs = outs[:2], outs[2:]
    rowbuf, xb, buf, x_sems = refs[-4:]
    rows = x.shape[0]
    loads = []
    for i, (k, s) in enumerate(keys + term_keys):
        cols, to = pl.ds(offset(sc, k, s), LANES), pl.ds(i * LANES, LANES)
        loads += [
            pltpu.make_async_copy(x.at[:, cols], xb.at[0, pl.ds(0, rows), to], x_sems.at[i, 0]),
            pltpu.make_async_copy(dy.at[:, cols], xb.at[1, pl.ds(0, rows), to], x_sems.at[i, 1]),
            pltpu.make_async_copy(xp.at[:, :, cols], xb.at[:, pl.ds(rows, rows), to], x_sems.at[i, 2]),
        ]
    for copy in loads:
        copy.start()
    clear_pad(buf, part)
    for i, pieces in enumerate(parts):
        for at, row, start, count in pieces:
            for first, n, to in spread(start, count, part):
                row_at = row + first - start
                buf[to : to + n, i * LANES : (i + 1) * LANES] = chunks[at][row_at : row_at + n]
    for copy in loads[: 3 * len(keys)]:
        copy.wait()
    used = len(keys) * LANES
    both = acc[:, : 2 * LANES] + mm_t(xb[0, :, :used], buf[: 2 * LANES])
    dhid = acc[:, 2 * LANES :] + mm_t(xb[1, :, :used], buf[2 * LANES :])
    gate, up_val = both[:, :LANES], both[:, LANES:]
    sig = 1.0 / (1.0 + jnp.exp(-gate))
    silu = gate * sig
    hidden = silu * up_val
    dup = dhid * silu
    dgate = dhid * up_val * sig * (1.0 + gate * (1.0 - sig))
    for m, value in enumerate((dgate, dup, hidden)):
        gt[m * part : (m + 1) * part] = value.T[:part].astype(BF)
    mid = 3 * part // 2
    two = 2 * part
    up, down = far
    for j in range(2):
        cols = slice(j * LANES, (j + 1) * LANES)
        top, low = mm(gt[:two], xb[0, :, cols]), mm(gt[two:], xb[1, :, cols])
        at = j * mid
        up[at : at + mid] = top[:mid].astype(BF)
        down[at : at + two - mid] = top[mid:].astype(BF)
        down[at + two - mid : at + mid] = low.astype(BF)
    for copy in loads[3 * len(keys) :]:
        copy.wait()
    put_terms(outs, part, mm(gt[:two], xb[0, :, used:]), mm(gt[two:], xb[1, :, used:]))
    group = rows // 16
    for m, value in enumerate((dgate, dup)):
        rowbuf[...] = value.astype(BF)
        for g in range(16):
            to = g // 2 * 4 * group + g % 2 * group
            at = pl.multiple_of(sc[2 + g] * group, group)
            dgu[m, to : to + group] = rowbuf[pl.ds(at, group)]
        for g in range(8):
            to = g * 4 * group + 2 * group
            at = pl.multiple_of(rows + sc[18 + g] * 2 * group, 2 * group)
            dgu[m, to : to + 2 * group] = rowbuf[pl.ds(at, 2 * group)]


def dx_kernel(keys, parts, part, sc, dgu, *refs):
    chunks, (keep, send, buf, w_sems) = refs[:-4], refs[-4:]
    rows = keep.shape[0]
    waits = load_chunks(parts, [offset(sc, *key) for key in keys], part, chunks, buf, w_sems)
    clear_pad(buf, part)
    for mine in waits:
        for copy in mine:
            copy.wait()
    step = 4 * LANES
    for at in range(0, keep.shape[1], step):
        cols = slice(at, at + step)
        dx = mm(dgu[0], buf[:LANES, cols]) + mm(dgu[1], buf[LANES : 2 * LANES, cols])
        keep[:, cols] = dx[:rows].astype(BF)
        send[:, cols] = dx[rows:].astype(BF)


def terms_kernel(keys, part, sc, gt, x, dy, xp, *refs):
    outs, (xb, x_sems) = refs[:-2], refs[-2:]
    rows = x.shape[0]
    loads = []
    for i, (k, s) in enumerate(keys):
        cols, to = pl.ds(offset(sc, k, s), LANES), pl.ds(i * LANES, LANES)
        mine = [
            pltpu.make_async_copy(x.at[:, cols], xb.at[0, pl.ds(0, rows), to], x_sems.at[i, 0]),
            pltpu.make_async_copy(dy.at[:, cols], xb.at[1, pl.ds(0, rows), to], x_sems.at[i, 1]),
            pltpu.make_async_copy(xp.at[:, :, cols], xb.at[:, pl.ds(rows, rows), to], x_sems.at[i, 2]),
        ]
        for copy in mine:
            copy.start()
        loads.append(mine)
    two = 2 * part
    for i in range(0, len(keys), 2):
        for copy in loads[i] + loads[i + 1]:
            copy.wait()
        cols = slice(i * LANES, (i + 2) * LANES)
        put_terms(outs[i // 2 : i // 2 + 1], part, mm(gt[:two], xb[0, :, cols]), mm(gt[two:], xb[1, :, cols]))


def join_kernel(part, sc, own, other, *outs):
    mine, theirs = pl.multiple_of(sc[1] * part, part), pl.multiple_of((1 - sc[1]) * part, part)
    for m, out in enumerate(outs):
        out[pl.ds(mine, part)] = own[m * part : (m + 1) * part]
        out[pl.ds(theirs, part)] = other[m * part : (m + 1) * part]


def params(mib):
    return pltpu.CompilerParams(vmem_limit_bytes=mib * 1024 * 1024)


def local(inputs, out_grad, w_gate, w_up, w_down):
    rows, width = inputs.shape[1:]
    part = w_down.shape[0] // 2
    dp, mp = lax.axis_index("dp"), lax.axis_index("mp")
    yl, z = dp // NZ, dp % NZ
    yh, x, c = mp // 8, mp // 2 % NX, mp % 2
    group = rows // 16
    x_own, dy_own = inputs[0], out_grad[0]

    slot = lax.iota(jnp.int32, 26)
    at = slot - 2
    dc, dx, dh = at // 8, at // 2 % NX, at % 2
    ordered = (yh ^ dh) * 8 + (x - (1 - 2 * (c ^ dc)) * dx + NX) % NX * 2 + (c ^ dc)
    at = slot - 18
    dc, dx = at // NX % 2, at % NX
    stands = dc * NX + (NX - (1 - 2 * (c ^ dc)) * dx) % NX
    sc = jnp.where(slot < 2, jnp.where(slot == 0, z, yl), jnp.where(slot < 18, ordered, stands)).astype(jnp.int32)

    u32 = jnp.uint32
    starts = [(yl * part).astype(u32), ((1 - yl) * part).astype(u32), (mp * group).astype(u32), ((mp ^ 8) * group).astype(u32)]
    w_gate, w_up, w_down, x_own, dy_own, sc, *starts = after_all(w_gate, w_up, w_down, x_own, dy_own, sc, *starts)

    def rows_from(array, start, count):
        return lax.dynamic_slice(array, (start, u32(0)), (count, array.shape[1]))

    own, other = (
        jnp.concatenate([rows_from(w, starts[i], part) for w in (w_gate.T, w_up.T, w_down)]) for i in range(2)
    )
    mid = own.shape[0] // 2

    def piece(array):
        return jnp.concatenate([rows_from(array, start, group) for start in starts[2:]])

    n = own.shape[0]
    up, down = pz(own, 1), pz(own, -1)
    other = pyl(other)
    chunks = {
        (0, 0): [(own, 0, 0, n)],
        (0, 7): [(up, 0, 0, n)],
        (0, 1): [(down, 0, 0, n)],
        (1, 0): [(other, 0, 0, n)],
    }
    first = jnp.stack([piece(after(x_own, own)), piece(after(dy_own, own))])
    first = pyl(first)
    up, down = jnp.concatenate([other, up]), jnp.concatenate([down, other])
    for step in (1, 2):
        up, down = pz(up, 1), pz(down, -1)
        chunks[1, NZ - step], chunks[0, NZ - step - 1] = [(up, 0, 0, n)], [(up, n, 0, n)]
        chunks[0, step + 1], chunks[1, step] = [(down, 0, 0, n)], [(down, n, 0, n)]
        if step == 1:
            left, right = pxs(first, 1), pxs(first, -1)
            left_s, right_s, first_s, _, _ = after_all(left, right, first, up, down)
            far_x, far_dy = pxs(left_s[0], 1), pxs(right_s[1], -1)
            swap = pc(jnp.stack([first_s, right_s, left_s]))
    up, down = up[: n + mid], down[mid:]
    far_x, far_dy, _, _ = after_all(far_x, far_dy, up, down)
    two_off = jnp.stack([far_x, far_dy])
    swap_two = pc(two_off)
    up, down = pz(up, 1), pz(down, -1)
    chunks[1, 5], chunks[1, 3] = [(up, 0, 0, n)], [(down, n - mid, 0, n)]
    chunks[0, 4] = [(up, n, 0, mid), (down, 0, mid, n - mid)]
    pieces = [first[None], right[None], two_off[None], left[None], swap, swap_two[None]]
    piece_at = [(0, 0), (1, 0), (2, 0), (3, 0), (4, 0), (4, 1), (5, 0), (4, 2)]

    late = [(1, 4), (0, 4), (1, 3), (1, 5)]
    early = [key for key in chunks if key not in late]

    def listed(keys):
        refs, where = [], []
        for key in keys:
            parts = []
            for array, *rest in chunks[key]:
                at = [i for i, a in enumerate(refs) if a is array]
                if not at:
                    refs.append(array)
                parts.append((at[0] if at else len(refs) - 1, *rest))
            where.append(tuple(parts))
        return tuple(where), refs

    parts, refs = listed(early)
    acc, xp = pl.pallas_call(
        functools.partial(early_kernel, early, late, parts, len(pieces), piece_at, part),
        out_shape=(
            jax.ShapeDtypeStruct((2 * rows, 3 * LANES), F32),
            jax.ShapeDtypeStruct((2, rows, width), BF),
        ),
        in_specs=[SMEM] + [HBM] * (2 + len(pieces) + len(refs)),
        out_specs=(VMEM, ANY),
        scratch_shapes=[
            pltpu.VMEM((2, 2 * rows, width), BF),
            pltpu.VMEM((3 * LANES, width), BF),
            pltpu.SemaphoreType.DMA((copies_of(parts, part),)),
            pltpu.SemaphoreType.DMA((2 + 2 * NX,)),
            pltpu.SemaphoreType.DMA,
        ],
        compiler_params=params(22),
        cost_estimate=COST,
        name="early",
    )(sc, x_own, dy_own, *pieces, *refs)

    up, down, acc, xp = after_all(up, down, acc, xp)
    up, down = pz(up[:mid], 1), pz(down[n:], -1)
    chunks[1, 4] = [(up, 0, 0, mid), (down, 0, mid, n - mid)]

    parts, refs = listed(late)
    full = jax.ShapeDtypeStruct((3 * part, LANES), BF)
    double = jax.ShapeDtypeStruct((6 * part, LANES), BF)
    late_terms = [(1, 3), (0, 3), (1, 5), (0, 5)]
    gt, dgu, *far = pl.pallas_call(
        functools.partial(late_kernel, late, parts, late_terms, part),
        out_shape=(
            jax.ShapeDtypeStruct((3 * part, 2 * rows), BF),
            jax.ShapeDtypeStruct((2, 2 * rows, LANES), BF),
            full, full, double, double,
        ),
        in_specs=[SMEM, VMEM] + [ANY] * 3 + [VMEM] * len(refs),
        out_specs=(VMEM,) * 6,
        scratch_shapes=[
            pltpu.VMEM((2 * rows, LANES), BF),
            pltpu.VMEM((2, 2 * rows, (len(late) + 4) * LANES), BF),
            pltpu.VMEM((3 * LANES, len(late) * LANES), BF),
            pltpu.SemaphoreType.DMA((len(late) + 4, 3)),
        ],
        compiler_params=params(22),
        cost_estimate=COST,
        name="late",
    )(sc, acc, x_own, dy_own, xp, *refs)
    far, got = far[:2], far[2:]

    term = dict(zip((3, 5), got))

    def ring(up, down):
        return pz(up, 1), pz(down, -1)

    up, down = ring(*far)

    keys = list(chunks)
    parts, refs = listed(keys)
    keep, send = pl.pallas_call(
        functools.partial(dx_kernel, keys, parts, part),
        out_shape=(jax.ShapeDtypeStruct((rows, width), BF),) * 2,
        in_specs=[SMEM, VMEM] + [HBM] * len(refs),
        out_specs=(VMEM, VMEM),
        scratch_shapes=[
            pltpu.VMEM((3 * LANES, width), BF),
            pltpu.SemaphoreType.DMA((copies_of(parts, part),)),
        ],
        compiler_params=params(20),
        cost_estimate=COST,
        name="dx",
    )(sc, dgu, *refs)

    up, down, send = after_all(up, down, send)
    sent = pc(send)

    def joined(whole, halves, first):
        rows_of = [whole[i * mid : (i + 1) * mid].astype(F32) for i in range(4)]
        for i in range(2):
            rows_of[2 * i + first] += halves[i * mid : (i + 1) * mid]
        return jnp.concatenate([r.astype(BF) for r in rows_of])

    up, down = joined(term[3], up, 0), joined(term[5], down, 1)
    gt_later = after(gt, up, down)
    up, down = ring(up, down)
    distances = (2, 6, 1, 7, 0)
    keys = [(k, s) for s in distances for k in (1, 0)]
    got = pl.pallas_call(
        functools.partial(terms_kernel, keys, part),
        out_shape=(double,) * len(distances),
        in_specs=[SMEM, VMEM] + [ANY] * 3,
        out_specs=(VMEM,) * len(distances),
        scratch_shapes=[
            pltpu.VMEM((2, 2 * rows, len(keys) * LANES), BF),
            pltpu.SemaphoreType.DMA((len(keys), 3)),
        ],
        compiler_params=params(20),
        cost_estimate=COST,
        name="terms",
    )(sc, gt_later, x_own, dy_own, xp)
    term.update(zip(distances, got))

    quarter = rows // NX

    def pair(i):
        rows_of = slice(i * quarter, (i + 1) * quarter)
        return keep[rows_of].astype(F32) + sent[rows_of].astype(F32)

    acc = px(pair(3).astype(BF), -1)

    up, down = after(up, acc), after(down, acc)
    up, down = (term[2].astype(F32) + up).astype(BF), (term[6].astype(F32) + down).astype(BF)
    up, down = ring(up, down)
    acc = px((pair(2) + acc).astype(BF), -1)

    acc = px((pair(1) + acc).astype(BF), -1)
    up, down = after(up, acc), after(down, acc)

    def last(k, up, down):
        rows_of = slice(k * n, (k + 1) * n)
        return (
            (term[1][rows_of].astype(F32) + up[rows_of]).astype(BF),
            (term[7][rows_of].astype(F32) + down[rows_of]).astype(BF),
        )

    p_in = last(0, up, down)
    p = ring(*p_in)
    acc = pair(0) + after(acc, *p_in)
    part_b = [acc[i * group : (i + 1) * group].astype(BF) for i in range(1, 4)]
    got = [pyh(part_b[0]), pyl(part_b[1]), pboth(part_b[2])]
    in_grad = (acc[:group] + got[0] + got[1] + got[2]).astype(BF).reshape(1, group, width)
    up, down, *_ = after_all(up, down, *got)
    o = ring(*last(1, up, down))
    sum_other = (term[0][:n].astype(F32) + p[0].astype(F32) + p[1].astype(F32)).astype(BF)
    o = after(tuple(o), sum_other)
    sum_other = pyl(sum_other)
    sum_own = (term[0][n:].astype(F32) + o[0].astype(F32) + o[1].astype(F32)).astype(BF)

    gate_grad, up_grad, down_grad = pl.pallas_call(
        functools.partial(join_kernel, part),
        out_shape=(jax.ShapeDtypeStruct((2 * part, LANES), BF),) * 3,
        in_specs=[SMEM, VMEM, VMEM],
        out_specs=(VMEM,) * 3,
        compiler_params=params(8),
        cost_estimate=COST,
        name="join",
    )(sc, sum_own, sum_other)
    return in_grad, gate_grad.T, up_grad.T, down_grad


def solution(mesh):
    placed = (P("dp", None, None), P("dp", None, None), P("dp", "mp"), P("dp", "mp"), P("mp", "dp"))
    return jax.shard_map(
        local,
        mesh=mesh,
        in_specs=placed,
        out_specs=(P("dp", "mp", None), P("dp", "mp"), P("dp", "mp"), P("mp", "dp")),
        check_vma=False,
    )
```

```python
import functools

import jax
import jax.numpy as jnp
from jax import lax
from jax.experimental import pallas as pl
from jax.experimental.pallas import tpu as pltpu
from jax.sharding import PartitionSpec as P

BF = jnp.bfloat16
F32 = jnp.float32
NX, NZ = 4, 8
LANES = 256
ANY = pl.BlockSpec(memory_space=pl.ANY)
HBM = pl.BlockSpec(memory_space=pltpu.HBM)
VMEM = pl.BlockSpec(memory_space=pltpu.VMEM)
COST = pl.CostEstimate(flops=1, bytes_accessed=1, transcendentals=0)
SMEM = pl.BlockSpec(memory_space=pltpu.SMEM)


def mm(left, right):
    return lax.dot_general(left, right, (((1,), (0,)), ((), ())), preferred_element_type=F32)


def mm_t(left, right):
    return lax.dot_general(left, right, (((1,), (1,)), ((), ())), preferred_element_type=F32)


def pz(value, step):
    pairs = [(y * NZ + z, y * NZ + (z + step) % NZ) for y in range(2) for z in range(NZ)]
    return lax.ppermute(value, "dp", pairs)


def pyl(value):
    return lax.ppermute(value, "dp", [(i, (i + NZ) % (2 * NZ)) for i in range(2 * NZ)])


def px(value, step):
    pairs = [
        (y * 8 + x * 2 + c, y * 8 + (x + (-step if c else step)) % NX * 2 + c)
        for y in range(2) for x in range(NX) for c in range(2)
    ]
    return lax.ppermute(value, "mp", pairs)


def pxs(value, step):
    pairs = [
        (y * 8 + x * 2 + c, y * 8 + (x + step) % NX * 2 + c)
        for y in range(2) for x in range(NX) for c in range(2)
    ]
    return lax.ppermute(value, "mp", pairs)


def pc(value):
    return lax.ppermute(value, "mp", [(i, i ^ 1) for i in range(16)])


def pyh(value):
    return lax.ppermute(value, "mp", [(i, i ^ 8) for i in range(16)])


def pboth(value):
    n = 2 * NZ
    pairs = [(m * n + d, (m ^ 8) * n + (d + NZ) % n) for m in range(16) for d in range(n)]
    return lax.ppermute(value, ("mp", "dp"), pairs)


def after(value, *others):
    return lax.optimization_barrier((value, *others))[0]


def after_all(*values):
    return lax.optimization_barrier(values)


def col_block(sc, k, s):
    yl = 1 - sc[1] if k else sc[1]
    return yl * NZ + lax.rem(sc[0] + s, NZ)


def offset(sc, k, s):
    return pl.multiple_of(col_block(sc, k, s) * LANES, LANES)


def spread(row, count, part):
    out, end = [], row + count
    while row < end:
        m = row // part
        n = min(end, (m + 1) * part) - row
        out.append((row, n, m * LANES + row - m * part))
        row += n
    return out


def load_chunks(where, places, part, refs, buf, sems):
    waits, sem = [], 0
    for parts, place in zip(where, places):
        mine = []
        for at, row, start, count in parts:
            for first, n, to in spread(start, count, part):
                copy = pltpu.make_async_copy(
                    refs[at].at[pl.ds(row + first - start, n)],
                    buf.at[pl.ds(to, n), pl.ds(place, LANES)],
                    sems.at[sem],
                )
                copy.start()
                mine.append(copy)
                sem += 1
        waits.append(mine)
    return waits


def copies_of(where, part):
    return sum(len(spread(start, count, part)) for parts in where for _, _, start, count in parts)


def clear_pad(buf, part):
    for m in range(3):
        buf[m * LANES + part : (m + 1) * LANES] = jnp.zeros((LANES - part, buf.shape[1]), BF)


def early_kernel(keys, missing, parts, n_pieces, piece_at, part, sc, x, dy, *refs):
    pieces, chunks = refs[:n_pieces], refs[n_pieces:-7]
    acc, xp, xs, buf, w_sems, x_sems, out_sem = refs[-7:]
    rows = x.shape[0]
    loads = [
        pltpu.make_async_copy(x, xs.at[0, pl.ds(0, rows)], x_sems.at[0]),
        pltpu.make_async_copy(dy, xs.at[1, pl.ds(0, rows)], x_sems.at[1]),
    ]
    row = rows
    pieces = [pieces[i].at[j] for i, j in piece_at]
    for i, piece in enumerate(pieces):
        n = piece.shape[1]
        loads.append(pltpu.make_async_copy(piece, xs.at[:, pl.ds(row, n)], x_sems.at[2 + i]))
        row += n
    for copy in loads:
        copy.start()
    waits = load_chunks(parts, [offset(sc, *key) for key in keys], part, chunks, buf, w_sems)
    clear_pad(buf, part)
    for key in missing:
        buf[:, pl.ds(offset(sc, *key), LANES)] = jnp.zeros((buf.shape[0], LANES), BF)
    for copy in loads:
        copy.wait()
    store = pltpu.make_async_copy(xs.at[:, pl.ds(rows, rows)], xp, out_sem)
    store.start()
    for mine in waits:
        for copy in mine:
            copy.wait()
    acc[:, : 2 * LANES] = mm_t(xs[0], buf[: 2 * LANES])
    acc[:, 2 * LANES :] = mm_t(xs[1], buf[2 * LANES :])
    store.wait()


def put_terms(outs, part, top, low):
    two, n = 2 * part, 3 * part
    top, low = top.astype(BF), low.astype(BF)
    for j, out in enumerate(outs):
        for k in range(2):
            cols = slice((2 * j + k) * LANES, (2 * j + k + 1) * LANES)
            out[k * n : k * n + two] = top[:, cols]
            out[k * n + two : (k + 1) * n] = low[:, cols]


def late_kernel(keys, parts, term_keys, part, sc, acc, x, dy, xp, *refs):
    n_out = 8 + len(term_keys) // 2
    chunks = refs[:-n_out]
    gt, dgu, *outs = refs[-n_out:-4]
    far, outs = outs[:2], outs[2:]
    rowbuf, xb, buf, x_sems = refs[-4:]
    rows = x.shape[0]
    loads = []
    for i, (k, s) in enumerate(keys + term_keys):
        cols, to = pl.ds(offset(sc, k, s), LANES), pl.ds(i * LANES, LANES)
        loads += [
            pltpu.make_async_copy(x.at[:, cols], xb.at[0, pl.ds(0, rows), to], x_sems.at[i, 0]),
            pltpu.make_async_copy(dy.at[:, cols], xb.at[1, pl.ds(0, rows), to], x_sems.at[i, 1]),
            pltpu.make_async_copy(xp.at[:, :, cols], xb.at[:, pl.ds(rows, rows), to], x_sems.at[i, 2]),
        ]
    for copy in loads:
        copy.start()
    clear_pad(buf, part)
    for i, pieces in enumerate(parts):
        for at, row, start, count in pieces:
            for first, n, to in spread(start, count, part):
                row_at = row + first - start
                buf[to : to + n, i * LANES : (i + 1) * LANES] = chunks[at][row_at : row_at + n]
    for copy in loads[: 3 * len(keys)]:
        copy.wait()
    used = len(keys) * LANES
    both = acc[:, : 2 * LANES] + mm_t(xb[0, :, :used], buf[: 2 * LANES])
    dhid = acc[:, 2 * LANES :] + mm_t(xb[1, :, :used], buf[2 * LANES :])
    gate, up_val = both[:, :LANES], both[:, LANES:]
    sig = 1.0 / (1.0 + jnp.exp(-gate))
    silu = gate * sig
    hidden = silu * up_val
    dup = dhid * silu
    dgate = dhid * up_val * sig * (1.0 + gate * (1.0 - sig))
    for m, value in enumerate((dgate, dup, hidden)):
        gt[m * part : (m + 1) * part] = value.T[:part].astype(BF)
    mid = 3 * part // 2
    two = 2 * part
    up, down = far
    for j in range(2):
        cols = slice(j * LANES, (j + 1) * LANES)
        top, low = mm(gt[:two], xb[0, :, cols]), mm(gt[two:], xb[1, :, cols])
        at = j * mid
        up[at : at + mid] = top[:mid].astype(BF)
        down[at : at + two - mid] = top[mid:].astype(BF)
        down[at + two - mid : at + mid] = low.astype(BF)
    for copy in loads[3 * len(keys) :]:
        copy.wait()
    put_terms(outs, part, mm(gt[:two], xb[0, :, used:]), mm(gt[two:], xb[1, :, used:]))
    group = rows // 16
    for m, value in enumerate((dgate, dup)):
        rowbuf[...] = value.astype(BF)
        for g in range(16):
            to = g // 2 * 4 * group + g % 2 * group
            at = pl.multiple_of(sc[2 + g] * group, group)
            dgu[m, to : to + group] = rowbuf[pl.ds(at, group)]
        for g in range(8):
            to = g * 4 * group + 2 * group
            at = pl.multiple_of(rows + sc[18 + g] * 2 * group, 2 * group)
            dgu[m, to : to + 2 * group] = rowbuf[pl.ds(at, 2 * group)]


def dx_kernel(keys, parts, part, sc, dgu, *refs):
    chunks, (keep, send, buf, w_sems) = refs[:-4], refs[-4:]
    rows = keep.shape[0]
    waits = load_chunks(parts, [offset(sc, *key) for key in keys], part, chunks, buf, w_sems)
    clear_pad(buf, part)
    for mine in waits:
        for copy in mine:
            copy.wait()
    step = 4 * LANES
    for at in range(0, keep.shape[1], step):
        cols = slice(at, at + step)
        dx = mm(dgu[0], buf[:LANES, cols]) + mm(dgu[1], buf[LANES : 2 * LANES, cols])
        keep[:, cols] = dx[:rows].astype(BF)
        send[:, cols] = dx[rows:].astype(BF)


def terms_kernel(keys, part, sc, gt, x, dy, xp, *refs):
    outs, (xb, x_sems) = refs[:-2], refs[-2:]
    rows = x.shape[0]
    loads = []
    for i, (k, s) in enumerate(keys):
        cols, to = pl.ds(offset(sc, k, s), LANES), pl.ds(i * LANES, LANES)
        mine = [
            pltpu.make_async_copy(x.at[:, cols], xb.at[0, pl.ds(0, rows), to], x_sems.at[i, 0]),
            pltpu.make_async_copy(dy.at[:, cols], xb.at[1, pl.ds(0, rows), to], x_sems.at[i, 1]),
            pltpu.make_async_copy(xp.at[:, :, cols], xb.at[:, pl.ds(rows, rows), to], x_sems.at[i, 2]),
        ]
        for copy in mine:
            copy.start()
        loads.append(mine)
    two = 2 * part
    for i in range(0, len(keys), 2):
        for copy in loads[i] + loads[i + 1]:
            copy.wait()
        cols = slice(i * LANES, (i + 2) * LANES)
        put_terms(outs[i // 2 : i // 2 + 1], part, mm(gt[:two], xb[0, :, cols]), mm(gt[two:], xb[1, :, cols]))


def join_kernel(part, sc, own, other, *outs):
    mine, theirs = pl.multiple_of(sc[1] * part, part), pl.multiple_of((1 - sc[1]) * part, part)
    for m, out in enumerate(outs):
        out[pl.ds(mine, part)] = own[m * part : (m + 1) * part]
        out[pl.ds(theirs, part)] = other[m * part : (m + 1) * part]


def params(mib):
    return pltpu.CompilerParams(vmem_limit_bytes=mib * 1024 * 1024)


def local(inputs, out_grad, w_gate, w_up, w_down):
    rows, width = inputs.shape[1:]
    part = w_down.shape[0] // 2
    dp, mp = lax.axis_index("dp"), lax.axis_index("mp")
    yl, z = dp // NZ, dp % NZ
    yh, x, c = mp // 8, mp // 2 % NX, mp % 2
    group = rows // 16
    x_own, dy_own = inputs[0], out_grad[0]

    slot = lax.iota(jnp.int32, 26)
    at = slot - 2
    dc, dx, dh = at // 8, at // 2 % NX, at % 2
    ordered = (yh ^ dh) * 8 + (x - (1 - 2 * (c ^ dc)) * dx + NX) % NX * 2 + (c ^ dc)
    at = slot - 18
    dc, dx = at // NX % 2, at % NX
    stands = dc * NX + (NX - (1 - 2 * (c ^ dc)) * dx) % NX
    sc = jnp.where(slot < 2, jnp.where(slot == 0, z, yl), jnp.where(slot < 18, ordered, stands)).astype(jnp.int32)

    u32 = jnp.uint32
    starts = [(yl * part).astype(u32), ((1 - yl) * part).astype(u32), (mp * group).astype(u32), ((mp ^ 8) * group).astype(u32)]
    w_gate, w_up, w_down, x_own, dy_own, sc, *starts = after_all(w_gate, w_up, w_down, x_own, dy_own, sc, *starts)

    def rows_from(array, start, count):
        return lax.dynamic_slice(array, (start, u32(0)), (count, array.shape[1]))

    own, other = (
        jnp.concatenate([rows_from(w, starts[i], part) for w in (w_gate.T, w_up.T, w_down)]) for i in range(2)
    )
    mid = own.shape[0] // 2

    def piece(array):
        return jnp.concatenate([rows_from(array, start, group) for start in starts[2:]])

    n = own.shape[0]
    up, down = pz(own, 1), pz(own, -1)
    other = pyl(other)
    chunks = {
        (0, 0): [(own, 0, 0, n)],
        (0, 7): [(up, 0, 0, n)],
        (0, 1): [(down, 0, 0, n)],
        (1, 0): [(other, 0, 0, n)],
    }
    first = jnp.stack([piece(after(x_own, own)), piece(after(dy_own, own))])
    first = pyl(first)
    up, down = jnp.concatenate([other, up]), jnp.concatenate([down, other])
    for step in (1, 2):
        up, down = pz(up, 1), pz(down, -1)
        chunks[1, NZ - step], chunks[0, NZ - step - 1] = [(up, 0, 0, n)], [(up, n, 0, n)]
        chunks[0, step + 1], chunks[1, step] = [(down, 0, 0, n)], [(down, n, 0, n)]
        if step == 1:
            left, right = pxs(first, 1), pxs(first, -1)
            left_s, right_s, first_s, _, _ = after_all(left, right, first, up, down)
            far_x, far_dy = pxs(left_s[0], 1), pxs(right_s[1], -1)
            swap = pc(jnp.stack([first_s, right_s, left_s]))
    up, down = up[: n + mid], down[mid:]
    far_x, far_dy, _, _ = after_all(far_x, far_dy, up, down)
    two_off = jnp.stack([far_x, far_dy])
    swap_two = pc(two_off)
    up, down = pz(up, 1), pz(down, -1)
    chunks[1, 5], chunks[1, 3] = [(up, 0, 0, n)], [(down, n - mid, 0, n)]
    chunks[0, 4] = [(up, n, 0, mid), (down, 0, mid, n - mid)]
    pieces = [first[None], right[None], two_off[None], left[None], swap, swap_two[None]]
    piece_at = [(0, 0), (1, 0), (2, 0), (3, 0), (4, 0), (4, 1), (5, 0), (4, 2)]

    late = [(1, 4), (0, 4), (1, 3), (1, 5)]
    early = [key for key in chunks if key not in late]

    def listed(keys):
        refs, where = [], []
        for key in keys:
            parts = []
            for array, *rest in chunks[key]:
                at = [i for i, a in enumerate(refs) if a is array]
                if not at:
                    refs.append(array)
                parts.append((at[0] if at else len(refs) - 1, *rest))
            where.append(tuple(parts))
        return tuple(where), refs

    parts, refs = listed(early)
    acc, xp = pl.pallas_call(
        functools.partial(early_kernel, early, late, parts, len(pieces), piece_at, part),
        out_shape=(
            jax.ShapeDtypeStruct((2 * rows, 3 * LANES), F32),
            jax.ShapeDtypeStruct((2, rows, width), BF),
        ),
        in_specs=[SMEM] + [HBM] * (2 + len(pieces) + len(refs)),
        out_specs=(VMEM, ANY),
        scratch_shapes=[
            pltpu.VMEM((2, 2 * rows, width), BF),
            pltpu.VMEM((3 * LANES, width), BF),
            pltpu.SemaphoreType.DMA((copies_of(parts, part),)),
            pltpu.SemaphoreType.DMA((2 + 2 * NX,)),
            pltpu.SemaphoreType.DMA,
        ],
        compiler_params=params(22),
        cost_estimate=COST,
        name="early",
    )(sc, x_own, dy_own, *pieces, *refs)

    up, down = after(up, acc, xp), after(down, acc, xp)
    up, down = pz(up[:mid], 1), pz(down[n:], -1)
    chunks[1, 4] = [(up, 0, 0, mid), (down, 0, mid, n - mid)]

    parts, refs = listed(late)
    full = jax.ShapeDtypeStruct((3 * part, LANES), BF)
    double = jax.ShapeDtypeStruct((6 * part, LANES), BF)
    late_terms = [(1, 3), (0, 3), (1, 5), (0, 5)]
    gt, dgu, *far = pl.pallas_call(
        functools.partial(late_kernel, late, parts, late_terms, part),
        out_shape=(
            jax.ShapeDtypeStruct((3 * part, 2 * rows), BF),
            jax.ShapeDtypeStruct((2, 2 * rows, LANES), BF),
            full, full, double, double,
        ),
        in_specs=[SMEM, VMEM] + [ANY] * 3 + [VMEM] * len(refs),
        out_specs=(VMEM,) * 6,
        scratch_shapes=[
            pltpu.VMEM((2 * rows, LANES), BF),
            pltpu.VMEM((2, 2 * rows, (len(late) + 4) * LANES), BF),
            pltpu.VMEM((3 * LANES, len(late) * LANES), BF),
            pltpu.SemaphoreType.DMA((len(late) + 4, 3)),
        ],
        compiler_params=params(22),
        cost_estimate=COST,
        name="late",
    )(sc, acc, x_own, dy_own, xp, *refs)
    far, got = far[:2], far[2:]

    term = dict(zip((3, 5), got))

    def ring(up, down):
        return pz(up, 1), pz(down, -1)

    up, down = ring(*far)

    keys = list(chunks)
    parts, refs = listed(keys)
    keep, send = pl.pallas_call(
        functools.partial(dx_kernel, keys, parts, part),
        out_shape=(jax.ShapeDtypeStruct((rows, width), BF),) * 2,
        in_specs=[SMEM, VMEM] + [HBM] * len(refs),
        out_specs=(VMEM, VMEM),
        scratch_shapes=[
            pltpu.VMEM((3 * LANES, width), BF),
            pltpu.SemaphoreType.DMA((copies_of(parts, part),)),
        ],
        compiler_params=params(20),
        cost_estimate=COST,
        name="dx",
    )(sc, dgu, *refs)

    up, down, send = after_all(up, down, send)
    sent = pc(send)

    def joined(whole, halves, k, first):
        whole, half = whole[k * n : (k + 1) * n].astype(F32), halves[k * mid : (k + 1) * mid]
        if first:
            return jnp.concatenate([whole[:mid], whole[mid:] + half]).astype(BF)
        return jnp.concatenate([whole[:mid] + half, whole[mid:]]).astype(BF)

    p_in, o_in = ((joined(term[3], up, k, 0), joined(term[5], down, k, 1)) for k in range(2))
    gt_later = after(gt, *p_in, *o_in)
    p, o = ring(*p_in), ring(*o_in)
    distances = (2, 6, 1, 7, 0)
    keys = [(k, s) for s in distances for k in (1, 0)]
    got = pl.pallas_call(
        functools.partial(terms_kernel, keys, part),
        out_shape=(double,) * len(distances),
        in_specs=[SMEM, VMEM] + [ANY] * 3,
        out_specs=(VMEM,) * len(distances),
        scratch_shapes=[
            pltpu.VMEM((2, 2 * rows, len(keys) * LANES), BF),
            pltpu.SemaphoreType.DMA((len(keys), 3)),
        ],
        compiler_params=params(20),
        cost_estimate=COST,
        name="terms",
    )(sc, gt_later, x_own, dy_own, xp)
    term.update(zip(distances, got))

    quarter = rows // NX

    def pair(i):
        rows_of = slice(i * quarter, (i + 1) * quarter)
        return keep[rows_of].astype(F32) + sent[rows_of].astype(F32)

    def add(k, s, up, down):
        rows_of = slice(k * n, (k + 1) * n)
        return (
            (term[s][rows_of].astype(F32) + up).astype(BF),
            (term[NZ - s][rows_of].astype(F32) + down).astype(BF),
        )

    acc = px(pair(3).astype(BF), -1)
    p_in = add(0, 2, *p)
    p = ring(*p_in)
    o_in = add(1, 2, *after(tuple(o), *p_in))
    o = ring(*o_in)
    acc = px((pair(2) + after(acc, *p_in)).astype(BF), -1)
    acc = px((pair(1) + after(acc, *o_in)).astype(BF), -1)
    p_in = add(0, 1, *p)
    p = ring(*p_in)
    o_in = add(1, 1, *after(tuple(o), *p_in))
    o = ring(*o_in)
    acc = pair(0) + after(acc, *p_in)
    part_b = [acc[i * group : (i + 1) * group].astype(BF) for i in range(1, 4)]
    sum_other = (term[0][:n].astype(F32) + p[0].astype(F32) + p[1].astype(F32)).astype(BF)
    *part_b, _ = after_all(*part_b, sum_other)
    got = [pyh(part_b[0]), pyl(part_b[1]), pboth(part_b[2])]
    in_grad = (acc[:group] + got[0] + got[1] + got[2]).astype(BF).reshape(1, group, width)
    o = after(tuple(o), sum_other, *part_b)
    sum_other = pyl(sum_other)
    sum_own = (term[0][n:].astype(F32) + o[0].astype(F32) + o[1].astype(F32)).astype(BF)

    gate_grad, up_grad, down_grad = pl.pallas_call(
        functools.partial(join_kernel, part),
        out_shape=(jax.ShapeDtypeStruct((2 * part, LANES), BF),) * 3,
        in_specs=[SMEM, VMEM, VMEM],
        out_specs=(VMEM,) * 3,
        compiler_params=params(8),
        cost_estimate=COST,
        name="join",
    )(sc, sum_own, sum_other)
    return in_grad, gate_grad.T, up_grad.T, down_grad


def solution(mesh):
    placed = (P("dp", None, None), P("dp", None, None), P("dp", "mp"), P("dp", "mp"), P("mp", "dp"))
    return jax.shard_map(
        local,
        mesh=mesh,
        in_specs=placed,
        out_specs=(P("dp", "mp", None), P("dp", "mp"), P("dp", "mp"), P("mp", "dp")),
        check_vma=False,
    )
```

```python
import functools

import jax
import jax.numpy as jnp
from jax import lax
from jax.experimental import pallas as pl
from jax.experimental.pallas import tpu as pltpu
from jax.sharding import PartitionSpec as P

BF = jnp.bfloat16
F32 = jnp.float32
NX, NZ = 4, 8
LANES = 256
ANY = pl.BlockSpec(memory_space=pl.ANY)
HBM = pl.BlockSpec(memory_space=pltpu.HBM)
VMEM = pl.BlockSpec(memory_space=pltpu.VMEM)
COST = pl.CostEstimate(flops=1, bytes_accessed=1, transcendentals=0)
SMEM = pl.BlockSpec(memory_space=pltpu.SMEM)


def mm(left, right):
    return lax.dot_general(left, right, (((1,), (0,)), ((), ())), preferred_element_type=F32)


def mm_t(left, right):
    return lax.dot_general(left, right, (((1,), (1,)), ((), ())), preferred_element_type=F32)


def pz(value, step):
    pairs = [(y * NZ + z, y * NZ + (z + step) % NZ) for y in range(2) for z in range(NZ)]
    return lax.ppermute(value, "dp", pairs)


def pyl(value):
    return lax.ppermute(value, "dp", [(i, (i + NZ) % (2 * NZ)) for i in range(2 * NZ)])


def px(value, step):
    pairs = [
        (y * 8 + x * 2 + c, y * 8 + (x + (-step if c else step)) % NX * 2 + c)
        for y in range(2) for x in range(NX) for c in range(2)
    ]
    return lax.ppermute(value, "mp", pairs)


def pxs(value, step):
    pairs = [
        (y * 8 + x * 2 + c, y * 8 + (x + step) % NX * 2 + c)
        for y in range(2) for x in range(NX) for c in range(2)
    ]
    return lax.ppermute(value, "mp", pairs)


def pc(value):
    return lax.ppermute(value, "mp", [(i, i ^ 1) for i in range(16)])


def pyh(value):
    return lax.ppermute(value, "mp", [(i, i ^ 8) for i in range(16)])


def pboth(value):
    n = 2 * NZ
    pairs = [(m * n + d, (m ^ 8) * n + (d + NZ) % n) for m in range(16) for d in range(n)]
    return lax.ppermute(value, ("mp", "dp"), pairs)


def after(value, *others):
    return lax.optimization_barrier((value, *others))[0]


def after_all(*values):
    return lax.optimization_barrier(values)


def col_block(sc, k, s):
    yl = 1 - sc[1] if k else sc[1]
    return yl * NZ + lax.rem(sc[0] + s, NZ)


def offset(sc, k, s):
    return pl.multiple_of(col_block(sc, k, s) * LANES, LANES)


def spread(row, count, part):
    out, end = [], row + count
    while row < end:
        m = row // part
        n = min(end, (m + 1) * part) - row
        out.append((row, n, m * LANES + row - m * part))
        row += n
    return out


def load_chunks(where, places, part, refs, buf, sems):
    waits, sem = [], 0
    for parts, place in zip(where, places):
        mine = []
        for at, row, start, count in parts:
            for first, n, to in spread(start, count, part):
                copy = pltpu.make_async_copy(
                    refs[at].at[pl.ds(row + first - start, n)],
                    buf.at[pl.ds(to, n), pl.ds(place, LANES)],
                    sems.at[sem],
                )
                copy.start()
                mine.append(copy)
                sem += 1
        waits.append(mine)
    return waits


def copies_of(where, part):
    return sum(len(spread(start, count, part)) for parts in where for _, _, start, count in parts)


def clear_pad(buf, part):
    for m in range(3):
        buf[m * LANES + part : (m + 1) * LANES] = jnp.zeros((LANES - part, buf.shape[1]), BF)


def early_kernel(keys, missing, parts, n_pieces, piece_at, part, sc, x, dy, *refs):
    pieces, chunks = refs[:n_pieces], refs[n_pieces:-7]
    acc, xp, xs, buf, w_sems, x_sems, out_sem = refs[-7:]
    rows = x.shape[0]
    loads = [
        pltpu.make_async_copy(x, xs.at[0, pl.ds(0, rows)], x_sems.at[0]),
        pltpu.make_async_copy(dy, xs.at[1, pl.ds(0, rows)], x_sems.at[1]),
    ]
    row = rows
    pieces = [pieces[i].at[j] for i, j in piece_at]
    for i, piece in enumerate(pieces):
        n = piece.shape[1]
        loads.append(pltpu.make_async_copy(piece, xs.at[:, pl.ds(row, n)], x_sems.at[2 + i]))
        row += n
    for copy in loads:
        copy.start()
    waits = load_chunks(parts, [offset(sc, *key) for key in keys], part, chunks, buf, w_sems)
    clear_pad(buf, part)
    for key in missing:
        buf[:, pl.ds(offset(sc, *key), LANES)] = jnp.zeros((buf.shape[0], LANES), BF)
    for copy in loads:
        copy.wait()
    store = pltpu.make_async_copy(xs.at[:, pl.ds(rows, rows)], xp, out_sem)
    store.start()
    for mine in waits:
        for copy in mine:
            copy.wait()
    acc[:, : 2 * LANES] = mm_t(xs[0], buf[: 2 * LANES])
    acc[:, 2 * LANES :] = mm_t(xs[1], buf[2 * LANES :])
    store.wait()


def put_terms(outs, part, top, low):
    two, n = 2 * part, 3 * part
    top, low = top.astype(BF), low.astype(BF)
    for j, out in enumerate(outs):
        for k in range(2):
            cols = slice((2 * j + k) * LANES, (2 * j + k + 1) * LANES)
            out[k * n : k * n + two] = top[:, cols]
            out[k * n + two : (k + 1) * n] = low[:, cols]


def late_kernel(keys, parts, part, sc, acc, x, dy, xp, *refs):
    chunks = refs[:-8]
    gt, dgu, *far = refs[-8:-4]
    rowbuf, xb, buf, x_sems = refs[-4:]
    rows = x.shape[0]
    loads = []
    for i, (k, s) in enumerate(keys):
        cols, to = pl.ds(offset(sc, k, s), LANES), pl.ds(i * LANES, LANES)
        loads += [
            pltpu.make_async_copy(x.at[:, cols], xb.at[0, pl.ds(0, rows), to], x_sems.at[i, 0]),
            pltpu.make_async_copy(dy.at[:, cols], xb.at[1, pl.ds(0, rows), to], x_sems.at[i, 1]),
            pltpu.make_async_copy(xp.at[:, :, cols], xb.at[:, pl.ds(rows, rows), to], x_sems.at[i, 2]),
        ]
    for copy in loads:
        copy.start()
    clear_pad(buf, part)
    for i, pieces in enumerate(parts):
        for at, row, start, count in pieces:
            for first, n, to in spread(start, count, part):
                row_at = row + first - start
                buf[to : to + n, i * LANES : (i + 1) * LANES] = chunks[at][row_at : row_at + n]
    for copy in loads:
        copy.wait()
    both = acc[:, : 2 * LANES] + mm_t(xb[0], buf[: 2 * LANES])
    dhid = acc[:, 2 * LANES :] + mm_t(xb[1], buf[2 * LANES :])
    gate, up_val = both[:, :LANES], both[:, LANES:]
    sig = 1.0 / (1.0 + jnp.exp(-gate))
    silu = gate * sig
    hidden = silu * up_val
    dup = dhid * silu
    dgate = dhid * up_val * sig * (1.0 + gate * (1.0 - sig))
    for m, value in enumerate((dgate, dup, hidden)):
        gt[m * part : (m + 1) * part] = value.T[:part].astype(BF)
    mid = 3 * part // 2
    two = 2 * part
    up, down = far
    for j in range(2):
        cols = slice(j * LANES, (j + 1) * LANES)
        top, low = mm(gt[:two], xb[0, :, cols]), mm(gt[two:], xb[1, :, cols])
        at = j * mid
        up[at : at + mid] = top[:mid].astype(BF)
        down[at : at + two - mid] = top[mid:].astype(BF)
        down[at + two - mid : at + mid] = low.astype(BF)
    group = rows // 16
    for m, value in enumerate((dgate, dup)):
        rowbuf[...] = value.astype(BF)
        for g in range(16):
            to = g // 2 * 4 * group + g % 2 * group
            at = pl.multiple_of(sc[2 + g] * group, group)
            dgu[m, to : to + group] = rowbuf[pl.ds(at, group)]
        for g in range(8):
            to = g * 4 * group + 2 * group
            at = pl.multiple_of(rows + sc[18 + g] * 2 * group, 2 * group)
            dgu[m, to : to + 2 * group] = rowbuf[pl.ds(at, 2 * group)]


def load_blocks(keys, sc, x, dy, xp, xb, sems):
    rows, loads = x.shape[0], []
    for i, (k, s) in enumerate(keys):
        cols, to = pl.ds(offset(sc, k, s), LANES), pl.ds(i * LANES, LANES)
        mine = [
            pltpu.make_async_copy(x.at[:, cols], xb.at[0, pl.ds(0, rows), to], sems.at[i, 0]),
            pltpu.make_async_copy(dy.at[:, cols], xb.at[1, pl.ds(0, rows), to], sems.at[i, 1]),
            pltpu.make_async_copy(xp.at[:, :, cols], xb.at[:, pl.ds(rows, rows), to], sems.at[i, 2]),
        ]
        for copy in mine:
            copy.start()
        loads.append(mine)
    return loads


def dx_kernel(keys, parts, term_keys, part, sc, dgu, gt, x, dy, xp, *refs):
    chunks, (keep, send, *outs), (buf, xb, w_sems, x_sems) = refs[:-8], refs[-8:-4], refs[-4:]
    rows, two = keep.shape[0], 2 * part
    loads = load_blocks(term_keys, sc, x, dy, xp, xb, x_sems)
    waits = load_chunks(parts, [offset(sc, *key) for key in keys], part, chunks, buf, w_sems)
    for mine in loads:
        for copy in mine:
            copy.wait()
    put_terms(outs, part, mm(gt[:two], xb[0]), mm(gt[two:], xb[1]))
    clear_pad(buf, part)
    for mine in waits:
        for copy in mine:
            copy.wait()
    step = 4 * LANES
    for at in range(0, keep.shape[1], step):
        cols = slice(at, at + step)
        dx = mm(dgu[0], buf[:LANES, cols]) + mm(dgu[1], buf[LANES : 2 * LANES, cols])
        keep[:, cols] = dx[:rows].astype(BF)
        send[:, cols] = dx[rows:].astype(BF)


def terms_kernel(keys, part, sc, gt, x, dy, xp, *refs):
    outs, (xb, x_sems) = refs[:-2], refs[-2:]
    rows = x.shape[0]
    loads = load_blocks(keys, sc, x, dy, xp, xb, x_sems)
    two = 2 * part
    for i in range(0, len(keys), 2):
        for copy in loads[i] + loads[i + 1]:
            copy.wait()
        cols = slice(i * LANES, (i + 2) * LANES)
        put_terms(outs[i // 2 : i // 2 + 1], part, mm(gt[:two], xb[0, :, cols]), mm(gt[two:], xb[1, :, cols]))


def join_kernel(part, sc, own, other, *outs):
    mine, theirs = pl.multiple_of(sc[1] * part, part), pl.multiple_of((1 - sc[1]) * part, part)
    for m, out in enumerate(outs):
        out[pl.ds(mine, part)] = own[m * part : (m + 1) * part]
        out[pl.ds(theirs, part)] = other[m * part : (m + 1) * part]


def params(mib):
    return pltpu.CompilerParams(vmem_limit_bytes=mib * 1024 * 1024)


def local(inputs, out_grad, w_gate, w_up, w_down):
    rows, width = inputs.shape[1:]
    part = w_down.shape[0] // 2
    dp, mp = lax.axis_index("dp"), lax.axis_index("mp")
    yl, z = dp // NZ, dp % NZ
    yh, x, c = mp // 8, mp // 2 % NX, mp % 2
    group = rows // 16
    x_own, dy_own = inputs[0], out_grad[0]

    slot = lax.iota(jnp.int32, 26)
    at = slot - 2
    dc, dx, dh = at // 8, at // 2 % NX, at % 2
    ordered = (yh ^ dh) * 8 + (x - (1 - 2 * (c ^ dc)) * dx + NX) % NX * 2 + (c ^ dc)
    at = slot - 18
    dc, dx = at // NX % 2, at % NX
    stands = dc * NX + (NX - (1 - 2 * (c ^ dc)) * dx) % NX
    sc = jnp.where(slot < 2, jnp.where(slot == 0, z, yl), jnp.where(slot < 18, ordered, stands)).astype(jnp.int32)

    u32 = jnp.uint32
    starts = [(yl * part).astype(u32), ((1 - yl) * part).astype(u32), (mp * group).astype(u32), ((mp ^ 8) * group).astype(u32)]
    w_gate, w_up, w_down, x_own, dy_own, sc, *starts = after_all(w_gate, w_up, w_down, x_own, dy_own, sc, *starts)

    def rows_from(array, start, count):
        return lax.dynamic_slice(array, (start, u32(0)), (count, array.shape[1]))

    stacked = jnp.stack([w_gate.T, w_up.T, w_down])
    own, other = (
        lax.dynamic_slice(stacked, (u32(0), starts[i], u32(0)), (3, part, LANES)).reshape(3 * part, LANES)
        for i in range(2)
    )
    mid = own.shape[0] // 2

    def piece(array):
        return jnp.concatenate([rows_from(array, start, group) for start in starts[2:]])

    n = own.shape[0]
    up, down = pz(own, 1), pz(own, -1)
    other = pyl(other)
    chunks = {
        (0, 0): [(own, 0, 0, n)],
        (0, 7): [(up, 0, 0, n)],
        (0, 1): [(down, 0, 0, n)],
        (1, 0): [(other, 0, 0, n)],
    }
    first = jnp.stack([piece(after(x_own, own)), piece(after(dy_own, own))])
    first = pyl(first)
    up, down = jnp.concatenate([other, up]), jnp.concatenate([down, other])
    for step in (1, 2):
        up, down = pz(up, 1), pz(down, -1)
        chunks[1, NZ - step], chunks[0, NZ - step - 1] = [(up, 0, 0, n)], [(up, n, 0, n)]
        chunks[0, step + 1], chunks[1, step] = [(down, 0, 0, n)], [(down, n, 0, n)]
        if step == 1:
            left, right = pxs(first, 1), pxs(first, -1)
            left_s, right_s, first_s, _, _ = after_all(left, right, first, up, down)
            far_x, far_dy = pxs(left_s[0], 1), pxs(right_s[1], -1)
            swap = pc(jnp.stack([first_s, right_s, left_s]))
    up, down = up[: n + mid], down[mid:]
    far_x, far_dy, _, _ = after_all(far_x, far_dy, up, down)
    two_off = jnp.stack([far_x, far_dy])
    swap_two = pc(two_off)
    up, down = pz(up, 1), pz(down, -1)
    chunks[1, 5], chunks[1, 3] = [(up, 0, 0, n)], [(down, n - mid, 0, n)]
    chunks[0, 4] = [(up, n, 0, mid), (down, 0, mid, n - mid)]
    pieces = [first[None], right[None], two_off[None], left[None], swap, swap_two[None]]
    piece_at = [(0, 0), (1, 0), (2, 0), (3, 0), (4, 0), (4, 1), (5, 0), (4, 2)]

    late = [(1, 4), (0, 4), (1, 3), (1, 5)]
    early = [key for key in chunks if key not in late]

    def listed(keys):
        refs, where = [], []
        for key in keys:
            parts = []
            for array, *rest in chunks[key]:
                at = [i for i, a in enumerate(refs) if a is array]
                if not at:
                    refs.append(array)
                parts.append((at[0] if at else len(refs) - 1, *rest))
            where.append(tuple(parts))
        return tuple(where), refs

    parts, refs = listed(early)
    acc, xp = pl.pallas_call(
        functools.partial(early_kernel, early, late, parts, len(pieces), piece_at, part),
        out_shape=(
            jax.ShapeDtypeStruct((2 * rows, 3 * LANES), F32),
            jax.ShapeDtypeStruct((2, rows, width), BF),
        ),
        in_specs=[SMEM] + [HBM] * (2 + len(pieces) + len(refs)),
        out_specs=(VMEM, ANY),
        scratch_shapes=[
            pltpu.VMEM((2, 2 * rows, width), BF),
            pltpu.VMEM((3 * LANES, width), BF),
            pltpu.SemaphoreType.DMA((copies_of(parts, part),)),
            pltpu.SemaphoreType.DMA((2 + 2 * NX,)),
            pltpu.SemaphoreType.DMA,
        ],
        compiler_params=params(22),
        cost_estimate=COST,
        name="early",
    )(sc, x_own, dy_own, *pieces, *refs)

    up, down = after(up, acc, xp), after(down, acc, xp)
    up, down = pz(up[:mid], 1), pz(down[n:], -1)
    chunks[1, 4] = [(up, 0, 0, mid), (down, 0, mid, n - mid)]

    parts, refs = listed(late)
    full = jax.ShapeDtypeStruct((3 * part, LANES), BF)
    double = jax.ShapeDtypeStruct((6 * part, LANES), BF)
    late_terms = [(1, 3), (0, 3), (1, 5), (0, 5)]
    gt, dgu, *far = pl.pallas_call(
        functools.partial(late_kernel, late, parts, part),
        out_shape=(
            jax.ShapeDtypeStruct((3 * part, 2 * rows), BF),
            jax.ShapeDtypeStruct((2, 2 * rows, LANES), BF),
            full, full,
        ),
        in_specs=[SMEM, VMEM] + [ANY] * 3 + [VMEM] * len(refs),
        out_specs=(VMEM,) * 4,
        scratch_shapes=[
            pltpu.VMEM((2 * rows, LANES), BF),
            pltpu.VMEM((2, 2 * rows, len(late) * LANES), BF),
            pltpu.VMEM((3 * LANES, len(late) * LANES), BF),
            pltpu.SemaphoreType.DMA((len(late), 3)),
        ],
        compiler_params=params(22),
        cost_estimate=COST,
        name="late",
    )(sc, acc, x_own, dy_own, xp, *refs)


    def ring(up, down):
        return pz(up, 1), pz(down, -1)

    up, down = ring(*far)

    keys = list(chunks)
    parts, refs = listed(keys)
    keep, send, *got = pl.pallas_call(
        functools.partial(dx_kernel, keys, parts, late_terms, part),
        out_shape=(jax.ShapeDtypeStruct((rows, width), BF),) * 2 + (double,) * 2,
        in_specs=[SMEM, VMEM, VMEM] + [ANY] * 3 + [HBM] * len(refs),
        out_specs=(VMEM,) * 4,
        scratch_shapes=[
            pltpu.VMEM((3 * LANES, width), BF),
            pltpu.VMEM((2, 2 * rows, 4 * LANES), BF),
            pltpu.SemaphoreType.DMA((copies_of(parts, part),)),
            pltpu.SemaphoreType.DMA((4, 3)),
        ],
        compiler_params=params(24),
        cost_estimate=COST,
        name="dx",
    )(sc, dgu, gt, x_own, dy_own, xp, *refs)
    term = dict(zip((3, 5), got))

    up, down, send = after_all(up, down, send)
    sent = pc(send)

    def joined(whole, halves, k, first):
        whole, half = whole[k * n : (k + 1) * n].astype(F32), halves[k * mid : (k + 1) * mid]
        if first:
            return jnp.concatenate([whole[:mid], whole[mid:] + half]).astype(BF)
        return jnp.concatenate([whole[:mid] + half, whole[mid:]]).astype(BF)

    p_in, o_in = ((joined(term[3], up, k, 0), joined(term[5], down, k, 1)) for k in range(2))
    gt_later = after(gt, *p_in, *o_in)
    p, o = ring(*p_in), ring(*o_in)
    distances = (2, 6, 1, 7, 0)
    keys = [(k, s) for s in distances for k in (1, 0)]
    got = pl.pallas_call(
        functools.partial(terms_kernel, keys, part),
        out_shape=(double,) * len(distances),
        in_specs=[SMEM, VMEM] + [ANY] * 3,
        out_specs=(VMEM,) * len(distances),
        scratch_shapes=[
            pltpu.VMEM((2, 2 * rows, len(keys) * LANES), BF),
            pltpu.SemaphoreType.DMA((len(keys), 3)),
        ],
        compiler_params=params(20),
        cost_estimate=COST,
        name="terms",
    )(sc, gt_later, x_own, dy_own, xp)
    term.update(zip(distances, got))

    quarter = rows // NX

    def pair(i):
        rows_of = slice(i * quarter, (i + 1) * quarter)
        return keep[rows_of].astype(F32) + sent[rows_of].astype(F32)

    def add(k, s, up, down):
        rows_of = slice(k * n, (k + 1) * n)
        return (
            (term[s][rows_of].astype(F32) + up).astype(BF),
            (term[NZ - s][rows_of].astype(F32) + down).astype(BF),
        )

    acc = px(pair(3).astype(BF), -1)
    p_in = add(0, 2, *p)
    p = ring(*p_in)
    o_in = add(1, 2, *after(tuple(o), *p_in))
    o = ring(*o_in)
    acc = px((pair(2) + after(acc, *p_in)).astype(BF), -1)
    acc = px((pair(1) + after(acc, *o_in)).astype(BF), -1)
    p_in = add(0, 1, *p)
    p = ring(*p_in)
    o_in = add(1, 1, *after(tuple(o), *p_in))
    o = ring(*o_in)
    acc = pair(0) + after(acc, *p_in)
    part_b = [acc[i * group : (i + 1) * group].astype(BF) for i in range(1, 4)]
    sum_other = (term[0][:n].astype(F32) + p[0].astype(F32) + p[1].astype(F32)).astype(BF)
    *part_b, _ = after_all(*part_b, sum_other)
    got = [pyh(part_b[0]), pyl(part_b[1]), pboth(part_b[2])]
    in_grad = (acc[:group] + got[0] + got[1] + got[2]).astype(BF).reshape(1, group, width)
    o = after(tuple(o), sum_other, *part_b)
    sum_other = pyl(sum_other)
    sum_own = (term[0][n:].astype(F32) + o[0].astype(F32) + o[1].astype(F32)).astype(BF)

    gate_grad, up_grad, down_grad = pl.pallas_call(
        functools.partial(join_kernel, part),
        out_shape=(jax.ShapeDtypeStruct((2 * part, LANES), BF),) * 3,
        in_specs=[SMEM, VMEM, VMEM],
        out_specs=(VMEM,) * 3,
        compiler_params=params(8),
        cost_estimate=COST,
        name="join",
    )(sc, sum_own, sum_other)
    return in_grad, gate_grad.T, up_grad.T, down_grad


def solution(mesh):
    placed = (P("dp", None, None), P("dp", None, None), P("dp", "mp"), P("dp", "mp"), P("mp", "dp"))
    return jax.shard_map(
        local,
        mesh=mesh,
        in_specs=placed,
        out_specs=(P("dp", "mp", None), P("dp", "mp"), P("dp", "mp"), P("mp", "dp")),
        check_vma=False,
    )
```

```python
import functools

import jax
import jax.numpy as jnp
from jax import lax
from jax.experimental import pallas as pl
from jax.experimental.pallas import tpu as pltpu
from jax.sharding import PartitionSpec as P

BF = jnp.bfloat16
F32 = jnp.float32
NX, NZ = 4, 8
LANES = 256
ANY = pl.BlockSpec(memory_space=pl.ANY)
HBM = pl.BlockSpec(memory_space=pltpu.HBM)
VMEM = pl.BlockSpec(memory_space=pltpu.VMEM)
COST = pl.CostEstimate(flops=1, bytes_accessed=1, transcendentals=0)
SMEM = pl.BlockSpec(memory_space=pltpu.SMEM)


def mm(left, right):
    return lax.dot_general(left, right, (((1,), (0,)), ((), ())), preferred_element_type=F32)


def mm_t(left, right):
    return lax.dot_general(left, right, (((1,), (1,)), ((), ())), preferred_element_type=F32)


def pz(value, step):
    pairs = [(y * NZ + z, y * NZ + (z + step) % NZ) for y in range(2) for z in range(NZ)]
    return lax.ppermute(value, "dp", pairs)


def pyl(value):
    return lax.ppermute(value, "dp", [(i, (i + NZ) % (2 * NZ)) for i in range(2 * NZ)])


def px(value, step):
    pairs = [
        (y * 8 + x * 2 + c, y * 8 + (x + (-step if c else step)) % NX * 2 + c)
        for y in range(2) for x in range(NX) for c in range(2)
    ]
    return lax.ppermute(value, "mp", pairs)


def pxs(value, step):
    pairs = [
        (y * 8 + x * 2 + c, y * 8 + (x + step) % NX * 2 + c)
        for y in range(2) for x in range(NX) for c in range(2)
    ]
    return lax.ppermute(value, "mp", pairs)


def pc(value):
    return lax.ppermute(value, "mp", [(i, i ^ 1) for i in range(16)])


def pyh(value):
    return lax.ppermute(value, "mp", [(i, i ^ 8) for i in range(16)])


def pboth(value):
    n = 2 * NZ
    pairs = [(m * n + d, (m ^ 8) * n + (d + NZ) % n) for m in range(16) for d in range(n)]
    return lax.ppermute(value, ("mp", "dp"), pairs)


def after(value, *others):
    return lax.optimization_barrier((value, *others))[0]


def after_all(*values):
    return lax.optimization_barrier(values)


def col_block(sc, k, s):
    yl = 1 - sc[1] if k else sc[1]
    return yl * NZ + lax.rem(sc[0] + s, NZ)


def offset(sc, k, s):
    return pl.multiple_of(col_block(sc, k, s) * LANES, LANES)


def spread(row, count, part):
    out, end = [], row + count
    while row < end:
        m = row // part
        n = min(end, (m + 1) * part) - row
        out.append((row, n, m * LANES + row - m * part))
        row += n
    return out


def load_chunks(where, places, part, refs, buf, sems):
    waits, sem = [], 0
    for parts, place in zip(where, places):
        mine = []
        for at, row, start, count in parts:
            for first, n, to in spread(start, count, part):
                copy = pltpu.make_async_copy(
                    refs[at].at[pl.ds(row + first - start, n)],
                    buf.at[pl.ds(to, n), pl.ds(place, LANES)],
                    sems.at[sem],
                )
                copy.start()
                mine.append(copy)
                sem += 1
        waits.append(mine)
    return waits


def copies_of(where, part):
    return sum(len(spread(start, count, part)) for parts in where for _, _, start, count in parts)


def clear_pad(buf, part):
    for m in range(3):
        buf[m * LANES + part : (m + 1) * LANES] = jnp.zeros((LANES - part, buf.shape[1]), BF)


def early_kernel(keys, missing, parts, n_pieces, piece_at, part, sc, x, dy, *refs):
    pieces, chunks, (acc, xp, buf, w_sems) = refs[:n_pieces], refs[n_pieces:-4], refs[-4:]
    rows = x.shape[0]
    waits = load_chunks(parts, [offset(sc, *key) for key in keys], part, chunks, buf, w_sems)
    clear_pad(buf, part)
    for key in missing:
        buf[:, pl.ds(offset(sc, *key), LANES)] = jnp.zeros((buf.shape[0], LANES), BF)
    row = 0
    for i, j in piece_at:
        count = pieces[i].shape[2]
        xp[:, row : row + count] = pieces[i][j]
        row += count
    for mine in waits:
        for copy in mine:
            copy.wait()
    both, down = buf[: 2 * LANES], buf[2 * LANES :]
    acc[:rows, : 2 * LANES] = mm_t(x[...], both)
    acc[rows:, : 2 * LANES] = mm_t(xp[0], both)
    acc[:rows, 2 * LANES :] = mm_t(dy[...], down)
    acc[rows:, 2 * LANES :] = mm_t(xp[1], down)


def put_terms(outs, part, top, low):
    two, n = 2 * part, 3 * part
    top, low = top.astype(BF), low.astype(BF)
    for j, out in enumerate(outs):
        for k in range(2):
            cols = slice((2 * j + k) * LANES, (2 * j + k + 1) * LANES)
            out[k * n : k * n + two] = top[:, cols]
            out[k * n + two : (k + 1) * n] = low[:, cols]


def late_kernel(keys, parts, part, sc, acc, x, dy, xp, *refs):
    chunks = refs[:-8]
    gt, dgu, *far = refs[-8:-4]
    rowbuf, xb, buf, x_sems = refs[-4:]
    rows = x.shape[0]
    loads = []
    for i, (k, s) in enumerate(keys):
        cols, to = pl.ds(offset(sc, k, s), LANES), pl.ds(i * LANES, LANES)
        loads += [
            pltpu.make_async_copy(x.at[:, cols], xb.at[0, pl.ds(0, rows), to], x_sems.at[i, 0]),
            pltpu.make_async_copy(dy.at[:, cols], xb.at[1, pl.ds(0, rows), to], x_sems.at[i, 1]),
            pltpu.make_async_copy(xp.at[:, :, cols], xb.at[:, pl.ds(rows, rows), to], x_sems.at[i, 2]),
        ]
    for copy in loads:
        copy.start()
    clear_pad(buf, part)
    for i, pieces in enumerate(parts):
        for at, row, start, count in pieces:
            for first, n, to in spread(start, count, part):
                row_at = row + first - start
                buf[to : to + n, i * LANES : (i + 1) * LANES] = chunks[at][row_at : row_at + n]
    for copy in loads:
        copy.wait()
    both = acc[:, : 2 * LANES] + mm_t(xb[0], buf[: 2 * LANES])
    dhid = acc[:, 2 * LANES :] + mm_t(xb[1], buf[2 * LANES :])
    gate, up_val = both[:, :LANES], both[:, LANES:]
    sig = 1.0 / (1.0 + jnp.exp(-gate))
    silu = gate * sig
    hidden = silu * up_val
    dup = dhid * silu
    dgate = dhid * up_val * sig * (1.0 + gate * (1.0 - sig))
    for m, value in enumerate((dgate, dup, hidden)):
        gt[m * part : (m + 1) * part] = value.T[:part].astype(BF)
    mid = 3 * part // 2
    two = 2 * part
    up, down = far
    for j in range(2):
        cols = slice(j * LANES, (j + 1) * LANES)
        top, low = mm(gt[:two], xb[0, :, cols]), mm(gt[two:], xb[1, :, cols])
        at = j * mid
        up[at : at + mid] = top[:mid].astype(BF)
        down[at : at + two - mid] = top[mid:].astype(BF)
        down[at + two - mid : at + mid] = low.astype(BF)
    group = rows // 16
    for m, value in enumerate((dgate, dup)):
        rowbuf[...] = value.astype(BF)
        for g in range(16):
            to = g // 2 * 4 * group + g % 2 * group
            at = pl.multiple_of(sc[2 + g] * group, group)
            dgu[m, to : to + group] = rowbuf[pl.ds(at, group)]
        for g in range(8):
            to = g * 4 * group + 2 * group
            at = pl.multiple_of(rows + sc[18 + g] * 2 * group, 2 * group)
            dgu[m, to : to + 2 * group] = rowbuf[pl.ds(at, 2 * group)]


def load_blocks(keys, sc, x, dy, xp, xb, sems):
    rows, loads = x.shape[0], []
    for i, (k, s) in enumerate(keys):
        cols, to = pl.ds(offset(sc, k, s), LANES), pl.ds(i * LANES, LANES)
        mine = [
            pltpu.make_async_copy(x.at[:, cols], xb.at[0, pl.ds(0, rows), to], sems.at[i, 0]),
            pltpu.make_async_copy(dy.at[:, cols], xb.at[1, pl.ds(0, rows), to], sems.at[i, 1]),
            pltpu.make_async_copy(xp.at[:, :, cols], xb.at[:, pl.ds(rows, rows), to], sems.at[i, 2]),
        ]
        for copy in mine:
            copy.start()
        loads.append(mine)
    return loads


def dx_kernel(keys, parts, term_keys, part, sc, dgu, gt, x, dy, xp, *refs):
    chunks, (keep, send, *outs), (buf, xb, w_sems, x_sems) = refs[:-8], refs[-8:-4], refs[-4:]
    rows, two = keep.shape[0], 2 * part
    loads = load_blocks(term_keys, sc, x, dy, xp, xb, x_sems)
    waits = load_chunks(parts, [offset(sc, *key) for key in keys], part, chunks, buf, w_sems)
    for mine in loads:
        for copy in mine:
            copy.wait()
    put_terms(outs, part, mm(gt[:two], xb[0]), mm(gt[two:], xb[1]))
    clear_pad(buf, part)
    for mine in waits:
        for copy in mine:
            copy.wait()
    step = 4 * LANES
    for at in range(0, keep.shape[1], step):
        cols = slice(at, at + step)
        dx = mm(dgu[0], buf[:LANES, cols]) + mm(dgu[1], buf[LANES : 2 * LANES, cols])
        keep[:, cols] = dx[:rows].astype(BF)
        send[:, cols] = dx[rows:].astype(BF)


def terms_kernel(keys, part, sc, gt, x, dy, xp, *refs):
    outs, (xb, x_sems) = refs[:-2], refs[-2:]
    rows = x.shape[0]
    loads = load_blocks(keys, sc, x, dy, xp, xb, x_sems)
    two = 2 * part
    for i in range(0, len(keys), 2):
        for copy in loads[i] + loads[i + 1]:
            copy.wait()
        cols = slice(i * LANES, (i + 2) * LANES)
        put_terms(outs[i // 2 : i // 2 + 1], part, mm(gt[:two], xb[0, :, cols]), mm(gt[two:], xb[1, :, cols]))


def join_kernel(part, sc, own, other, *outs):
    mine, theirs = pl.multiple_of(sc[1] * part, part), pl.multiple_of((1 - sc[1]) * part, part)
    for m, out in enumerate(outs):
        out[pl.ds(mine, part)] = own[m * part : (m + 1) * part]
        out[pl.ds(theirs, part)] = other[m * part : (m + 1) * part]


def params(mib):
    return pltpu.CompilerParams(vmem_limit_bytes=mib * 1024 * 1024)


def local(inputs, out_grad, w_gate, w_up, w_down):
    rows, width = inputs.shape[1:]
    part = w_down.shape[0] // 2
    dp, mp = lax.axis_index("dp"), lax.axis_index("mp")
    yl, z = dp // NZ, dp % NZ
    yh, x, c = mp // 8, mp // 2 % NX, mp % 2
    group = rows // 16
    x_own, dy_own = inputs[0], out_grad[0]

    slot = lax.iota(jnp.int32, 26)
    at = slot - 2
    dc, dx, dh = at // 8, at // 2 % NX, at % 2
    ordered = (yh ^ dh) * 8 + (x - (1 - 2 * (c ^ dc)) * dx + NX) % NX * 2 + (c ^ dc)
    at = slot - 18
    dc, dx = at // NX % 2, at % NX
    stands = dc * NX + (NX - (1 - 2 * (c ^ dc)) * dx) % NX
    sc = jnp.where(slot < 2, jnp.where(slot == 0, z, yl), jnp.where(slot < 18, ordered, stands)).astype(jnp.int32)

    u32 = jnp.uint32
    starts = [(yl * part).astype(u32), ((1 - yl) * part).astype(u32), (mp * group).astype(u32), ((mp ^ 8) * group).astype(u32)]
    w_gate, w_up, w_down, x_own, dy_own, sc, *starts = after_all(w_gate, w_up, w_down, x_own, dy_own, sc, *starts)

    def rows_from(array, start, count):
        return lax.dynamic_slice(array, (start, u32(0)), (count, array.shape[1]))

    stacked = jnp.stack([w_gate.T, w_up.T, w_down])
    own, other = (
        lax.dynamic_slice(stacked, (u32(0), starts[i], u32(0)), (3, part, LANES)).reshape(3 * part, LANES)
        for i in range(2)
    )
    mid = own.shape[0] // 2

    def piece(array):
        return jnp.concatenate([rows_from(array, start, group) for start in starts[2:]])

    n = own.shape[0]
    up, down = pz(own, 1), pz(own, -1)
    other = pyl(other)
    chunks = {
        (0, 0): [(own, 0, 0, n)],
        (0, 7): [(up, 0, 0, n)],
        (0, 1): [(down, 0, 0, n)],
        (1, 0): [(other, 0, 0, n)],
    }
    first = jnp.stack([piece(after(x_own, own)), piece(after(dy_own, own))])
    first = pyl(after(first, up))
    up, down = jnp.concatenate([other, up]), jnp.concatenate([down, other])
    for step in (1, 2):
        up, down = pz(up, 1), pz(down, -1)
        chunks[1, NZ - step], chunks[0, NZ - step - 1] = [(up, 0, 0, n)], [(up, n, 0, n)]
        chunks[0, step + 1], chunks[1, step] = [(down, 0, 0, n)], [(down, n, 0, n)]
        if step == 1:
            left, right = pxs(first, 1), pxs(first, -1)
            left_s, right_s, first_s, _, _ = after_all(left, right, first, up, down)
            far_x, far_dy = pxs(left_s[0], 1), pxs(right_s[1], -1)
            swap = pc(jnp.stack([first_s, right_s, left_s]))
    up, down = up[: n + mid], down[mid:]
    far_x, far_dy, _, _ = after_all(far_x, far_dy, up, down)
    two_off = jnp.stack([far_x, far_dy])
    swap_two = pc(two_off)
    up, down = pz(up, 1), pz(down, -1)
    chunks[1, 5], chunks[1, 3] = [(up, 0, 0, n)], [(down, n - mid, 0, n)]
    chunks[0, 4] = [(up, n, 0, mid), (down, 0, mid, n - mid)]
    pieces = [first[None], right[None], two_off[None], left[None], swap, swap_two[None]]
    piece_at = [(0, 0), (1, 0), (2, 0), (3, 0), (4, 0), (4, 1), (5, 0), (4, 2)]

    late = [(1, 4), (0, 4), (1, 3), (1, 5)]
    early = [key for key in chunks if key not in late]

    def listed(keys):
        refs, where = [], []
        for key in keys:
            parts = []
            for array, *rest in chunks[key]:
                at = [i for i, a in enumerate(refs) if a is array]
                if not at:
                    refs.append(array)
                parts.append((at[0] if at else len(refs) - 1, *rest))
            where.append(tuple(parts))
        return tuple(where), refs

    parts, refs = listed(early)
    acc, xp = pl.pallas_call(
        functools.partial(early_kernel, early, late, parts, len(pieces), piece_at, part),
        out_shape=(
            jax.ShapeDtypeStruct((2 * rows, 3 * LANES), F32),
            jax.ShapeDtypeStruct((2, rows, width), BF),
        ),
        in_specs=[SMEM] + [VMEM] * (2 + len(pieces)) + [HBM] * len(refs),
        out_specs=(VMEM, VMEM),
        scratch_shapes=[
            pltpu.VMEM((3 * LANES, width), BF),
            pltpu.SemaphoreType.DMA((copies_of(parts, part),)),
        ],
        compiler_params=params(22),
        cost_estimate=COST,
        name="early",
    )(sc, x_own, dy_own, *pieces, *refs)

    up, down = after(up, acc, xp), after(down, acc, xp)
    up, down = pz(up[:mid], 1), pz(down[n:], -1)
    chunks[1, 4] = [(up, 0, 0, mid), (down, 0, mid, n - mid)]

    parts, refs = listed(late)
    full = jax.ShapeDtypeStruct((3 * part, LANES), BF)
    double = jax.ShapeDtypeStruct((6 * part, LANES), BF)
    late_terms = [(1, 3), (0, 3), (1, 5), (0, 5)]
    gt, dgu, *far = pl.pallas_call(
        functools.partial(late_kernel, late, parts, part),
        out_shape=(
            jax.ShapeDtypeStruct((3 * part, 2 * rows), BF),
            jax.ShapeDtypeStruct((2, 2 * rows, LANES), BF),
            full, full,
        ),
        in_specs=[SMEM, VMEM] + [ANY] * 3 + [VMEM] * len(refs),
        out_specs=(VMEM,) * 4,
        scratch_shapes=[
            pltpu.VMEM((2 * rows, LANES), BF),
            pltpu.VMEM((2, 2 * rows, len(late) * LANES), BF),
            pltpu.VMEM((3 * LANES, len(late) * LANES), BF),
            pltpu.SemaphoreType.DMA((len(late), 3)),
        ],
        compiler_params=params(22),
        cost_estimate=COST,
        name="late",
    )(sc, acc, x_own, dy_own, xp, *refs)


    def ring(up, down):
        return pz(up, 1), pz(down, -1)

    up, down = ring(*far)

    keys = list(chunks)
    parts, refs = listed(keys)
    keep, send, *got = pl.pallas_call(
        functools.partial(dx_kernel, keys, parts, late_terms, part),
        out_shape=(jax.ShapeDtypeStruct((rows, width), BF),) * 2 + (double,) * 2,
        in_specs=[SMEM, VMEM, VMEM] + [ANY] * 3 + [HBM] * len(refs),
        out_specs=(VMEM,) * 4,
        scratch_shapes=[
            pltpu.VMEM((3 * LANES, width), BF),
            pltpu.VMEM((2, 2 * rows, 4 * LANES), BF),
            pltpu.SemaphoreType.DMA((copies_of(parts, part),)),
            pltpu.SemaphoreType.DMA((4, 3)),
        ],
        compiler_params=params(24),
        cost_estimate=COST,
        name="dx",
    )(sc, dgu, gt, x_own, dy_own, xp, *refs)
    term = dict(zip((3, 5), got))

    up, down, send = after_all(up, down, send)
    sent = pc(send)

    def joined(whole, halves, k, first):
        whole, half = whole[k * n : (k + 1) * n].astype(F32), halves[k * mid : (k + 1) * mid]
        if first:
            return jnp.concatenate([whole[:mid], whole[mid:] + half]).astype(BF)
        return jnp.concatenate([whole[:mid] + half, whole[mid:]]).astype(BF)

    p_in, o_in = ((joined(term[3], up, k, 0), joined(term[5], down, k, 1)) for k in range(2))
    gt_later = after(gt, *p_in, *o_in)
    p, o = ring(*p_in), ring(*o_in)
    distances = (2, 6, 1, 7, 0)
    keys = [(k, s) for s in distances for k in (1, 0)]
    got = pl.pallas_call(
        functools.partial(terms_kernel, keys, part),
        out_shape=(double,) * len(distances),
        in_specs=[SMEM, VMEM] + [ANY] * 3,
        out_specs=(VMEM,) * len(distances),
        scratch_shapes=[
            pltpu.VMEM((2, 2 * rows, len(keys) * LANES), BF),
            pltpu.SemaphoreType.DMA((len(keys), 3)),
        ],
        compiler_params=params(20),
        cost_estimate=COST,
        name="terms",
    )(sc, gt_later, x_own, dy_own, xp)
    term.update(zip(distances, got))

    quarter = rows // NX

    def pair(i):
        rows_of = slice(i * quarter, (i + 1) * quarter)
        return keep[rows_of].astype(F32) + sent[rows_of].astype(F32)

    def add(k, s, up, down):
        rows_of = slice(k * n, (k + 1) * n)
        return (
            (term[s][rows_of].astype(F32) + up).astype(BF),
            (term[NZ - s][rows_of].astype(F32) + down).astype(BF),
        )

    acc = px(pair(3).astype(BF), -1)
    p_in = add(0, 2, *p)
    p = ring(*p_in)
    o_in = add(1, 2, *after(tuple(o), *p_in))
    o = ring(*o_in)
    acc = px((pair(2) + after(acc, *p_in)).astype(BF), -1)
    acc = px((pair(1) + after(acc, *o_in)).astype(BF), -1)
    p_in = add(0, 1, *p)
    p = ring(*p_in)
    o_in = add(1, 1, *after(tuple(o), *p_in))
    o = ring(*o_in)
    acc = pair(0) + after(acc, *p_in)
    part_b = [acc[i * group : (i + 1) * group].astype(BF) for i in range(1, 4)]
    sum_other = (term[0][:n].astype(F32) + p[0].astype(F32) + p[1].astype(F32)).astype(BF)
    *part_b, _ = after_all(*part_b, sum_other)
    got = [pyh(part_b[0]), pyl(part_b[1]), pboth(part_b[2])]
    in_grad = (acc[:group] + got[0] + got[1] + got[2]).astype(BF).reshape(1, group, width)
    o = after(tuple(o), sum_other, *part_b)
    sum_other = pyl(sum_other)
    sum_own = (term[0][n:].astype(F32) + o[0].astype(F32) + o[1].astype(F32)).astype(BF)

    gate_grad, up_grad, down_grad = pl.pallas_call(
        functools.partial(join_kernel, part),
        out_shape=(jax.ShapeDtypeStruct((2 * part, LANES), BF),) * 3,
        in_specs=[SMEM, VMEM, VMEM],
        out_specs=(VMEM,) * 3,
        compiler_params=params(8),
        cost_estimate=COST,
        name="join",
    )(sc, sum_own, sum_other)
    return in_grad, gate_grad.T, up_grad.T, down_grad


def solution(mesh):
    placed = (P("dp", None, None), P("dp", None, None), P("dp", "mp"), P("dp", "mp"), P("mp", "dp"))
    return jax.shard_map(
        local,
        mesh=mesh,
        in_specs=placed,
        out_specs=(P("dp", "mp", None), P("dp", "mp"), P("dp", "mp"), P("mp", "dp")),
        check_vma=False,
    )
```

```python
import functools

import jax
import jax.numpy as jnp
from jax import lax
from jax.experimental import pallas as pl
from jax.experimental.pallas import tpu as pltpu
from jax.sharding import PartitionSpec as P

BF = jnp.bfloat16
F32 = jnp.float32
NX, NZ = 4, 8
LANES = 256
ANY = pl.BlockSpec(memory_space=pl.ANY)
HBM = pl.BlockSpec(memory_space=pltpu.HBM)
VMEM = pl.BlockSpec(memory_space=pltpu.VMEM)
COST = pl.CostEstimate(flops=1, bytes_accessed=1, transcendentals=0)
SMEM = pl.BlockSpec(memory_space=pltpu.SMEM)


def mm(left, right):
    return lax.dot_general(left, right, (((1,), (0,)), ((), ())), preferred_element_type=F32)


def mm_t(left, right):
    return lax.dot_general(left, right, (((1,), (1,)), ((), ())), preferred_element_type=F32)


def pz(value, step):
    pairs = [(y * NZ + z, y * NZ + (z + step) % NZ) for y in range(2) for z in range(NZ)]
    return lax.ppermute(value, "dp", pairs)


def pyl(value):
    return lax.ppermute(value, "dp", [(i, (i + NZ) % (2 * NZ)) for i in range(2 * NZ)])


def px(value, step):
    pairs = [
        (y * 8 + x * 2 + c, y * 8 + (x + (-step if c else step)) % NX * 2 + c)
        for y in range(2) for x in range(NX) for c in range(2)
    ]
    return lax.ppermute(value, "mp", pairs)


def pxs(value, step):
    pairs = [
        (y * 8 + x * 2 + c, y * 8 + (x + step) % NX * 2 + c)
        for y in range(2) for x in range(NX) for c in range(2)
    ]
    return lax.ppermute(value, "mp", pairs)


def pc(value):
    return lax.ppermute(value, "mp", [(i, i ^ 1) for i in range(16)])


def pyh(value):
    return lax.ppermute(value, "mp", [(i, i ^ 8) for i in range(16)])


def pboth(value):
    n = 2 * NZ
    pairs = [(m * n + d, (m ^ 8) * n + (d + NZ) % n) for m in range(16) for d in range(n)]
    return lax.ppermute(value, ("mp", "dp"), pairs)


def after(value, *others):
    return lax.optimization_barrier((value, *others))[0]


def after_all(*values):
    return lax.optimization_barrier(values)


def col_block(sc, k, s):
    yl = 1 - sc[1] if k else sc[1]
    return yl * NZ + lax.rem(sc[0] + s, NZ)


def offset(sc, k, s):
    return pl.multiple_of(col_block(sc, k, s) * LANES, LANES)


def spread(row, count, part):
    out, end = [], row + count
    while row < end:
        m = row // part
        n = min(end, (m + 1) * part) - row
        out.append((row, n, m * LANES + row - m * part))
        row += n
    return out


def load_chunks(where, places, part, refs, buf, sems):
    waits, sem = [], 0
    for parts, place in zip(where, places):
        mine = []
        for at, row, start, count in parts:
            for first, n, to in spread(start, count, part):
                copy = pltpu.make_async_copy(
                    refs[at].at[pl.ds(row + first - start, n)],
                    buf.at[pl.ds(to, n), pl.ds(place, LANES)],
                    sems.at[sem],
                )
                copy.start()
                mine.append(copy)
                sem += 1
        waits.append(mine)
    return waits


def copies_of(where, part):
    return sum(len(spread(start, count, part)) for parts in where for _, _, start, count in parts)


def clear_pad(buf, part):
    for m in range(3):
        buf[m * LANES + part : (m + 1) * LANES] = jnp.zeros((LANES - part, buf.shape[1]), BF)


def early_kernel(keys, missing, parts, n_pieces, piece_at, part, sc, x, dy, *refs):
    pieces, chunks, (acc, xp, buf, w_sems) = refs[:n_pieces], refs[n_pieces:-4], refs[-4:]
    rows = x.shape[0]
    waits = load_chunks(parts, [offset(sc, *key) for key in keys], part, chunks, buf, w_sems)
    clear_pad(buf, part)
    for key in missing:
        buf[:, pl.ds(offset(sc, *key), LANES)] = jnp.zeros((buf.shape[0], LANES), BF)
    row = 0
    for i, j in piece_at:
        count = pieces[i].shape[2]
        xp[:, row : row + count] = pieces[i][j]
        row += count
    for mine in waits:
        for copy in mine:
            copy.wait()
    both, down = buf[: 2 * LANES], buf[2 * LANES :]
    acc[:rows, : 2 * LANES] = mm_t(x[...], both)
    acc[rows:, : 2 * LANES] = mm_t(xp[0], both)
    acc[:rows, 2 * LANES :] = mm_t(dy[...], down)
    acc[rows:, 2 * LANES :] = mm_t(xp[1], down)


def put_terms(outs, part, top, low):
    two, n = 2 * part, 3 * part
    top, low = top.astype(BF), low.astype(BF)
    for j, out in enumerate(outs):
        for k in range(2):
            cols = slice((2 * j + k) * LANES, (2 * j + k + 1) * LANES)
            out[k * n : k * n + two] = top[:, cols]
            out[k * n + two : (k + 1) * n] = low[:, cols]


def late_kernel(keys, parts, part, sc, acc, x, dy, xp, *refs):
    chunks = refs[:-8]
    gt, dgu, *far = refs[-8:-4]
    rowbuf, xb, buf, x_sems = refs[-4:]
    rows = x.shape[0]
    loads = []
    for i, (k, s) in enumerate(keys):
        cols, to = pl.ds(offset(sc, k, s), LANES), pl.ds(i * LANES, LANES)
        loads += [
            pltpu.make_async_copy(x.at[:, cols], xb.at[0, pl.ds(0, rows), to], x_sems.at[i, 0]),
            pltpu.make_async_copy(dy.at[:, cols], xb.at[1, pl.ds(0, rows), to], x_sems.at[i, 1]),
            pltpu.make_async_copy(xp.at[:, :, cols], xb.at[:, pl.ds(rows, rows), to], x_sems.at[i, 2]),
        ]
    for copy in loads:
        copy.start()
    clear_pad(buf, part)
    for i, pieces in enumerate(parts):
        for at, row, start, count in pieces:
            for first, n, to in spread(start, count, part):
                row_at = row + first - start
                buf[to : to + n, i * LANES : (i + 1) * LANES] = chunks[at][row_at : row_at + n]
    for copy in loads:
        copy.wait()
    both = acc[:, : 2 * LANES] + mm_t(xb[0], buf[: 2 * LANES])
    dhid = acc[:, 2 * LANES :] + mm_t(xb[1], buf[2 * LANES :])
    gate, up_val = both[:, :LANES], both[:, LANES:]
    sig = 1.0 / (1.0 + jnp.exp(-gate))
    silu = gate * sig
    hidden = silu * up_val
    dup = dhid * silu
    dgate = dhid * up_val * sig * (1.0 + gate * (1.0 - sig))
    for m, value in enumerate((dgate, dup, hidden)):
        gt[m * part : (m + 1) * part] = value.T[:part].astype(BF)
    mid = 3 * part // 2
    two = 2 * part
    up, down = far
    for j in range(2):
        cols = slice(j * LANES, (j + 1) * LANES)
        top, low = mm(gt[:two], xb[0, :, cols]), mm(gt[two:], xb[1, :, cols])
        at = j * mid
        up[at : at + mid] = top[:mid].astype(BF)
        down[at : at + two - mid] = top[mid:].astype(BF)
        down[at + two - mid : at + mid] = low.astype(BF)
    group = rows // 16
    for m, value in enumerate((dgate, dup)):
        rowbuf[...] = value.astype(BF)
        for g in range(16):
            to = g // 2 * 4 * group + g % 2 * group
            at = pl.multiple_of(sc[2 + g] * group, group)
            dgu[m, to : to + group] = rowbuf[pl.ds(at, group)]
        for g in range(8):
            to = g * 4 * group + 2 * group
            at = pl.multiple_of(rows + sc[18 + g] * 2 * group, 2 * group)
            dgu[m, to : to + 2 * group] = rowbuf[pl.ds(at, 2 * group)]


def load_blocks(keys, sc, x, dy, xp, xb, sems):
    rows, loads = x.shape[0], []
    for i, (k, s) in enumerate(keys):
        cols, to = pl.ds(offset(sc, k, s), LANES), pl.ds(i * LANES, LANES)
        mine = [
            pltpu.make_async_copy(x.at[:, cols], xb.at[0, pl.ds(0, rows), to], sems.at[i, 0]),
            pltpu.make_async_copy(dy.at[:, cols], xb.at[1, pl.ds(0, rows), to], sems.at[i, 1]),
            pltpu.make_async_copy(xp.at[:, :, cols], xb.at[:, pl.ds(rows, rows), to], sems.at[i, 2]),
        ]
        for copy in mine:
            copy.start()
        loads.append(mine)
    return loads


def dx_kernel(keys, parts, term_keys, part, sc, dgu, gt, x, dy, xp, *refs):
    chunks, (keep, send, *outs), (buf, xb, w_sems, x_sems) = refs[:-8], refs[-8:-4], refs[-4:]
    rows, two = keep.shape[0], 2 * part
    loads = load_blocks(term_keys, sc, x, dy, xp, xb, x_sems)
    waits = load_chunks(parts, [offset(sc, *key) for key in keys], part, chunks, buf, w_sems)
    for mine in loads:
        for copy in mine:
            copy.wait()
    put_terms(outs, part, mm(gt[:two], xb[0]), mm(gt[two:], xb[1]))
    clear_pad(buf, part)
    for mine in waits:
        for copy in mine:
            copy.wait()
    step = 4 * LANES
    for at in range(0, keep.shape[1], step):
        cols = slice(at, at + step)
        dx = mm(dgu[0], buf[:LANES, cols]) + mm(dgu[1], buf[LANES : 2 * LANES, cols])
        keep[:, cols] = dx[:rows].astype(BF)
        send[:, cols] = dx[rows:].astype(BF)


def terms_kernel(keys, part, sc, gt, x, dy, xp, *refs):
    outs, (xb, x_sems) = refs[:-2], refs[-2:]
    rows = x.shape[0]
    loads = load_blocks(keys, sc, x, dy, xp, xb, x_sems)
    two = 2 * part
    for i in range(0, len(keys), 2):
        for copy in loads[i] + loads[i + 1]:
            copy.wait()
        cols = slice(i * LANES, (i + 2) * LANES)
        put_terms(outs[i // 2 : i // 2 + 1], part, mm(gt[:two], xb[0, :, cols]), mm(gt[two:], xb[1, :, cols]))


def join_kernel(part, sc, own, other, *outs):
    mine, theirs = pl.multiple_of(sc[1] * part, part), pl.multiple_of((1 - sc[1]) * part, part)
    for m, out in enumerate(outs):
        out[pl.ds(mine, part)] = own[m * part : (m + 1) * part]
        out[pl.ds(theirs, part)] = other[m * part : (m + 1) * part]


def params(mib):
    return pltpu.CompilerParams(vmem_limit_bytes=mib * 1024 * 1024)


def local(inputs, out_grad, w_gate, w_up, w_down):
    rows, width = inputs.shape[1:]
    part = w_down.shape[0] // 2
    dp, mp = lax.axis_index("dp"), lax.axis_index("mp")
    yl, z = dp // NZ, dp % NZ
    yh, x, c = mp // 8, mp // 2 % NX, mp % 2
    group = rows // 16
    x_own, dy_own = inputs[0], out_grad[0]

    slot = lax.iota(jnp.int32, 26)
    at = slot - 2
    dc, dx, dh = at // 8, at // 2 % NX, at % 2
    ordered = (yh ^ dh) * 8 + (x - (1 - 2 * (c ^ dc)) * dx + NX) % NX * 2 + (c ^ dc)
    at = slot - 18
    dc, dx = at // NX % 2, at % NX
    stands = dc * NX + (NX - (1 - 2 * (c ^ dc)) * dx) % NX
    sc = jnp.where(slot < 2, jnp.where(slot == 0, z, yl), jnp.where(slot < 18, ordered, stands)).astype(jnp.int32)

    u32 = jnp.uint32
    starts = [(yl * part).astype(u32), ((1 - yl) * part).astype(u32), (mp * group).astype(u32), ((mp ^ 8) * group).astype(u32)]
    w_gate, w_up, w_down, x_own, dy_own, sc, *starts = after_all(w_gate, w_up, w_down, x_own, dy_own, sc, *starts)

    def rows_from(array, start, count):
        return lax.dynamic_slice(array, (start, u32(0)), (count, array.shape[1]))

    stacked = jnp.stack([w_gate.T, w_up.T, w_down])
    own, other = (
        lax.dynamic_slice(stacked, (u32(0), starts[i], u32(0)), (3, part, LANES)).reshape(3 * part, LANES)
        for i in range(2)
    )
    mid = own.shape[0] // 2

    def piece(array):
        return jnp.concatenate([rows_from(array, start, group) for start in starts[2:]])

    n = own.shape[0]
    up, down = pz(own, 1), pz(own, -1)
    other = pyl(other)
    chunks = {
        (0, 0): [(own, 0, 0, n)],
        (0, 7): [(up, 0, 0, n)],
        (0, 1): [(down, 0, 0, n)],
        (1, 0): [(other, 0, 0, n)],
    }
    first = jnp.stack([piece(after(x_own, own)), piece(after(dy_own, own))])
    first = pyl(after(first, up))
    up, down = jnp.concatenate([other, up]), jnp.concatenate([down, other])
    for step in (1, 2):
        up, down = pz(up, 1), pz(down, -1)
        chunks[1, NZ - step], chunks[0, NZ - step - 1] = [(up, 0, 0, n)], [(up, n, 0, n)]
        chunks[0, step + 1], chunks[1, step] = [(down, 0, 0, n)], [(down, n, 0, n)]
        if step == 1:
            left, right = pxs(first, 1), pxs(first, -1)
            left_s, right_s, first_s, _, _ = after_all(left, right, first, up, down)
            far_x, far_dy = pxs(left_s[0], 1), pxs(right_s[1], -1)
            swap = pc(jnp.stack([first_s, right_s, left_s]))
    up, down = up[: n + mid], down[mid:]
    far_x, far_dy, _, _ = after_all(far_x, far_dy, up, down)
    two_off = jnp.stack([far_x, far_dy])
    swap_two = pc(two_off)
    up, down = pz(up, 1), pz(down, -1)
    chunks[1, 5], chunks[1, 3] = [(up, 0, 0, n)], [(down, n - mid, 0, n)]
    chunks[0, 4] = [(up, n, 0, mid), (down, 0, mid, n - mid)]
    pieces = [first[None], right[None], two_off[None], left[None], swap, swap_two[None]]
    piece_at = [(0, 0), (1, 0), (2, 0), (3, 0), (4, 0), (4, 1), (5, 0), (4, 2)]

    late = [(1, 4), (0, 4)]
    early = [key for key in chunks if key not in late]

    def listed(keys):
        refs, where = [], []
        for key in keys:
            parts = []
            for array, *rest in chunks[key]:
                at = [i for i, a in enumerate(refs) if a is array]
                if not at:
                    refs.append(array)
                parts.append((at[0] if at else len(refs) - 1, *rest))
            where.append(tuple(parts))
        return tuple(where), refs

    parts, refs = listed(early)
    acc, xp = pl.pallas_call(
        functools.partial(early_kernel, early, late, parts, len(pieces), piece_at, part),
        out_shape=(
            jax.ShapeDtypeStruct((2 * rows, 3 * LANES), F32),
            jax.ShapeDtypeStruct((2, rows, width), BF),
        ),
        in_specs=[SMEM] + [VMEM] * (2 + len(pieces)) + [HBM] * len(refs),
        out_specs=(VMEM, VMEM),
        scratch_shapes=[
            pltpu.VMEM((3 * LANES, width), BF),
            pltpu.SemaphoreType.DMA((copies_of(parts, part),)),
        ],
        compiler_params=params(22),
        cost_estimate=COST,
        name="early",
    )(sc, x_own, dy_own, *pieces, *refs)

    up, down = pz(up[:mid], 1), pz(down[n:], -1)
    chunks[1, 4] = [(up, 0, 0, mid), (down, 0, mid, n - mid)]

    parts, refs = listed(late)
    full = jax.ShapeDtypeStruct((3 * part, LANES), BF)
    double = jax.ShapeDtypeStruct((6 * part, LANES), BF)
    late_terms = [(1, 3), (0, 3), (1, 5), (0, 5)]
    gt, dgu, *far = pl.pallas_call(
        functools.partial(late_kernel, late, parts, part),
        out_shape=(
            jax.ShapeDtypeStruct((3 * part, 2 * rows), BF),
            jax.ShapeDtypeStruct((2, 2 * rows, LANES), BF),
            full, full,
        ),
        in_specs=[SMEM, VMEM] + [ANY] * 3 + [VMEM] * len(refs),
        out_specs=(VMEM,) * 4,
        scratch_shapes=[
            pltpu.VMEM((2 * rows, LANES), BF),
            pltpu.VMEM((2, 2 * rows, len(late) * LANES), BF),
            pltpu.VMEM((3 * LANES, len(late) * LANES), BF),
            pltpu.SemaphoreType.DMA((len(late), 3)),
        ],
        compiler_params=params(22),
        cost_estimate=COST,
        name="late",
    )(sc, acc, x_own, dy_own, xp, *refs)


    def ring(up, down):
        return pz(up, 1), pz(down, -1)

    up, down = ring(*far)

    keys = list(chunks)
    parts, refs = listed(keys)
    keep, send, *got = pl.pallas_call(
        functools.partial(dx_kernel, keys, parts, late_terms, part),
        out_shape=(jax.ShapeDtypeStruct((rows, width), BF),) * 2 + (double,) * 2,
        in_specs=[SMEM, VMEM, VMEM] + [ANY] * 3 + [HBM] * len(refs),
        out_specs=(VMEM,) * 4,
        scratch_shapes=[
            pltpu.VMEM((3 * LANES, width), BF),
            pltpu.VMEM((2, 2 * rows, 4 * LANES), BF),
            pltpu.SemaphoreType.DMA((copies_of(parts, part),)),
            pltpu.SemaphoreType.DMA((4, 3)),
        ],
        compiler_params=params(24),
        cost_estimate=COST,
        name="dx",
    )(sc, dgu, gt, x_own, dy_own, xp, *refs)
    term = dict(zip((3, 5), got))

    up, down, send = after_all(up, down, send)
    sent = pc(send)

    def joined(whole, halves, k, first):
        whole, half = whole[k * n : (k + 1) * n].astype(F32), halves[k * mid : (k + 1) * mid]
        if first:
            return jnp.concatenate([whole[:mid], whole[mid:] + half]).astype(BF)
        return jnp.concatenate([whole[:mid] + half, whole[mid:]]).astype(BF)

    p_in, o_in = ((joined(term[3], up, k, 0), joined(term[5], down, k, 1)) for k in range(2))
    gt_later = after(gt, *p_in, *o_in)
    p, o = ring(*p_in), ring(*o_in)
    distances = (2, 6, 1, 7, 0)
    keys = [(k, s) for s in distances for k in (1, 0)]
    got = pl.pallas_call(
        functools.partial(terms_kernel, keys, part),
        out_shape=(double,) * len(distances),
        in_specs=[SMEM, VMEM] + [ANY] * 3,
        out_specs=(VMEM,) * len(distances),
        scratch_shapes=[
            pltpu.VMEM((2, 2 * rows, len(keys) * LANES), BF),
            pltpu.SemaphoreType.DMA((len(keys), 3)),
        ],
        compiler_params=params(20),
        cost_estimate=COST,
        name="terms",
    )(sc, gt_later, x_own, dy_own, xp)
    term.update(zip(distances, got))

    quarter = rows // NX

    def pair(i):
        rows_of = slice(i * quarter, (i + 1) * quarter)
        return keep[rows_of].astype(F32) + sent[rows_of].astype(F32)

    def add(k, s, up, down):
        rows_of = slice(k * n, (k + 1) * n)
        return (
            (term[s][rows_of].astype(F32) + up).astype(BF),
            (term[NZ - s][rows_of].astype(F32) + down).astype(BF),
        )

    acc = px(pair(3).astype(BF), -1)
    p_in = add(0, 2, *p)
    p = ring(*p_in)
    o_in = add(1, 2, *after(tuple(o), *p_in))
    o = ring(*o_in)
    acc = px((pair(2) + after(acc, *p_in)).astype(BF), -1)
    acc = px((pair(1) + after(acc, *o_in)).astype(BF), -1)
    p_in = add(0, 1, *p)
    p = ring(*p_in)
    o_in = add(1, 1, *after(tuple(o), *p_in))
    o = ring(*o_in)
    acc = pair(0) + after(acc, *p_in)
    part_b = [acc[i * group : (i + 1) * group].astype(BF) for i in range(1, 4)]
    sum_other = (term[0][:n].astype(F32) + p[0].astype(F32) + p[1].astype(F32)).astype(BF)
    *part_b, _ = after_all(*part_b, sum_other)
    got = [pyh(part_b[0]), pyl(part_b[1]), pboth(part_b[2])]
    in_grad = (acc[:group] + got[0] + got[1] + got[2]).astype(BF).reshape(1, group, width)
    o = after(tuple(o), sum_other, *part_b)
    sum_other = pyl(sum_other)
    sum_own = (term[0][n:].astype(F32) + o[0].astype(F32) + o[1].astype(F32)).astype(BF)

    gate_grad, up_grad, down_grad = pl.pallas_call(
        functools.partial(join_kernel, part),
        out_shape=(jax.ShapeDtypeStruct((2 * part, LANES), BF),) * 3,
        in_specs=[SMEM, VMEM, VMEM],
        out_specs=(VMEM,) * 3,
        compiler_params=params(8),
        cost_estimate=COST,
        name="join",
    )(sc, sum_own, sum_other)
    return in_grad, gate_grad.T, up_grad.T, down_grad


def solution(mesh):
    placed = (P("dp", None, None), P("dp", None, None), P("dp", "mp"), P("dp", "mp"), P("mp", "dp"))
    return jax.shard_map(
        local,
        mesh=mesh,
        in_specs=placed,
        out_specs=(P("dp", "mp", None), P("dp", "mp"), P("dp", "mp"), P("mp", "dp")),
        check_vma=False,
    )
```

```python
import functools

import jax
import jax.numpy as jnp
from jax import lax
from jax.experimental import pallas as pl
from jax.experimental.pallas import tpu as pltpu
from jax.sharding import PartitionSpec as P

BF = jnp.bfloat16
F32 = jnp.float32
NX, NZ = 4, 8
LANES = 256
ANY = pl.BlockSpec(memory_space=pl.ANY)
HBM = pl.BlockSpec(memory_space=pltpu.HBM)
VMEM = pl.BlockSpec(memory_space=pltpu.VMEM)
COST = pl.CostEstimate(flops=1, bytes_accessed=1, transcendentals=0)
SMEM = pl.BlockSpec(memory_space=pltpu.SMEM)


def mm(left, right):
    return lax.dot_general(left, right, (((1,), (0,)), ((), ())), preferred_element_type=F32)


def mm_t(left, right):
    return lax.dot_general(left, right, (((1,), (1,)), ((), ())), preferred_element_type=F32)


def pz(value, step):
    pairs = [(y * NZ + z, y * NZ + (z + step) % NZ) for y in range(2) for z in range(NZ)]
    return lax.ppermute(value, "dp", pairs)


def pyl(value):
    return lax.ppermute(value, "dp", [(i, (i + NZ) % (2 * NZ)) for i in range(2 * NZ)])


def px(value, step):
    pairs = [
        (y * 8 + x * 2 + c, y * 8 + (x + (-step if c else step)) % NX * 2 + c)
        for y in range(2) for x in range(NX) for c in range(2)
    ]
    return lax.ppermute(value, "mp", pairs)


def pxs(value, step):
    pairs = [
        (y * 8 + x * 2 + c, y * 8 + (x + step) % NX * 2 + c)
        for y in range(2) for x in range(NX) for c in range(2)
    ]
    return lax.ppermute(value, "mp", pairs)


def pc(value):
    return lax.ppermute(value, "mp", [(i, i ^ 1) for i in range(16)])


def pyh(value):
    return lax.ppermute(value, "mp", [(i, i ^ 8) for i in range(16)])


def pboth(value):
    n = 2 * NZ
    pairs = [(m * n + d, (m ^ 8) * n + (d + NZ) % n) for m in range(16) for d in range(n)]
    return lax.ppermute(value, ("mp", "dp"), pairs)


def after(value, *others):
    return lax.optimization_barrier((value, *others))[0]


def after_all(*values):
    return lax.optimization_barrier(values)


def col_block(sc, k, s):
    yl = 1 - sc[1] if k else sc[1]
    return yl * NZ + lax.rem(sc[0] + s, NZ)


def offset(sc, k, s):
    return pl.multiple_of(col_block(sc, k, s) * LANES, LANES)


def spread(row, count, part):
    out, end = [], row + count
    while row < end:
        m = row // part
        n = min(end, (m + 1) * part) - row
        out.append((row, n, m * LANES + row - m * part))
        row += n
    return out


def load_chunks(where, places, part, refs, buf, sems):
    waits, sem = [], 0
    for parts, place in zip(where, places):
        mine = []
        for at, row, start, count in parts:
            for first, n, to in spread(start, count, part):
                copy = pltpu.make_async_copy(
                    refs[at].at[pl.ds(row + first - start, n)],
                    buf.at[pl.ds(to, n), pl.ds(place, LANES)],
                    sems.at[sem],
                )
                copy.start()
                mine.append(copy)
                sem += 1
        waits.append(mine)
    return waits


def copies_of(where, part):
    return sum(len(spread(start, count, part)) for parts in where for _, _, start, count in parts)


def clear_pad(buf, part):
    for m in range(3):
        buf[m * LANES + part : (m + 1) * LANES] = jnp.zeros((LANES - part, buf.shape[1]), BF)


def early_kernel(keys, missing, parts, n_pieces, piece_at, part, sc, x, dy, *refs):
    pieces, chunks, (acc, xp, buf, w_sems) = refs[:n_pieces], refs[n_pieces:-4], refs[-4:]
    rows = x.shape[0]
    waits = load_chunks(parts, [offset(sc, *key) for key in keys], part, chunks, buf, w_sems)
    clear_pad(buf, part)
    for key in missing:
        buf[:, pl.ds(offset(sc, *key), LANES)] = jnp.zeros((buf.shape[0], LANES), BF)
    row = 0
    for i, j in piece_at:
        count = pieces[i].shape[2]
        xp[:, row : row + count] = pieces[i][j]
        row += count
    for mine in waits:
        for copy in mine:
            copy.wait()
    both, down = buf[: 2 * LANES], buf[2 * LANES :]
    acc[:rows, : 2 * LANES] = mm_t(x[...], both)
    acc[rows:, : 2 * LANES] = mm_t(xp[0], both)
    acc[:rows, 2 * LANES :] = mm_t(dy[...], down)
    acc[rows:, 2 * LANES :] = mm_t(xp[1], down)


def put_terms(outs, part, top, low):
    two, n = 2 * part, 3 * part
    top, low = top.astype(BF), low.astype(BF)
    for j, out in enumerate(outs):
        for k in range(2):
            cols = slice((2 * j + k) * LANES, (2 * j + k + 1) * LANES)
            out[k * n : k * n + two] = top[:, cols]
            out[k * n + two : (k + 1) * n] = low[:, cols]


def late_kernel(keys, parts, part, sc, acc, x, dy, xp, *refs):
    chunks = refs[:-8]
    gt, dgu, *far = refs[-8:-4]
    rowbuf, xb, buf, x_sems = refs[-4:]
    rows = x.shape[0]
    loads = []
    for i, (k, s) in enumerate(keys):
        cols, to = pl.ds(offset(sc, k, s), LANES), pl.ds(i * LANES, LANES)
        loads += [
            pltpu.make_async_copy(x.at[:, cols], xb.at[0, pl.ds(0, rows), to], x_sems.at[i, 0]),
            pltpu.make_async_copy(dy.at[:, cols], xb.at[1, pl.ds(0, rows), to], x_sems.at[i, 1]),
            pltpu.make_async_copy(xp.at[:, :, cols], xb.at[:, pl.ds(rows, rows), to], x_sems.at[i, 2]),
        ]
    for copy in loads:
        copy.start()
    clear_pad(buf, part)
    for i, pieces in enumerate(parts):
        for at, row, start, count in pieces:
            for first, n, to in spread(start, count, part):
                row_at = row + first - start
                buf[to : to + n, i * LANES : (i + 1) * LANES] = chunks[at][row_at : row_at + n]
    for copy in loads:
        copy.wait()
    both = acc[:, : 2 * LANES] + mm_t(xb[0], buf[: 2 * LANES])
    dhid = acc[:, 2 * LANES :] + mm_t(xb[1], buf[2 * LANES :])
    gate, up_val = both[:, :LANES], both[:, LANES:]
    sig = 1.0 / (1.0 + jnp.exp(-gate))
    silu = gate * sig
    hidden = silu * up_val
    dup = dhid * silu
    dgate = dhid * up_val * sig * (1.0 + gate * (1.0 - sig))
    for m, value in enumerate((dgate, dup, hidden)):
        gt[m * part : (m + 1) * part] = value.T[:part].astype(BF)
    mid = 3 * part // 2
    two = 2 * part
    up, down = far
    for j in range(2):
        cols = slice(j * LANES, (j + 1) * LANES)
        top, low = mm(gt[:two], xb[0, :, cols]), mm(gt[two:], xb[1, :, cols])
        at = j * mid
        up[at : at + mid] = top[:mid].astype(BF)
        down[at : at + two - mid] = top[mid:].astype(BF)
        down[at + two - mid : at + mid] = low.astype(BF)
    group = rows // 16
    for m, value in enumerate((dgate, dup)):
        rowbuf[...] = value.astype(BF)
        for g in range(16):
            to = g // 2 * 4 * group + g % 2 * group
            at = pl.multiple_of(sc[2 + g] * group, group)
            dgu[m, to : to + group] = rowbuf[pl.ds(at, group)]
        for g in range(8):
            to = g * 4 * group + 2 * group
            at = pl.multiple_of(rows + sc[18 + g] * 2 * group, 2 * group)
            dgu[m, to : to + 2 * group] = rowbuf[pl.ds(at, 2 * group)]


def load_blocks(keys, sc, x, dy, xp, xb, sems):
    rows, loads = x.shape[0], []
    for i, (k, s) in enumerate(keys):
        cols, to = pl.ds(offset(sc, k, s), LANES), pl.ds(i * LANES, LANES)
        mine = [
            pltpu.make_async_copy(x.at[:, cols], xb.at[0, pl.ds(0, rows), to], sems.at[i, 0]),
            pltpu.make_async_copy(dy.at[:, cols], xb.at[1, pl.ds(0, rows), to], sems.at[i, 1]),
            pltpu.make_async_copy(xp.at[:, :, cols], xb.at[:, pl.ds(rows, rows), to], sems.at[i, 2]),
        ]
        for copy in mine:
            copy.start()
        loads.append(mine)
    return loads


def dx_kernel(keys, parts, term_keys, part, sc, dgu, gt, x, dy, xp, *refs):
    chunks, (keep, send, *outs), (buf, xb, w_sems, x_sems) = refs[:-8], refs[-8:-4], refs[-4:]
    rows, two = keep.shape[0], 2 * part
    loads = load_blocks(term_keys, sc, x, dy, xp, xb, x_sems)
    waits = load_chunks(parts, [offset(sc, *key) for key in keys], part, chunks, buf, w_sems)
    for mine in loads:
        for copy in mine:
            copy.wait()
    put_terms(outs, part, mm(gt[:two], xb[0]), mm(gt[two:], xb[1]))
    clear_pad(buf, part)
    for mine in waits:
        for copy in mine:
            copy.wait()
    step = 4 * LANES
    for at in range(0, keep.shape[1], step):
        cols = slice(at, at + step)
        dx = mm(dgu[0], buf[:LANES, cols]) + mm(dgu[1], buf[LANES : 2 * LANES, cols])
        keep[:, cols] = dx[:rows].astype(BF)
        send[:, cols] = dx[rows:].astype(BF)


def terms_kernel(keys, part, sc, gt, x, dy, xp, *refs):
    outs, (xb, x_sems) = refs[:-2], refs[-2:]
    rows = x.shape[0]
    loads = load_blocks(keys, sc, x, dy, xp, xb, x_sems)
    two = 2 * part
    for i in range(0, len(keys), 2):
        for copy in loads[i] + loads[i + 1]:
            copy.wait()
        cols = slice(i * LANES, (i + 2) * LANES)
        put_terms(outs[i // 2 : i // 2 + 1], part, mm(gt[:two], xb[0, :, cols]), mm(gt[two:], xb[1, :, cols]))


def join_kernel(part, sc, own, other, *outs):
    mine, theirs = pl.multiple_of(sc[1] * part, part), pl.multiple_of((1 - sc[1]) * part, part)
    for m, out in enumerate(outs):
        out[pl.ds(mine, part)] = own[m * part : (m + 1) * part]
        out[pl.ds(theirs, part)] = other[m * part : (m + 1) * part]


def params(mib):
    return pltpu.CompilerParams(vmem_limit_bytes=mib * 1024 * 1024)


def local(inputs, out_grad, w_gate, w_up, w_down):
    rows, width = inputs.shape[1:]
    part = w_down.shape[0] // 2
    dp, mp = lax.axis_index("dp"), lax.axis_index("mp")
    yl, z = dp // NZ, dp % NZ
    yh, x, c = mp // 8, mp // 2 % NX, mp % 2
    group = rows // 16
    x_own, dy_own = inputs[0], out_grad[0]

    slot = lax.iota(jnp.int32, 26)
    at = slot - 2
    dc, dx, dh = at // 8, at // 2 % NX, at % 2
    ordered = (yh ^ dh) * 8 + (x - (1 - 2 * (c ^ dc)) * dx + NX) % NX * 2 + (c ^ dc)
    at = slot - 18
    dc, dx = at // NX % 2, at % NX
    stands = dc * NX + (NX - (1 - 2 * (c ^ dc)) * dx) % NX
    sc = jnp.where(slot < 2, jnp.where(slot == 0, z, yl), jnp.where(slot < 18, ordered, stands)).astype(jnp.int32)

    u32 = jnp.uint32
    starts = [(yl * part).astype(u32), ((1 - yl) * part).astype(u32), (mp * group).astype(u32), ((mp ^ 8) * group).astype(u32)]
    w_gate, w_up, w_down, x_own, dy_own, sc, *starts = after_all(w_gate, w_up, w_down, x_own, dy_own, sc, *starts)

    def rows_from(array, start, count):
        return lax.dynamic_slice(array, (start, u32(0)), (count, array.shape[1]))

    stacked = jnp.stack([w_gate.T, w_up.T, w_down])
    own, other = (
        lax.dynamic_slice(stacked, (u32(0), starts[i], u32(0)), (3, part, LANES)).reshape(3 * part, LANES)
        for i in range(2)
    )
    mid = own.shape[0] // 2

    def piece(array):
        return jnp.concatenate([rows_from(array, start, group) for start in starts[2:]])

    n = own.shape[0]
    up, down = pz(own, 1), pz(own, -1)
    other = pyl(other)
    chunks = {
        (0, 0): [(own, 0, 0, n)],
        (0, 7): [(up, 0, 0, n)],
        (0, 1): [(down, 0, 0, n)],
        (1, 0): [(other, 0, 0, n)],
    }
    first = jnp.stack([piece(after(x_own, own)), piece(after(dy_own, own))])
    first = pyl(first)
    up, down = jnp.concatenate([other, up]), jnp.concatenate([down, other])
    for step in (1, 2):
        up, down = pz(up, 1), pz(down, -1)
        chunks[1, NZ - step], chunks[0, NZ - step - 1] = [(up, 0, 0, n)], [(up, n, 0, n)]
        chunks[0, step + 1], chunks[1, step] = [(down, 0, 0, n)], [(down, n, 0, n)]
        if step == 1:
            left, right = pxs(first, 1), pxs(first, -1)
            left_s, right_s, first_s, _, _ = after_all(left, right, first, up, down)
            far_x, far_dy = pxs(left_s[0], 1), pxs(right_s[1], -1)
            swap = pc(jnp.stack([first_s, right_s, left_s]))
    up, down = up[: n + mid], down[mid:]
    far_x, far_dy, _, _ = after_all(far_x, far_dy, up, down)
    two_off = jnp.stack([far_x, far_dy])
    swap_two = pc(two_off)
    up, down = pz(up, 1), pz(down, -1)
    chunks[1, 5], chunks[1, 3] = [(up, 0, 0, n)], [(down, n - mid, 0, n)]
    chunks[0, 4] = [(up, n, 0, mid), (down, 0, mid, n - mid)]
    pieces = [first[None], right[None], two_off[None], left[None], swap, swap_two[None]]
    piece_at = [(0, 0), (1, 0), (2, 0), (3, 0), (4, 0), (4, 1), (5, 0), (4, 2)]

    late = [(1, 4), (0, 4)]
    early = [key for key in chunks if key not in late]

    def listed(keys):
        refs, where = [], []
        for key in keys:
            parts = []
            for array, *rest in chunks[key]:
                at = [i for i, a in enumerate(refs) if a is array]
                if not at:
                    refs.append(array)
                parts.append((at[0] if at else len(refs) - 1, *rest))
            where.append(tuple(parts))
        return tuple(where), refs

    parts, refs = listed(early)
    acc, xp = pl.pallas_call(
        functools.partial(early_kernel, early, late, parts, len(pieces), piece_at, part),
        out_shape=(
            jax.ShapeDtypeStruct((2 * rows, 3 * LANES), F32),
            jax.ShapeDtypeStruct((2, rows, width), BF),
        ),
        in_specs=[SMEM] + [VMEM] * (2 + len(pieces)) + [HBM] * len(refs),
        out_specs=(VMEM, VMEM),
        scratch_shapes=[
            pltpu.VMEM((3 * LANES, width), BF),
            pltpu.SemaphoreType.DMA((copies_of(parts, part),)),
        ],
        compiler_params=params(22),
        cost_estimate=COST,
        name="early",
    )(sc, x_own, dy_own, *pieces, *refs)

    up, down = pz(up[:mid], 1), pz(down[n:], -1)
    chunks[1, 4] = [(up, 0, 0, mid), (down, 0, mid, n - mid)]

    parts, refs = listed(late)
    full = jax.ShapeDtypeStruct((3 * part, LANES), BF)
    double = jax.ShapeDtypeStruct((6 * part, LANES), BF)
    late_terms = [(1, 3), (0, 3), (1, 5), (0, 5)]
    gt, dgu, *far = pl.pallas_call(
        functools.partial(late_kernel, late, parts, part),
        out_shape=(
            jax.ShapeDtypeStruct((3 * part, 2 * rows), BF),
            jax.ShapeDtypeStruct((2, 2 * rows, LANES), BF),
            full, full,
        ),
        in_specs=[SMEM, VMEM] + [ANY] * 3 + [VMEM] * len(refs),
        out_specs=(VMEM,) * 4,
        scratch_shapes=[
            pltpu.VMEM((2 * rows, LANES), BF),
            pltpu.VMEM((2, 2 * rows, len(late) * LANES), BF),
            pltpu.VMEM((3 * LANES, len(late) * LANES), BF),
            pltpu.SemaphoreType.DMA((len(late), 3)),
        ],
        compiler_params=params(22),
        cost_estimate=COST,
        name="late",
    )(sc, acc, x_own, dy_own, xp, *refs)


    def ring(up, down):
        return pz(up, 1), pz(down, -1)

    up, down = ring(*far)

    keys = list(chunks)
    parts, refs = listed(keys)
    keep, send, *got = pl.pallas_call(
        functools.partial(dx_kernel, keys, parts, late_terms, part),
        out_shape=(jax.ShapeDtypeStruct((rows, width), BF),) * 2 + (double,) * 2,
        in_specs=[SMEM, VMEM, VMEM] + [ANY] * 3 + [HBM] * len(refs),
        out_specs=(VMEM,) * 4,
        scratch_shapes=[
            pltpu.VMEM((3 * LANES, width), BF),
            pltpu.VMEM((2, 2 * rows, 4 * LANES), BF),
            pltpu.SemaphoreType.DMA((copies_of(parts, part),)),
            pltpu.SemaphoreType.DMA((4, 3)),
        ],
        compiler_params=params(24),
        cost_estimate=COST,
        name="dx",
    )(sc, dgu, gt, x_own, dy_own, xp, *refs)
    term = dict(zip((3, 5), got))

    up, down, send = after_all(up, down, send)
    sent = pc(send)

    def joined(whole, halves, k, first):
        whole, half = whole[k * n : (k + 1) * n].astype(F32), halves[k * mid : (k + 1) * mid]
        if first:
            return jnp.concatenate([whole[:mid], whole[mid:] + half]).astype(BF)
        return jnp.concatenate([whole[:mid] + half, whole[mid:]]).astype(BF)

    p_in, o_in = ((joined(term[3], up, k, 0), joined(term[5], down, k, 1)) for k in range(2))
    gt_later = after(gt, *p_in, *o_in)
    p, o = ring(*p_in), ring(*o_in)
    distances = (2, 6, 1, 7, 0)
    keys = [(k, s) for s in distances for k in (1, 0)]
    got = pl.pallas_call(
        functools.partial(terms_kernel, keys, part),
        out_shape=(double,) * len(distances),
        in_specs=[SMEM, VMEM] + [ANY] * 3,
        out_specs=(VMEM,) * len(distances),
        scratch_shapes=[
            pltpu.VMEM((2, 2 * rows, len(keys) * LANES), BF),
            pltpu.SemaphoreType.DMA((len(keys), 3)),
        ],
        compiler_params=params(20),
        cost_estimate=COST,
        name="terms",
    )(sc, gt_later, x_own, dy_own, xp)
    term.update(zip(distances, got))

    quarter = rows // NX

    def pair(i):
        rows_of = slice(i * quarter, (i + 1) * quarter)
        return keep[rows_of].astype(F32) + sent[rows_of].astype(F32)

    def add(k, s, up, down):
        rows_of = slice(k * n, (k + 1) * n)
        return (
            (term[s][rows_of].astype(F32) + up).astype(BF),
            (term[NZ - s][rows_of].astype(F32) + down).astype(BF),
        )

    acc = px(pair(3).astype(BF), -1)
    p_in = add(0, 2, *p)
    p = ring(*p_in)
    o_in = add(1, 2, *after(tuple(o), *p_in))
    o = ring(*o_in)
    acc = px((pair(2) + after(acc, *p_in)).astype(BF), -1)
    acc = px((pair(1) + after(acc, *o_in)).astype(BF), -1)
    p_in = add(0, 1, *p)
    p = ring(*p_in)
    o_in = add(1, 1, *after(tuple(o), *p_in))
    o = ring(*o_in)
    acc = pair(0) + after(acc, *p_in)
    part_b = [acc[i * group : (i + 1) * group].astype(BF) for i in range(1, 4)]
    sum_other = (term[0][:n].astype(F32) + p[0].astype(F32) + p[1].astype(F32)).astype(BF)
    *part_b, _ = after_all(*part_b, sum_other)
    got = [pyh(part_b[0]), pyl(part_b[1]), pboth(part_b[2])]
    in_grad = (acc[:group] + got[0] + got[1] + got[2]).astype(BF).reshape(1, group, width)
    o = after(tuple(o), sum_other, *part_b)
    sum_other = pyl(sum_other)
    sum_own = (term[0][n:].astype(F32) + o[0].astype(F32) + o[1].astype(F32)).astype(BF)

    gate_grad, up_grad, down_grad = pl.pallas_call(
        functools.partial(join_kernel, part),
        out_shape=(jax.ShapeDtypeStruct((2 * part, LANES), BF),) * 3,
        in_specs=[SMEM, VMEM, VMEM],
        out_specs=(VMEM,) * 3,
        compiler_params=params(8),
        cost_estimate=COST,
        name="join",
    )(sc, sum_own, sum_other)
    return in_grad, gate_grad.T, up_grad.T, down_grad


def solution(mesh):
    placed = (P("dp", None, None), P("dp", None, None), P("dp", "mp"), P("dp", "mp"), P("mp", "dp"))
    return jax.shard_map(
        local,
        mesh=mesh,
        in_specs=placed,
        out_specs=(P("dp", "mp", None), P("dp", "mp"), P("dp", "mp"), P("mp", "dp")),
        check_vma=False,
    )
```

```python
import functools

import jax
import jax.numpy as jnp
from jax import lax
from jax.experimental import pallas as pl
from jax.experimental.pallas import tpu as pltpu
from jax.sharding import PartitionSpec as P

BF = jnp.bfloat16
F32 = jnp.float32
NX, NZ = 4, 8
LANES = 256
ANY = pl.BlockSpec(memory_space=pl.ANY)
HBM = pl.BlockSpec(memory_space=pltpu.HBM)
VMEM = pl.BlockSpec(memory_space=pltpu.VMEM)
COST = pl.CostEstimate(flops=1, bytes_accessed=1, transcendentals=0)
SMEM = pl.BlockSpec(memory_space=pltpu.SMEM)


def mm(left, right):
    return lax.dot_general(left, right, (((1,), (0,)), ((), ())), preferred_element_type=F32)


def mm_t(left, right):
    return lax.dot_general(left, right, (((1,), (1,)), ((), ())), preferred_element_type=F32)


def pz(value, step):
    pairs = [(y * NZ + z, y * NZ + (z + step) % NZ) for y in range(2) for z in range(NZ)]
    return lax.ppermute(value, "dp", pairs)


def pyl(value):
    return lax.ppermute(value, "dp", [(i, (i + NZ) % (2 * NZ)) for i in range(2 * NZ)])


def px(value, step):
    pairs = [
        (y * 8 + x * 2 + c, y * 8 + (x + (-step if c else step)) % NX * 2 + c)
        for y in range(2) for x in range(NX) for c in range(2)
    ]
    return lax.ppermute(value, "mp", pairs)


def pxs(value, step):
    pairs = [
        (y * 8 + x * 2 + c, y * 8 + (x + step) % NX * 2 + c)
        for y in range(2) for x in range(NX) for c in range(2)
    ]
    return lax.ppermute(value, "mp", pairs)


def pc(value):
    return lax.ppermute(value, "mp", [(i, i ^ 1) for i in range(16)])


def pyh(value):
    return lax.ppermute(value, "mp", [(i, i ^ 8) for i in range(16)])


def pboth(value):
    n = 2 * NZ
    pairs = [(m * n + d, (m ^ 8) * n + (d + NZ) % n) for m in range(16) for d in range(n)]
    return lax.ppermute(value, ("mp", "dp"), pairs)


def after(value, *others):
    return lax.optimization_barrier((value, *others))[0]


def after_all(*values):
    return lax.optimization_barrier(values)


def col_block(sc, k, s):
    yl = 1 - sc[1] if k else sc[1]
    return yl * NZ + lax.rem(sc[0] + s, NZ)


def offset(sc, k, s):
    return pl.multiple_of(col_block(sc, k, s) * LANES, LANES)


def spread(row, count, part):
    out, end = [], row + count
    while row < end:
        m = row // part
        n = min(end, (m + 1) * part) - row
        out.append((row, n, m * LANES + row - m * part))
        row += n
    return out


def load_chunks(where, places, part, refs, buf, sems):
    waits, sem = [], 0
    for parts, place in zip(where, places):
        mine = []
        for at, row, start, count in parts:
            for first, n, to in spread(start, count, part):
                copy = pltpu.make_async_copy(
                    refs[at].at[pl.ds(row + first - start, n)],
                    buf.at[pl.ds(to, n), pl.ds(place, LANES)],
                    sems.at[sem],
                )
                copy.start()
                mine.append(copy)
                sem += 1
        waits.append(mine)
    return waits


def copies_of(where, part):
    return sum(len(spread(start, count, part)) for parts in where for _, _, start, count in parts)


def clear_pad(buf, part):
    for m in range(3):
        buf[m * LANES + part : (m + 1) * LANES] = jnp.zeros((LANES - part, buf.shape[1]), BF)


def early_kernel(keys, missing, parts, n_pieces, piece_at, part, sc, x, dy, *refs):
    pieces, chunks, (acc, xp, buf, w_sems) = refs[:n_pieces], refs[n_pieces:-4], refs[-4:]
    rows = x.shape[0]
    waits = load_chunks(parts, [offset(sc, *key) for key in keys], part, chunks, buf, w_sems)
    clear_pad(buf, part)
    for key in missing:
        buf[:, pl.ds(offset(sc, *key), LANES)] = jnp.zeros((buf.shape[0], LANES), BF)
    row = 0
    for i, j in piece_at:
        count = pieces[i].shape[2]
        xp[:, row : row + count] = pieces[i][j]
        row += count
    for mine in waits:
        for copy in mine:
            copy.wait()
    both, down = buf[: 2 * LANES], buf[2 * LANES :]
    acc[:rows, : 2 * LANES] = mm_t(x[...], both)
    acc[rows:, : 2 * LANES] = mm_t(xp[0], both)
    acc[:rows, 2 * LANES :] = mm_t(dy[...], down)
    acc[rows:, 2 * LANES :] = mm_t(xp[1], down)


def put_terms(outs, part, top, low):
    two, n = 2 * part, 3 * part
    top, low = top.astype(BF), low.astype(BF)
    for j, out in enumerate(outs):
        for k in range(2):
            cols = slice((2 * j + k) * LANES, (2 * j + k + 1) * LANES)
            out[k * n : k * n + two] = top[:, cols]
            out[k * n + two : (k + 1) * n] = low[:, cols]


def late_kernel(keys, parts, part, sc, acc, x, dy, xp, *refs):
    chunks = refs[:-8]
    gt, dgu, *far = refs[-8:-4]
    rowbuf, xb, buf, x_sems = refs[-4:]
    rows = x.shape[0]
    loads = []
    for i, (k, s) in enumerate(keys):
        cols, to = pl.ds(offset(sc, k, s), LANES), pl.ds(i * LANES, LANES)
        loads += [
            pltpu.make_async_copy(x.at[:, cols], xb.at[0, pl.ds(0, rows), to], x_sems.at[i, 0]),
            pltpu.make_async_copy(dy.at[:, cols], xb.at[1, pl.ds(0, rows), to], x_sems.at[i, 1]),
            pltpu.make_async_copy(xp.at[:, :, cols], xb.at[:, pl.ds(rows, rows), to], x_sems.at[i, 2]),
        ]
    for copy in loads:
        copy.start()
    clear_pad(buf, part)
    for i, pieces in enumerate(parts):
        for at, row, start, count in pieces:
            for first, n, to in spread(start, count, part):
                row_at = row + first - start
                buf[to : to + n, i * LANES : (i + 1) * LANES] = chunks[at][row_at : row_at + n]
    for copy in loads:
        copy.wait()
    both = acc[:, : 2 * LANES] + mm_t(xb[0], buf[: 2 * LANES])
    dhid = acc[:, 2 * LANES :] + mm_t(xb[1], buf[2 * LANES :])
    gate, up_val = both[:, :LANES], both[:, LANES:]
    sig = 1.0 / (1.0 + jnp.exp(-gate))
    silu = gate * sig
    hidden = silu * up_val
    dup = dhid * silu
    dgate = dhid * up_val * sig * (1.0 + gate * (1.0 - sig))
    for m, value in enumerate((dgate, dup, hidden)):
        gt[m * part : (m + 1) * part] = value.T[:part].astype(BF)
    mid = 3 * part // 2
    two = 2 * part
    up, down = far
    for j in range(2):
        cols = slice(j * LANES, (j + 1) * LANES)
        top, low = mm(gt[:two], xb[0, :, cols]), mm(gt[two:], xb[1, :, cols])
        at = j * mid
        up[at : at + mid] = top[:mid].astype(BF)
        down[at : at + two - mid] = top[mid:].astype(BF)
        down[at + two - mid : at + mid] = low.astype(BF)
    group = rows // 16
    for m, value in enumerate((dgate, dup)):
        rowbuf[...] = value.astype(BF)
        for g in range(16):
            to = g // 2 * 4 * group + g % 2 * group
            at = pl.multiple_of(sc[2 + g] * group, group)
            dgu[m, to : to + group] = rowbuf[pl.ds(at, group)]
        for g in range(8):
            to = g * 4 * group + 2 * group
            at = pl.multiple_of(rows + sc[18 + g] * 2 * group, 2 * group)
            dgu[m, to : to + 2 * group] = rowbuf[pl.ds(at, 2 * group)]


def load_blocks(keys, sc, x, dy, xp, xb, sems):
    rows, loads = x.shape[0], []
    for i, (k, s) in enumerate(keys):
        cols, to = pl.ds(offset(sc, k, s), LANES), pl.ds(i * LANES, LANES)
        mine = [
            pltpu.make_async_copy(x.at[:, cols], xb.at[0, pl.ds(0, rows), to], sems.at[i, 0]),
            pltpu.make_async_copy(dy.at[:, cols], xb.at[1, pl.ds(0, rows), to], sems.at[i, 1]),
            pltpu.make_async_copy(xp.at[:, :, cols], xb.at[:, pl.ds(rows, rows), to], sems.at[i, 2]),
        ]
        for copy in mine:
            copy.start()
        loads.append(mine)
    return loads


def dx_kernel(keys, parts, term_keys, part, sc, dgu, gt, x, dy, xp, *refs):
    chunks, (keep, send, *outs), (buf, xb, w_sems, x_sems) = refs[:-8], refs[-8:-4], refs[-4:]
    rows, two = keep.shape[0], 2 * part
    loads = load_blocks(term_keys, sc, x, dy, xp, xb, x_sems)
    waits = load_chunks(parts, [offset(sc, *key) for key in keys], part, chunks, buf, w_sems)
    for mine in loads:
        for copy in mine:
            copy.wait()
    put_terms(outs, part, mm(gt[:two], xb[0]), mm(gt[two:], xb[1]))
    clear_pad(buf, part)
    for mine in waits:
        for copy in mine:
            copy.wait()
    step = 4 * LANES
    for at in range(0, keep.shape[1], step):
        cols = slice(at, at + step)
        dx = mm(dgu[0], buf[:LANES, cols]) + mm(dgu[1], buf[LANES : 2 * LANES, cols])
        keep[:, cols] = dx[:rows].astype(BF)
        send[:, cols] = dx[rows:].astype(BF)


def terms_kernel(keys, part, sc, gt, x, dy, xp, *refs):
    outs, (xb, x_sems) = refs[:-2], refs[-2:]
    rows = x.shape[0]
    loads = load_blocks(keys, sc, x, dy, xp, xb, x_sems)
    two = 2 * part
    for i in range(0, len(keys), 2):
        for copy in loads[i] + loads[i + 1]:
            copy.wait()
        cols = slice(i * LANES, (i + 2) * LANES)
        put_terms(outs[i // 2 : i // 2 + 1], part, mm(gt[:two], xb[0, :, cols]), mm(gt[two:], xb[1, :, cols]))


def join_kernel(part, sc, own, other, *outs):
    mine, theirs = pl.multiple_of(sc[1] * part, part), pl.multiple_of((1 - sc[1]) * part, part)
    for m, out in enumerate(outs):
        out[pl.ds(mine, part)] = own[m * part : (m + 1) * part]
        out[pl.ds(theirs, part)] = other[m * part : (m + 1) * part]


def params(mib):
    return pltpu.CompilerParams(vmem_limit_bytes=mib * 1024 * 1024)


def local(inputs, out_grad, w_gate, w_up, w_down):
    rows, width = inputs.shape[1:]
    part = w_down.shape[0] // 2
    dp, mp = lax.axis_index("dp"), lax.axis_index("mp")
    yl, z = dp // NZ, dp % NZ
    yh, x, c = mp // 8, mp // 2 % NX, mp % 2
    group = rows // 16
    x_own, dy_own = inputs[0], out_grad[0]

    slot = lax.iota(jnp.int32, 26)
    at = slot - 2
    dc, dx, dh = at // 8, at // 2 % NX, at % 2
    ordered = (yh ^ dh) * 8 + (x - (1 - 2 * (c ^ dc)) * dx + NX) % NX * 2 + (c ^ dc)
    at = slot - 18
    dc, dx = at // NX % 2, at % NX
    stands = dc * NX + (NX - (1 - 2 * (c ^ dc)) * dx) % NX
    sc = jnp.where(slot < 2, jnp.where(slot == 0, z, yl), jnp.where(slot < 18, ordered, stands)).astype(jnp.int32)

    u32 = jnp.uint32
    starts = [(yl * part).astype(u32), ((1 - yl) * part).astype(u32), (mp * group).astype(u32), ((mp ^ 8) * group).astype(u32)]
    w_gate, w_up, w_down, x_own, dy_own, sc, *starts = after_all(w_gate, w_up, w_down, x_own, dy_own, sc, *starts)

    def rows_from(array, start, count):
        return lax.dynamic_slice(array, (start, u32(0)), (count, array.shape[1]))

    stacked = jnp.stack([w_gate.T, w_up.T, w_down])
    own, other = (
        lax.dynamic_slice(stacked, (u32(0), starts[i], u32(0)), (3, part, LANES)).reshape(3 * part, LANES)
        for i in range(2)
    )
    mid = own.shape[0] // 2

    def piece(array):
        return jnp.concatenate([rows_from(array, start, group) for start in starts[2:]])

    n = own.shape[0]
    up, down = pz(own, 1), pz(own, -1)
    other = pyl(other)
    chunks = {
        (0, 0): [(own, 0, 0, n)],
        (0, 7): [(up, 0, 0, n)],
        (0, 1): [(down, 0, 0, n)],
        (1, 0): [(other, 0, 0, n)],
    }
    first = jnp.stack([piece(after(x_own, own)), piece(after(dy_own, own))])
    first = pyl(after(first, other))
    up, down = jnp.concatenate([other, up]), jnp.concatenate([down, other])
    for step in (1, 2):
        up, down = pz(up, 1), pz(down, -1)
        chunks[1, NZ - step], chunks[0, NZ - step - 1] = [(up, 0, 0, n)], [(up, n, 0, n)]
        chunks[0, step + 1], chunks[1, step] = [(down, 0, 0, n)], [(down, n, 0, n)]
        if step == 1:
            left, right = pxs(first, 1), pxs(first, -1)
            left_s, right_s, first_s, _, _ = after_all(left, right, first, up, down)
            far_x, far_dy = pxs(left_s[0], 1), pxs(right_s[1], -1)
            swap = pc(jnp.stack([first_s, right_s, left_s]))
    up, down = up[: n + mid], down[mid:]
    far_x, far_dy, _, _ = after_all(far_x, far_dy, up, down)
    two_off = jnp.stack([far_x, far_dy])
    swap_two = pc(two_off)
    up, down = pz(up, 1), pz(down, -1)
    chunks[1, 5], chunks[1, 3] = [(up, 0, 0, n)], [(down, n - mid, 0, n)]
    chunks[0, 4] = [(up, n, 0, mid), (down, 0, mid, n - mid)]
    pieces = [first[None], right[None], two_off[None], left[None], swap, swap_two[None]]
    piece_at = [(0, 0), (1, 0), (2, 0), (3, 0), (4, 0), (4, 1), (5, 0), (4, 2)]

    late = [(1, 4), (0, 4)]
    early = [key for key in chunks if key not in late]

    def listed(keys):
        refs, where = [], []
        for key in keys:
            parts = []
            for array, *rest in chunks[key]:
                at = [i for i, a in enumerate(refs) if a is array]
                if not at:
                    refs.append(array)
                parts.append((at[0] if at else len(refs) - 1, *rest))
            where.append(tuple(parts))
        return tuple(where), refs

    parts, refs = listed(early)
    acc, xp = pl.pallas_call(
        functools.partial(early_kernel, early, late, parts, len(pieces), piece_at, part),
        out_shape=(
            jax.ShapeDtypeStruct((2 * rows, 3 * LANES), F32),
            jax.ShapeDtypeStruct((2, rows, width), BF),
        ),
        in_specs=[SMEM] + [VMEM] * (2 + len(pieces)) + [HBM] * len(refs),
        out_specs=(VMEM, VMEM),
        scratch_shapes=[
            pltpu.VMEM((3 * LANES, width), BF),
            pltpu.SemaphoreType.DMA((copies_of(parts, part),)),
        ],
        compiler_params=params(22),
        cost_estimate=COST,
        name="early",
    )(sc, x_own, dy_own, *pieces, *refs)

    up, down = pz(up[:mid], 1), pz(down[n:], -1)
    chunks[1, 4] = [(up, 0, 0, mid), (down, 0, mid, n - mid)]

    parts, refs = listed(late)
    full = jax.ShapeDtypeStruct((3 * part, LANES), BF)
    double = jax.ShapeDtypeStruct((6 * part, LANES), BF)
    late_terms = [(1, 3), (0, 3), (1, 5), (0, 5)]
    gt, dgu, *far = pl.pallas_call(
        functools.partial(late_kernel, late, parts, part),
        out_shape=(
            jax.ShapeDtypeStruct((3 * part, 2 * rows), BF),
            jax.ShapeDtypeStruct((2, 2 * rows, LANES), BF),
            full, full,
        ),
        in_specs=[SMEM, VMEM] + [ANY] * 3 + [VMEM] * len(refs),
        out_specs=(VMEM,) * 4,
        scratch_shapes=[
            pltpu.VMEM((2 * rows, LANES), BF),
            pltpu.VMEM((2, 2 * rows, len(late) * LANES), BF),
            pltpu.VMEM((3 * LANES, len(late) * LANES), BF),
            pltpu.SemaphoreType.DMA((len(late), 3)),
        ],
        compiler_params=params(22),
        cost_estimate=COST,
        name="late",
    )(sc, acc, x_own, dy_own, xp, *refs)


    def ring(up, down):
        return pz(up, 1), pz(down, -1)

    up, down = ring(*far)

    keys = list(chunks)
    parts, refs = listed(keys)
    keep, send, *got = pl.pallas_call(
        functools.partial(dx_kernel, keys, parts, late_terms, part),
        out_shape=(jax.ShapeDtypeStruct((rows, width), BF),) * 2 + (double,) * 2,
        in_specs=[SMEM, VMEM, VMEM] + [ANY] * 3 + [HBM] * len(refs),
        out_specs=(VMEM,) * 4,
        scratch_shapes=[
            pltpu.VMEM((3 * LANES, width), BF),
            pltpu.VMEM((2, 2 * rows, 4 * LANES), BF),
            pltpu.SemaphoreType.DMA((copies_of(parts, part),)),
            pltpu.SemaphoreType.DMA((4, 3)),
        ],
        compiler_params=params(24),
        cost_estimate=COST,
        name="dx",
    )(sc, dgu, gt, x_own, dy_own, xp, *refs)
    term = dict(zip((3, 5), got))

    up, down, send = after_all(up, down, send)
    sent = pc(send)

    def joined(whole, halves, k, first):
        whole, half = whole[k * n : (k + 1) * n].astype(F32), halves[k * mid : (k + 1) * mid]
        if first:
            return jnp.concatenate([whole[:mid], whole[mid:] + half]).astype(BF)
        return jnp.concatenate([whole[:mid] + half, whole[mid:]]).astype(BF)

    p_in, o_in = ((joined(term[3], up, k, 0), joined(term[5], down, k, 1)) for k in range(2))
    gt_later = after(gt, *p_in, *o_in)
    p, o = ring(*p_in), ring(*o_in)
    distances = (2, 6, 1, 7, 0)
    keys = [(k, s) for s in distances for k in (1, 0)]
    got = pl.pallas_call(
        functools.partial(terms_kernel, keys, part),
        out_shape=(double,) * len(distances),
        in_specs=[SMEM, VMEM] + [ANY] * 3,
        out_specs=(VMEM,) * len(distances),
        scratch_shapes=[
            pltpu.VMEM((2, 2 * rows, len(keys) * LANES), BF),
            pltpu.SemaphoreType.DMA((len(keys), 3)),
        ],
        compiler_params=params(20),
        cost_estimate=COST,
        name="terms",
    )(sc, gt_later, x_own, dy_own, xp)
    term.update(zip(distances, got))

    quarter = rows // NX

    def pair(i):
        rows_of = slice(i * quarter, (i + 1) * quarter)
        return keep[rows_of].astype(F32) + sent[rows_of].astype(F32)

    def add(k, s, up, down):
        rows_of = slice(k * n, (k + 1) * n)
        return (
            (term[s][rows_of].astype(F32) + up).astype(BF),
            (term[NZ - s][rows_of].astype(F32) + down).astype(BF),
        )

    acc = px(pair(3).astype(BF), -1)
    p_in = add(0, 2, *p)
    p = ring(*p_in)
    o_in = add(1, 2, *after(tuple(o), *p_in))
    o = ring(*o_in)
    acc = px((pair(2) + after(acc, *p_in)).astype(BF), -1)
    acc = px((pair(1) + after(acc, *o_in)).astype(BF), -1)
    p_in = add(0, 1, *p)
    p = ring(*p_in)
    o_in = add(1, 1, *after(tuple(o), *p_in))
    o = ring(*o_in)
    acc = pair(0) + after(acc, *p_in)
    part_b = [acc[i * group : (i + 1) * group].astype(BF) for i in range(1, 4)]
    sum_other = (term[0][:n].astype(F32) + p[0].astype(F32) + p[1].astype(F32)).astype(BF)
    *part_b, _ = after_all(*part_b, sum_other)
    got = [pyh(part_b[0]), pyl(part_b[1]), pboth(part_b[2])]
    in_grad = (acc[:group] + got[0] + got[1] + got[2]).astype(BF).reshape(1, group, width)
    o = after(tuple(o), sum_other, *part_b)
    sum_other = pyl(sum_other)
    sum_own = (term[0][n:].astype(F32) + o[0].astype(F32) + o[1].astype(F32)).astype(BF)

    gate_grad, up_grad, down_grad = pl.pallas_call(
        functools.partial(join_kernel, part),
        out_shape=(jax.ShapeDtypeStruct((2 * part, LANES), BF),) * 3,
        in_specs=[SMEM, VMEM, VMEM],
        out_specs=(VMEM,) * 3,
        compiler_params=params(8),
        cost_estimate=COST,
        name="join",
    )(sc, sum_own, sum_other)
    return in_grad, gate_grad.T, up_grad.T, down_grad


def solution(mesh):
    placed = (P("dp", None, None), P("dp", None, None), P("dp", "mp"), P("dp", "mp"), P("mp", "dp"))
    return jax.shard_map(
        local,
        mesh=mesh,
        in_specs=placed,
        out_specs=(P("dp", "mp", None), P("dp", "mp"), P("dp", "mp"), P("mp", "dp")),
        check_vma=False,
    )
```
